256 devices in a mesh: seq: 16 (over x_lo, y, core), ctx: 16 (over x_hi, z).
Axes of the slice: x: 4 (x_hi: 2, x_lo: 2; x = x_hi * 2 + x_lo), y: 4, z: 8, core: 2. Of those that a mesh axis runs over, the one named last changes fastest.
Arguments:
- order: int32 [16, 32], P('seq'), may hold values from 0 to 31, each once within a row
- queries: bfloat16 [16, 4096, 5, 128], P('seq', 'ctx'), may hold values from -11 to 11
- keys: bfloat16 [16, 4096, 128], P('seq', 'ctx'), may hold values from -6 to 6
- w_query_gate: float32 [5, 128, 128], replicated, may hold values from -12.5 to 12.5
- w_key_gate: float32 [384, 128], replicated, may hold values from -0.3125 to 0.3125
Outputs:
- target: float32 [16, 16, 5, 4, 64], P('seq', 'ctx')
- grad_query_gate: float32 [5, 128, 128], replicated
- grad_key_gate: float32 [384, 128], replicated
- loss: float32 [16], P('seq')
The draws below stay inside these ranges and needn't reach their ends.
Inputs may be any that keep to these rules, and one draw needn't show every extreme that they name: Each row names every half-block of 128 tokens of its sequence once; device c of ctx holds the half-blocks named at entries 2 c and 2 c + 1, in that order.
All inputs are finite; a program needn't handle non-finite values.
Results may differ from the reference program's by a relative error of at most 0.0003.
Values may be sent and summed in bfloat16 or wider, within the bound.
No kernel may reach another device: no remote copies, remote signals or barrier semaphores. Data moves between devices by JAX's collectives and lax.ppermute only.
A program may use at most 192 MiB of HBM per device.

```python
import jax
import jax.numpy as jnp
from jax import lax

H = 5
HD = 128
DG = 128
POOL = 64
TOK_DEV = 256
HALF = 128
TOKENS = 4096
SEQS = 16
QB_DEV = 4
NB = 64
N_CTX = 16


def draw_keys(key, part):
    key = jax.random.fold_in(key, 11)
    base = jax.random.truncated_normal(key, -6.0, 6.0, (SEQS, TOKENS, HD), jnp.float32)
    return base.astype(jnp.bfloat16)


def draw_queries(key, part):
    key = jax.random.fold_in(key, 12)
    base = jax.random.truncated_normal(key, -6.0, 6.0, (SEQS, TOKENS, H, HD), jnp.float32)
    return base.astype(jnp.bfloat16)


def draw_w_query_gate(key, part):
    key = jax.random.fold_in(key, 13)
    base = jax.random.truncated_normal(key, -4.0, 4.0, (H, HD, DG), jnp.float32) * (8.0 / HD ** 0.5)
    return base


def normal_values(key, dims, spread, bound, kind=jnp.bfloat16):
    entries = spread * jax.random.normal(key, dims, jnp.float32)
    return jnp.clip(entries, min=-bound, max=bound).astype(kind)


def setup_inputs(seed: int = 0) -> dict:
    arg_keys = jax.random.split(jax.random.key(seed), 6)
    return {
        "order": jax.vmap(lambda own: jax.random.permutation(own, 2 * N_CTX))(jax.random.split(arg_keys[0], SEQS)).reshape((SEQS, 2 * N_CTX)).astype(jnp.int32),
        "queries": draw_queries(jax.random.fold_in(arg_keys[5], 71), 0),
        "keys": draw_keys(jax.random.fold_in(arg_keys[5], 71), 0),
        "w_query_gate": draw_w_query_gate(jax.random.fold_in(arg_keys[5], 71), 0),
        "w_key_gate": normal_values(arg_keys[4], (3 * HD, DG), (3 * HD) ** -0.5, 0.3125, jnp.float32),
    }


masked_low = -1.0e30


def one_sequence(order_row, queries, keys, w_query_gate, w_key_gate):
    highest = lax.Precision.HIGHEST
    rows = jnp.arange(TOKENS, dtype=jnp.int32)
    token_pos = jnp.take(order_row, rows // HALF) * HALF + rows % HALF
    per_half = HALF // POOL
    blocks = jnp.arange(NB, dtype=jnp.int32)
    block_pos = jnp.take(order_row, blocks // per_half) * per_half + blocks % per_half

    def one_shard(index):
        start = (index * TOK_DEV).astype(jnp.int32)
        q_part = lax.dynamic_slice_in_dim(queries, start, TOK_DEV, 0).reshape(TOK_DEV * H, HD)
        q_pos = jnp.repeat(lax.dynamic_slice_in_dim(token_pos, start, TOK_DEV, 0), H)
        scores = lax.dot_general(q_part, keys, (((1,), (1,)), ((), ())), preferred_element_type=jnp.float32) * (HD ** -0.5)
        allowed = token_pos[None, :] <= q_pos[:, None]
        row_top = jnp.max(jnp.where(allowed, scores, masked_low), axis=1, keepdims=True)
        row_total = jnp.sum(jnp.where(allowed, jnp.exp(scores - row_top), 0.0), axis=1, keepdims=True)
        lse = row_top + jnp.log(row_total)
        probs = jnp.where(allowed, jnp.exp(scores - lse), 0.0)
        return probs.reshape(QB_DEV, POOL, H, NB, POOL).max(axis=(1, 4))

    maps = lax.map(one_shard, jnp.arange(N_CTX, dtype=jnp.int32))
    maps = jnp.transpose(maps, (0, 2, 1, 3))
    target = maps / jnp.sum(maps, axis=-1, keepdims=True)
    gate_target = jnp.transpose(target, (1, 0, 2, 3)).reshape(H, NB, NB)
    pooled_q = queries.astype(jnp.float32).reshape(NB, POOL, H, HD).mean(axis=1)
    key_blocks = keys.reshape(NB, POOL, HD)
    pooled_k = jnp.concatenate([key_blocks.max(axis=1).astype(jnp.float32), key_blocks.min(axis=1).astype(jnp.float32), key_blocks.astype(jnp.float32).mean(axis=1)], axis=1)
    gate_q = jnp.einsum('qhd,hdg->hqg', pooled_q, w_query_gate, precision=highest)
    gate_k = jnp.dot(pooled_k, w_key_gate, precision=highest)
    logits = jnp.einsum('hqg,kg->hqk', gate_q, gate_k, precision=highest) * (DG ** -0.5)
    visible = (block_pos[None, :] <= block_pos[:, None])[None]
    peak = jnp.max(jnp.where(visible, logits, masked_low), axis=-1, keepdims=True)
    weights = jnp.where(visible, jnp.exp(logits - peak), 0.0)
    norm_sum = jnp.sum(weights, axis=-1, keepdims=True)
    log_gate = logits - peak - jnp.log(norm_sum)
    gate = weights / norm_sum
    count = H * NB
    loss = -jnp.sum(jnp.where(visible, gate_target * log_gate, 0.0)) / count
    d_logits = jnp.where(visible, gate - gate_target, 0.0) / count * (DG ** -0.5)
    d_gate_q = jnp.einsum('hqk,kg->hqg', d_logits, gate_k, precision=highest)
    d_gate_k = jnp.einsum('hqk,hqg->kg', d_logits, gate_q, precision=highest)
    grad_q = jnp.einsum('qhd,hqg->hdg', pooled_q, d_gate_q, precision=highest)
    grad_k = jnp.dot(pooled_k.T, d_gate_k, precision=highest)
    return target, loss, grad_q, grad_k


def reference(order, queries, keys, w_query_gate, w_key_gate):
    def per_sequence(items):
        return one_sequence(items[0], items[1], items[2], w_query_gate, w_key_gate)

    target, losses, grad_q, grad_k = lax.map(per_sequence, (order, queries, keys))
    return target, jnp.sum(grad_q, axis=0), jnp.sum(grad_k, axis=0), losses
```

```python
import functools
import math

import jax
import jax.numpy as jnp
from jax import lax
from jax.experimental import pallas as pl
from jax.experimental.pallas import tpu as pltpu
from jax.sharding import PartitionSpec as P

POOL = 64
LOW = -1e30
HIGHEST = lax.Precision.HIGHEST
VMEM = pl.BlockSpec(memory_space=pltpu.VMEM)
SMEM = pl.BlockSpec(memory_space=pltpu.SMEM)
PARAMS = pltpu.CompilerParams(vmem_limit_bytes=40 * 1024 * 1024)
CHUNK = 512
SUB = 8


def dot_nt(a, b, precision=None):
    return lax.dot_general(
        a, b, (((1,), (1,)), ((), ())), precision=precision, preferred_element_type=jnp.float32
    )


def dot_tn(a, b, precision=None):
    return lax.dot_general(
        a, b, (((0,), (0,)), ((), ())), precision=precision, preferred_element_type=jnp.float32
    )


def dot_nn(a, b, precision=None):
    return lax.dot_general(
        a, b, (((1,), (0,)), ((), ())), precision=precision, preferred_element_type=jnp.float32
    )


def local_kernel(scale, q_ref, k_ref, wq_ref, diag_ref, top_ref, tot_ref, pooled_ref, gate_q_ref):
    heads, rows, width = q_ref.shape
    half = rows // 2
    blocks = rows // POOL
    diag_ref[...] = jnp.full(diag_ref.shape, LOW, jnp.float32)
    key_row = lax.broadcasted_iota(jnp.int32, (half, half), 0)
    query_lane = lax.broadcasted_iota(jnp.int32, (half, half), 1)
    causal = key_row <= query_lane
    blank = jnp.zeros((SUB - blocks, width), jnp.float32)
    for h in range(heads):
        q = q_ref[h]
        pooled = jnp.sum(q.astype(jnp.float32).reshape(blocks, POOL, width), axis=1) * (1.0 / POOL)
        pooled_ref[h * SUB : (h + 1) * SUB, :] = jnp.concatenate([blank, pooled], axis=0)
        gate_q_ref[h * SUB : (h + 1) * SUB, :] = dot_nn(
            jnp.concatenate([pooled, blank], axis=0), wq_ref[h], HIGHEST
        )
        for part in range(2):
            s = dot_nt(k_ref[part * half : (part + 1) * half, :], q[part * half : (part + 1) * half, :])
            s = jnp.where(causal, s * scale, LOW)
            per = half // POOL
            block_top = jnp.max(s.reshape(per, POOL, half), axis=1)
            top = jnp.max(block_top, axis=0, keepdims=True)
            p = jnp.exp2(s - top)
            lanes = slice(h * rows + part * half, h * rows + (part + 1) * half)
            diag_ref[part * per : (part + 1) * per, lanes] = block_top
            top_ref[:, lanes] = top
            tot_ref[:, lanes] = jnp.sum(p.reshape(half // SUB, SUB, half), axis=0)


def attend(scale, base, order_ref, own_ref, q_ref, k_ref, top_ref, tot_ref, map_ref, map_row, pool_ref, pool_row):
    heads, rows, width = q_ref.shape
    half = rows // 2
    kb_chunk = CHUNK // POOL
    halves_chunk = CHUNK // half
    kb_row = lax.broadcasted_iota(jnp.int32, (kb_chunk, rows), 0)
    lane = lax.broadcasted_iota(jnp.int32, (kb_chunk, rows), 1)
    query_half = jnp.where(lane < half, own_ref[1], own_ref[2])

    def step(i, carry):
        start = pl.multiple_of(i * CHUNK, CHUNK)
        keys = k_ref[pl.ds(start, CHUNK), :]
        key_half = jnp.full((kb_chunk, rows), order_ref[0, base + i * halves_chunk], jnp.int32)
        for j in range(1, halves_chunk):
            key_half = jnp.where(
                kb_row >= j * (half // POOL), order_ref[0, base + i * halves_chunk + j], key_half
            )
        seen = jnp.where(key_half < query_half, 1.0, 0.0)
        seen_rows = jnp.broadcast_to(seen[:, None, :], (kb_chunk, SUB, rows)) > 0.5
        seen = seen > 0.5
        blocks = keys.astype(jnp.float32).reshape(kb_chunk, POOL, width)
        pool_at = pl.ds(pl.multiple_of(pool_row + i * kb_chunk, kb_chunk), kb_chunk)
        pool_ref[pool_at, 0:width] = jnp.max(blocks, axis=1)
        pool_ref[pool_at, width : 2 * width] = jnp.min(blocks, axis=1)
        pool_ref[pool_at, 2 * width : 3 * width] = jnp.sum(blocks, axis=1) * (1.0 / POOL)
        map_at = pl.ds(pl.multiple_of(map_row + i * kb_chunk, kb_chunk), kb_chunk)
        for h in range(heads):
            lanes = slice(h * rows, (h + 1) * rows)
            s = dot_nt(keys, q_ref[h]) * scale
            s = s.reshape(kb_chunk, POOL // SUB, SUB, rows)
            block_top = jnp.max(jnp.max(s, axis=1), axis=1)
            block_top = jnp.where(seen, block_top, LOW)
            map_ref[map_at, lanes] = block_top
            top = top_ref[:, lanes]
            new_top = jnp.maximum(top, jnp.max(block_top, axis=0, keepdims=True))
            part = jnp.sum(jnp.exp2(s - new_top.reshape(1, 1, 1, rows)), axis=1)
            part = jnp.sum(jnp.where(seen_rows, part, 0.0), axis=0)
            tot_ref[:, lanes] = tot_ref[:, lanes] * jnp.exp2(top - new_top) + part
            top_ref[:, lanes] = new_top
        return carry

    lax.fori_loop(0, k_ref.shape[0] // CHUNK, step, 0)


def near_kernel(
    scale, order_ref, own_ref, q_ref, k_ref, top_in, tot_in, map_ref, top_ref, tot_ref, pool_ref
):
    top_ref[...] = top_in[...]
    tot_ref[...] = tot_in[...]
    attend(
        scale, own_ref[3], order_ref, own_ref, q_ref, k_ref, top_ref, tot_ref, map_ref, 0, pool_ref, 0
    )


def far_kernel(
    scale,
    order_ref,
    own_ref,
    q_ref,
    k_ref,
    top_in,
    tot_in,
    near_map,
    near_pool,
    diag_ref,
    pooled_ref,
    gate_q_ref,
    wk_ref,
    kb_pos_ref,
    target_ref,
    send_ref,
    pool_ref,
    gate_k_ref,
    map_ref,
    top_ref,
    tot_ref,
    block_ref,
):
    heads, rows, width = q_ref.shape
    half = rows // 2
    blocks = rows // POOL
    near_rows = near_map.shape[0]
    total = 2 * near_rows
    per = half // POOL
    top_ref[...] = top_in[...]
    tot_ref[...] = tot_in[...]
    near_at = pl.multiple_of(own_ref[3] * per, near_rows)
    far_at = pl.multiple_of(own_ref[4] * per, near_rows)
    map_ref[pl.ds(near_at, near_rows), :] = near_map[...]
    pool_ref[pl.ds(near_at, near_rows), :] = near_pool[...]
    attend(
        scale, own_ref[4], order_ref, own_ref, q_ref, k_ref, top_ref, tot_ref, map_ref, far_at, pool_ref, far_at
    )
    block_ref[...] = jnp.ones(block_ref.shape, jnp.float32)
    kb_index = lax.broadcasted_iota(jnp.int32, (total, half), 0)
    own_block = own_ref[0] * blocks
    for h in range(heads):
        for part in range(2):
            lanes = slice(h * rows + part * half, h * rows + (part + 1) * half)
            m = map_ref[:, lanes]
            for j in range(part * per, (part + 1) * per):
                m = jnp.where(kb_index == own_block + j, diag_ref[j : j + 1, lanes], m)
            lse = top_ref[:, lanes] + jnp.log2(jnp.sum(tot_ref[:, lanes], axis=0, keepdims=True))
            b = jnp.exp2(m - lse).T.reshape(per, POOL, total)
            block_ref[h * SUB + part * per : h * SUB + (part + 1) * per, :] = jnp.max(b, axis=1)
    block_map = block_ref[...]
    target = block_map / jnp.sum(block_map, axis=1, keepdims=True)
    for h in range(heads):
        target_ref[h] = target[h * SUB : h * SUB + blocks, :]
    gate_k = dot_nn(pool_ref[...], wk_ref[...], HIGHEST)
    gate_k_ref[...] = gate_k
    gate_width = gate_k.shape[1]
    row = lax.broadcasted_iota(jnp.int32, (heads * SUB, total), 0) % SUB
    query_pos = jnp.where(row < per, own_ref[1], own_ref[2]) * per + row % per
    visible = (kb_pos_ref[...] <= query_pos) & (row < blocks)
    logits = dot_nt(gate_q_ref[...], gate_k, HIGHEST) * gate_width ** (-0.5)
    peak = jnp.max(jnp.where(visible, logits, LOW), axis=1, keepdims=True)
    weights = jnp.where(visible, jnp.exp(logits - peak), 0.0)
    norm_sum = jnp.where(row[:, :1] < blocks, jnp.sum(weights, axis=1, keepdims=True), 1.0)
    log_gate = logits - peak - jnp.log(norm_sum)
    count = heads * total
    loss = -jnp.sum(jnp.where(visible, target * log_gate, 0.0)) / count
    d_logits = jnp.where(visible, weights / norm_sum - target, 0.0) / count * gate_width ** (-0.5)
    msg = jnp.concatenate([d_logits, jnp.zeros((heads * SUB, width - total), jnp.float32)], axis=1)
    msg_row = lax.broadcasted_iota(jnp.int32, msg.shape, 0)
    msg_lane = lax.broadcasted_iota(jnp.int32, msg.shape, 1)
    msg = jnp.where((msg_row == 0) & (msg_lane == total), loss, msg + pooled_ref[...])
    send_ref[...] = jnp.broadcast_to(msg[None], send_ref.shape)


def grad_kernel(got_ref, pool_ref, gate_k_ref, wq_ref, grad_ref, loss_ref):
    peers, msg_rows, width = got_ref.shape
    heads = wq_ref.shape[0]
    total = gate_k_ref.shape[0]
    gate_k = gate_k_ref[...]
    gate_k_grad = jnp.zeros(gate_k.shape, jnp.float32)
    row = lax.broadcasted_iota(jnp.int32, (peers * SUB, width), 0) % SUB
    for h in range(heads):
        both = got_ref[:, h * SUB : (h + 1) * SUB, :].reshape(peers * SUB, width)
        d_logits = jnp.where(row < SUB // 2, both, 0.0)[:, :total]
        pooled = pltpu.roll(both, peers * SUB - SUB // 2, 0)
        mixed = dot_tn(d_logits, pooled, HIGHEST)
        grad_ref[h * width : (h + 1) * width, :] = dot_tn(mixed, gate_k, HIGHEST)
        gate_k_grad = gate_k_grad + dot_nn(mixed, wq_ref[h], HIGHEST)
    grad_ref[heads * width :, :] = dot_tn(pool_ref[...], gate_k_grad, HIGHEST)
    first = got_ref[:, 0, :]
    lane = lax.broadcasted_iota(jnp.int32, first.shape, 1)
    loss_ref[...] = jnp.sum(
        jnp.sum(jnp.where(lane == total, first, 0.0), axis=0, keepdims=True), axis=1, keepdims=True
    )


def on_device(order, queries, keys, w_query_gate, w_key_gate):
    tok_rows = queries.shape[1]
    heads = queries.shape[2]
    width = queries.shape[3]
    per_half = tok_rows // 2 // POOL
    blocks = tok_rows // POOL
    ctx_count = lax.axis_size("ctx")
    seq_count = lax.axis_size("seq")
    near = ctx_count // 2
    total = ctx_count * blocks
    scale = width ** (-0.5) * math.log2(math.e)
    f32 = jnp.float32
    columns = heads * tok_rows

    place = lax.axis_index("ctx")
    group = place // near
    own_halves = lax.dynamic_slice(order, (0, place * 2), (1, 2))[0]
    own = jnp.concatenate(
        [place[None], own_halves, (group * near * 2)[None], ((1 - group) * near * 2)[None]]
    ).astype(jnp.int32)
    kb_pos = (order.reshape(-1, 1) * per_half + jnp.arange(per_half, dtype=jnp.int32)[None]).reshape(1, total)

    groups = [list(range(near)), list(range(near, 2 * near))]
    spread = jnp.broadcast_to(keys, (near,) + keys.shape[1:])
    near_keys = lax.all_to_all(spread, "ctx", 0, 0, axis_index_groups=groups, tiled=True)
    far_keys = lax.ppermute(near_keys, "ctx", [(j, (j + near) % ctx_count) for j in range(ctx_count)])
    near_keys = near_keys.reshape(near * tok_rows, width)
    far_keys = far_keys.reshape(near * tok_rows, width)

    q = jnp.transpose(queries[0], (1, 0, 2))
    diag, top, tot, pooled, gate_q = pl.pallas_call(
        functools.partial(local_kernel, scale),
        out_shape=(
            jax.ShapeDtypeStruct((SUB, columns), f32),
            jax.ShapeDtypeStruct((1, columns), f32),
            jax.ShapeDtypeStruct((SUB, columns), f32),
            jax.ShapeDtypeStruct((heads * SUB, width), f32),
            jax.ShapeDtypeStruct((heads * SUB, width), f32),
        ),
        in_specs=[VMEM] * 3,
        out_specs=(VMEM,) * 5,
        compiler_params=PARAMS,
        name="local",
    )(q, keys[0], w_query_gate)

    flops = 2 * near * tok_rows * columns * width
    near_map, top, tot, near_pool = pl.pallas_call(
        functools.partial(near_kernel, scale),
        out_shape=(
            jax.ShapeDtypeStruct((total // 2, columns), f32),
            jax.ShapeDtypeStruct((1, columns), f32),
            jax.ShapeDtypeStruct((SUB, columns), f32),
            jax.ShapeDtypeStruct((total // 2, 3 * width), f32),
        ),
        in_specs=[SMEM, SMEM] + [VMEM] * 4,
        out_specs=(VMEM,) * 4,
        compiler_params=PARAMS,
        cost_estimate=pl.CostEstimate(
            flops=4 * flops, bytes_accessed=2 * 1024 * 1024, transcendentals=near * tok_rows * columns
        ),
        name="near",
    )(order, own, q, near_keys, top, tot)

    target, send, pool, gate_k = pl.pallas_call(
        functools.partial(far_kernel, scale),
        out_shape=(
            jax.ShapeDtypeStruct((heads, blocks, total), f32),
            jax.ShapeDtypeStruct((ctx_count, heads * SUB, width), f32),
            jax.ShapeDtypeStruct((total, 3 * width), f32),
            jax.ShapeDtypeStruct((total, w_key_gate.shape[1]), f32),
        ),
        in_specs=[SMEM, SMEM] + [VMEM] * 11,
        out_specs=(VMEM,) * 4,
        scratch_shapes=[
            pltpu.VMEM((total, columns), f32),
            pltpu.VMEM((1, columns), f32),
            pltpu.VMEM((SUB, columns), f32),
            pltpu.VMEM((heads * SUB, total), f32),
        ],
        compiler_params=PARAMS,
        name="far",
    )(order, own, q, far_keys, top, tot, near_map, near_pool, diag, pooled, gate_q, w_key_gate, kb_pos)

    got = lax.all_to_all(send, "ctx", 0, 0, tiled=True)
    grads, loss = pl.pallas_call(
        grad_kernel,
        out_shape=(
            jax.ShapeDtypeStruct((heads * width + 3 * width, w_key_gate.shape[1]), f32),
            jax.ShapeDtypeStruct((1, 1), f32),
        ),
        in_specs=[VMEM] * 4,
        out_specs=(VMEM, VMEM),
        compiler_params=PARAMS,
        name="grad",
    )(got, pool, gate_k, w_query_gate)

    tiles = grads.reshape(seq_count, -1, grads.shape[1])
    own_tile = jnp.sum(lax.all_to_all(tiles, "seq", 0, 0, tiled=True), axis=0)
    spread = jnp.broadcast_to(own_tile[None], tiles.shape)
    grads = lax.all_to_all(spread, "seq", 0, 0, tiled=True).reshape(grads.shape)
    grad_q = grads[: heads * width].reshape(heads, width, -1)
    grad_k = grads[heads * width :]
    return (target[None, None], grad_q, grad_k, loss.reshape(1))


def solution(mesh):
    placed = (P("seq", None), P("seq", "ctx", None, None), P("seq", "ctx", None), P(), P())
    return jax.shard_map(
        on_device,
        mesh=mesh,
        in_specs=placed,
        out_specs=(P("seq", "ctx", None, None, None), P(), P(), P("seq")),
        check_vma=False,
    )
```

```python
import functools
import math

import jax
import jax.numpy as jnp
from jax import lax
from jax.experimental import pallas as pl
from jax.experimental.pallas import tpu as pltpu
from jax.sharding import PartitionSpec as P

POOL = 64
LOW = -1e30
HIGHEST = lax.Precision.HIGHEST
VMEM = pl.BlockSpec(memory_space=pltpu.VMEM)
SMEM = pl.BlockSpec(memory_space=pltpu.SMEM)
PARAMS = pltpu.CompilerParams(vmem_limit_bytes=40 * 1024 * 1024)
SUB = 8
CHUNK = 512


def dot_nt(a, b, precision=None):
    return lax.dot_general(
        a, b, (((1,), (1,)), ((), ())), precision=precision, preferred_element_type=jnp.float32
    )


def dot_tn(a, b, precision=None):
    return lax.dot_general(
        a, b, (((0,), (0,)), ((), ())), precision=precision, preferred_element_type=jnp.float32
    )


def dot_nn(a, b, precision=None):
    return lax.dot_general(
        a, b, (((1,), (0,)), ((), ())), precision=precision, preferred_element_type=jnp.float32
    )


def local_kernel(scale, q_ref, k_ref, wq_ref, diag_ref, top_ref, tot_ref, pooled_ref, gate_q_ref):
    heads, rows, width = q_ref.shape
    half = rows // 2
    blocks = rows // POOL
    diag_ref[...] = jnp.full(diag_ref.shape, LOW, jnp.float32)
    key_row = lax.broadcasted_iota(jnp.int32, (half, half), 0)
    query_lane = lax.broadcasted_iota(jnp.int32, (half, half), 1)
    causal = key_row <= query_lane
    blank = jnp.zeros((SUB - blocks, width), jnp.float32)
    for h in range(heads):
        q = q_ref[h]
        pooled = jnp.sum(q.astype(jnp.float32).reshape(blocks, POOL, width), axis=1) * (1.0 / POOL)
        pooled = jnp.concatenate([pooled, blank], axis=0)
        pooled_ref[h * SUB : (h + 1) * SUB, :] = pooled
        gate_q_ref[h * SUB : (h + 1) * SUB, :] = dot_nn(pooled, wq_ref[h], HIGHEST)
        for part in range(2):
            s = dot_nt(k_ref[part * half : (part + 1) * half, :], q[part * half : (part + 1) * half, :])
            s = jnp.where(causal, s * scale, LOW)
            per = half // POOL
            block_top = jnp.max(s.reshape(per, POOL, half), axis=1)
            top = jnp.max(block_top, axis=0, keepdims=True)
            p = jnp.exp2(s - top)
            lanes = slice(h * rows + part * half, h * rows + (part + 1) * half)
            diag_ref[part * per : (part + 1) * per, lanes] = block_top
            top_ref[:, lanes] = top
            tot_ref[:, lanes] = jnp.sum(p.reshape(half // SUB, SUB, half), axis=0)


def spread_kernel(k_ref, out_ref):
    k = k_ref[...]
    for j in range(out_ref.shape[0]):
        out_ref[j] = k


def attend(scale, order_ref, first_half, query_owner, q_ref, k_ref, top_ref, tot_ref, map_ref, pool_ref=None):
    heads, rows, width = q_ref.shape
    half = rows // 2
    per = half // POOL
    kb_count = CHUNK // POOL
    halves = CHUNK // half
    kb_row = lax.broadcasted_iota(jnp.int32, (kb_count, rows), 0)
    lane = lax.broadcasted_iota(jnp.int32, (kb_count, rows), 1)
    query_half = jnp.where(lane < half, order_ref[0, 2 * query_owner], order_ref[0, 2 * query_owner + 1])

    def step(i, carry):
        start = pl.multiple_of(i * CHUNK, CHUNK)
        keys = k_ref[pl.ds(start, CHUNK), :]
        key_half = jnp.full((kb_count, rows), order_ref[0, first_half + i * halves], jnp.int32)
        for j in range(1, halves):
            key_half = jnp.where(kb_row >= j * per, order_ref[0, first_half + i * halves + j], key_half)
        seen = jnp.where(key_half < query_half, 1.0, 0.0)
        seen_rows = jnp.broadcast_to(seen[:, None, :], (kb_count, SUB, rows)) > 0.5
        seen = seen > 0.5
        here = pl.ds(pl.multiple_of(i * kb_count, kb_count), kb_count)
        if pool_ref is not None:
            x = keys.astype(jnp.float32).reshape(kb_count, POOL, width)
            pool_ref[here, 0:width] = jnp.max(x, axis=1)
            pool_ref[here, width : 2 * width] = jnp.min(x, axis=1)
            pool_ref[here, 2 * width : 3 * width] = jnp.sum(x, axis=1) * (1.0 / POOL)
        for h in range(heads):
            lanes = slice(h * rows, (h + 1) * rows)
            s = dot_nt(keys, q_ref[h]) * scale
            s = s.reshape(kb_count, POOL // SUB, SUB, rows)
            block_top = jnp.max(jnp.max(s, axis=1), axis=1)
            block_top = jnp.where(seen, block_top, LOW)
            map_ref[here, lanes] = block_top
            top = top_ref[:, lanes]
            new_top = jnp.maximum(top, jnp.max(block_top, axis=0, keepdims=True))
            part = jnp.sum(jnp.exp2(s - new_top.reshape(1, 1, 1, rows)), axis=1)
            part = jnp.sum(jnp.where(seen_rows, part, 0.0), axis=0)
            tot_ref[:, lanes] = tot_ref[:, lanes] * jnp.exp2(top - new_top) + part
            top_ref[:, lanes] = new_top
        return carry

    lax.fori_loop(0, k_ref.shape[0] // CHUNK, step, 0)


def partner_kernel(scale, order_ref, own_ref, q_ref, k_ref, send_ref, top_ref, tot_ref):
    heads, rows, width = q_ref.shape
    columns = heads * rows
    near = k_ref.shape[0] // POOL
    top_ref[...] = jnp.full(top_ref.shape, LOW, jnp.float32)
    tot_ref[...] = jnp.zeros(tot_ref.shape, jnp.float32)
    attend(
        scale,
        order_ref,
        own_ref[1],
        own_ref[2],
        q_ref,
        k_ref,
        top_ref,
        tot_ref,
        send_ref,
        send_ref.at[:, pl.ds(columns, 3 * width)],
    )
    send_ref[near:, :] = jnp.zeros((send_ref.shape[0] - near, send_ref.shape[1]), jnp.float32)
    send_ref[near : near + 1, 0:columns] = top_ref[...]
    send_ref[near + 1 : near + 2, 0:columns] = jnp.sum(tot_ref[...], axis=0, keepdims=True)


def own_kernel(
    scale, order_ref, own_ref, q_ref, k_ref, top_in, tot_in, sent_ref, wk_ref, map_ref, top_ref, tot_ref, gate_k_ref
):
    columns = map_ref.shape[1]
    near = map_ref.shape[0]
    top_ref[...] = top_in[...]
    tot_ref[...] = tot_in[...]
    gate_k_ref[...] = dot_nn(sent_ref[0:near, columns:], wk_ref[...], HIGHEST)
    attend(scale, order_ref, own_ref[1], own_ref[0], q_ref, k_ref, top_ref, tot_ref, map_ref)


def finish_kernel(
    order_ref,
    own_ref,
    near_map,
    near_top,
    near_tot,
    near_gate_k,
    sent_ref,
    got_ref,
    diag_ref,
    pooled_ref,
    gate_q_ref,
    wk_ref,
    kb_pos_ref,
    target_ref,
    keep_ref,
    give_ref,
    gate_k_ref,
    pool_ref,
    map_ref,
    block_ref,
    grad_ref,
):
    width = pooled_ref.shape[1]
    columns = near_top.shape[1]
    near = near_map.shape[0]
    total = 2 * near
    heads, blocks, _ = target_ref.shape
    rows = columns // heads
    half = rows // 2
    per = half // POOL
    place = own_ref[0]
    near_at = pl.multiple_of(own_ref[1] * per, near)
    far_at = pl.multiple_of(near - own_ref[1] * per, near)
    map_ref[pl.ds(near_at, near), :] = near_map[...]
    map_ref[pl.ds(far_at, near), :] = got_ref[0:near, 0:columns]
    pool_ref[pl.ds(near_at, near), :] = sent_ref[0:near, columns:]
    pool_ref[pl.ds(far_at, near), :] = got_ref[0:near, columns:]
    gate_k_ref[pl.ds(near_at, near), :] = near_gate_k[...]
    gate_k_ref[pl.ds(far_at, near), :] = dot_nn(got_ref[0:near, columns:], wk_ref[...], HIGHEST)
    block_ref[...] = jnp.ones(block_ref.shape, jnp.float32)
    kb_index = lax.broadcasted_iota(jnp.int32, (total, half), 0)
    own_block = place * blocks
    for h in range(heads):
        for part in range(2):
            lanes = slice(h * rows + part * half, h * rows + (part + 1) * half)
            m = map_ref[:, lanes]
            for j in range(part * per, (part + 1) * per):
                m = jnp.where(kb_index == own_block + j, diag_ref[j : j + 1, lanes], m)
            far_top = got_ref[near : near + 1, lanes]
            top = jnp.maximum(near_top[:, lanes], far_top)
            tot = jnp.sum(near_tot[:, lanes], axis=0, keepdims=True) * jnp.exp2(near_top[:, lanes] - top)
            tot = tot + got_ref[near + 1 : near + 2, lanes] * jnp.exp2(far_top - top)
            b = jnp.exp2(m - (top + jnp.log2(tot))).T.reshape(per, POOL, total)
            block_ref[h * SUB + part * per : h * SUB + (part + 1) * per, :] = jnp.max(b, axis=1)
    block_map = block_ref[...]
    target = block_map / jnp.sum(block_map, axis=1, keepdims=True)
    for h in range(heads):
        target_ref[h] = target[h * SUB : h * SUB + blocks, :]
    gate_k = gate_k_ref[...]
    gate_width = gate_k.shape[1]
    row = lax.broadcasted_iota(jnp.int32, (heads * SUB, total), 0) % SUB
    query_half = jnp.where(row < per, order_ref[0, 2 * place], order_ref[0, 2 * place + 1])
    visible = (kb_pos_ref[...] <= query_half * per + row % per) & (row < blocks)
    logits = dot_nt(gate_q_ref[...], gate_k, HIGHEST) * gate_width ** (-0.5)
    peak = jnp.max(jnp.where(visible, logits, LOW), axis=1, keepdims=True)
    weights = jnp.where(visible, jnp.exp(logits - peak), 0.0)
    norm_sum = jnp.where(row[:, :1] < blocks, jnp.sum(weights, axis=1, keepdims=True), 1.0)
    log_gate = logits - peak - jnp.log(norm_sum)
    count = heads * total
    loss = -jnp.sum(jnp.where(visible, target * log_gate, 0.0)) / count
    d_logits = jnp.where(visible, weights / norm_sum - target, 0.0) / count * gate_width ** (-0.5)
    gate_q = gate_q_ref[...]
    gate_q_grad = dot_nn(d_logits, gate_k, HIGHEST)
    for h in range(heads):
        here = slice(h * SUB, (h + 1) * SUB)
        grad_ref[h * width : (h + 1) * width, :] = dot_tn(pooled_ref[here, :], gate_q_grad[here], HIGHEST)
    grad_ref[heads * width :, :] = dot_tn(pool_ref[...], dot_tn(d_logits, gate_q, HIGHEST), HIGHEST)
    part = keep_ref.shape[0]
    keep_ref[...] = grad_ref[pl.ds(pl.multiple_of(own_ref[3] * part, part), part), :]
    give_ref[0:part, :] = grad_ref[pl.ds(pl.multiple_of((1 - own_ref[3]) * part, part), part), :]
    lane = lax.broadcasted_iota(jnp.int32, (SUB, gate_width), 1)
    give_ref[part:, :] = jnp.where(lane == own_ref[4], loss, 0.0)


def fold_kernel(keep_ref, give_ref, got_ref, out_ref):
    tiles, tile_rows, width = out_ref.shape
    part = keep_ref.shape[0]
    rows = part // tiles
    out_ref[:, 0:rows, :] = (keep_ref[...] + got_ref[0:part, :]).reshape(tiles, rows, width)
    loss = give_ref[part:, :] + got_ref[part:, :]
    out_ref[:, rows:, :] = jnp.broadcast_to(loss[None], (tiles, tile_rows - rows, width))


def sum_kernel(parts_ref, out_ref):
    total = jnp.sum(parts_ref[...], axis=0)
    for j in range(out_ref.shape[0]):
        out_ref[j] = total


def join_kernel(own_ref, parts_ref, out_ref, loss_ref):
    total = jnp.sum(parts_ref[...], axis=0)
    rows = out_ref.shape[1]
    for j in range(out_ref.shape[0]):
        out_ref[j] = total[:rows]
    losses = total[rows : rows + 1]
    lane = lax.broadcasted_iota(jnp.int32, losses.shape, 1)
    loss_ref[...] = jnp.sum(jnp.where(lane == own_ref[4], losses, 0.0), axis=1, keepdims=True)


def last_kernel(own_ref, mine_ref, other_ref, grad_q_ref, grad_k_ref):
    heads, width, _ = grad_q_ref.shape
    part = mine_ref.shape[0]
    whole = part // width
    first = own_ref[3] == 0
    for h in range(2 * whole):
        here = slice(h % whole * width, (h % whole + 1) * width)
        mine = first if h < whole else jnp.logical_not(first)
        tile = jnp.where(mine, mine_ref[here, :], other_ref[here, :])
        if h < heads:
            grad_q_ref[h] = tile
        else:
            grad_k_ref[(h - heads) * width : (h - heads + 1) * width, :] = tile


def f32(*shape):
    return jax.ShapeDtypeStruct(shape, jnp.float32)


def call(kernel, out_shape, specs, name, scratch=(), cost=None):
    return pl.pallas_call(
        kernel,
        out_shape=out_shape,
        in_specs=specs,
        out_specs=tuple(VMEM for _ in out_shape),
        scratch_shapes=scratch,
        compiler_params=PARAMS,
        cost_estimate=cost,
        name=name,
    )


def on_device(order, queries, keys, w_query_gate, w_key_gate):
    tok_rows = queries.shape[1]
    heads = queries.shape[2]
    width = queries.shape[3]
    gate_width = w_key_gate.shape[1]
    per_half = tok_rows // 2 // POOL
    blocks = tok_rows // POOL
    ctx_count = lax.axis_size("ctx")
    seq_count = lax.axis_size("seq")
    near = ctx_count // 2
    total = ctx_count * blocks
    scale = width ** (-0.5) * math.log2(math.e)
    columns = heads * tok_rows

    place = lax.axis_index("ctx")
    own_seq = lax.axis_index("seq")
    own = jnp.stack(
        [place, jnp.where(place < near, 0, 2 * near), lax.rem(place + near, ctx_count), lax.rem(own_seq, 2), own_seq]
    ).astype(jnp.int32)
    kb_pos = (order.reshape(-1, 1) * per_half + jnp.arange(per_half, dtype=jnp.int32)[None]).reshape(1, total)

    across = [(j, (j + near) % ctx_count) for j in range(ctx_count)]
    q = jnp.transpose(queries[0], (1, 0, 2))
    partner_q = lax.ppermute(q, "ctx", across)
    (spread,) = call(
        spread_kernel, (jax.ShapeDtypeStruct((near, tok_rows, width), keys.dtype),), [VMEM], "spread"
    )(keys[0])
    groups = [list(range(near)), list(range(near, ctx_count))]
    near_keys = lax.all_to_all(spread, "ctx", 0, 0, axis_index_groups=groups, tiled=True)
    near_keys = near_keys.reshape(near * tok_rows, width)

    diag, top, tot, pooled, gate_q = call(
        functools.partial(local_kernel, scale),
        (f32(SUB, columns), f32(1, columns), f32(SUB, columns), f32(heads * SUB, width), f32(heads * SUB, gate_width)),
        [VMEM] * 3,
        "local",
        cost=pl.CostEstimate(flops=4 * 10**8, bytes_accessed=10**6, transcendentals=10**5),
    )(q, keys[0], w_query_gate)

    cost = pl.CostEstimate(
        flops=8 * near * tok_rows * columns * width,
        bytes_accessed=10**6,
        transcendentals=near * tok_rows * columns,
    )
    state = [pltpu.VMEM((1, columns), jnp.float32), pltpu.VMEM((SUB, columns), jnp.float32)]
    (sent,) = call(
        functools.partial(partner_kernel, scale),
        (f32(near * blocks + SUB, columns + 3 * width),),
        [SMEM, SMEM, VMEM, VMEM],
        "partner",
        scratch=state,
        cost=cost,
    )(order, own, partner_q, near_keys)
    far = lax.ppermute(sent, "ctx", across)

    near_map, top, tot, near_gate_k = call(
        functools.partial(own_kernel, scale),
        (f32(near * blocks, columns), f32(1, columns), f32(SUB, columns), f32(near * blocks, gate_width)),
        [SMEM, SMEM] + [VMEM] * 6,
        "own",
        cost=cost,
    )(order, own, q, near_keys, top, tot, sent, w_key_gate)

    grad_rows = heads * width + 3 * width
    part = grad_rows // 2
    target, keep, give = call(
        finish_kernel,
        (f32(heads, blocks, total), f32(part, gate_width), f32(part + SUB, gate_width)),
        [SMEM, SMEM] + [VMEM] * 11,
        "finish",
        scratch=[
            pltpu.VMEM((total, gate_width), jnp.float32),
            pltpu.VMEM((total, 3 * width), jnp.float32),
            pltpu.VMEM((total, columns), jnp.float32),
            pltpu.VMEM((heads * SUB, total), jnp.float32),
            pltpu.VMEM((grad_rows, gate_width), jnp.float32),
        ],
    )(order, own, near_map, top, tot, near_gate_k, sent, far, diag, pooled, gate_q, w_key_gate, kb_pos)

    every = ("seq", "ctx")
    half_seq = seq_count // 2

    def flat(x_lo, y, core, x_hi, z):
        return (x_lo * half_seq + y * 2 + core) * ctx_count + x_hi * near + z

    ys = range(half_seq // 2)
    zs = range(near)
    pair = (0, 1)
    cores = [
        (flat(a, y, b, c, z), flat(a, y, 1 - b, c, z)) for a in pair for y in ys for b in pair for c in pair for z in zs
    ]
    planes = [[flat(a, y, b, c, z) for a in pair for c in pair for y in ys] for b in pair for z in zs]
    tiles = len(planes[0])
    got = lax.ppermute(give, every, cores)
    (parts,) = call(
        fold_kernel, (f32(tiles, part // tiles + SUB, gate_width),), [VMEM] * 3, "fold"
    )(keep, give, got)
    parts = lax.all_to_all(parts, every, 0, 0, axis_index_groups=planes, tiled=True)
    (spread,) = call(sum_kernel, (f32(near, part // tiles + SUB, gate_width),), [VMEM], "sum")(parts)
    parts = lax.all_to_all(spread, "ctx", 0, 0, axis_index_groups=groups, tiled=True)
    spread, loss = call(
        join_kernel, (f32(tiles, part // tiles, gate_width), f32(1, 1)), [SMEM, VMEM], "join"
    )(own, parts)
    mine = lax.all_to_all(spread, every, 0, 0, axis_index_groups=planes, tiled=True).reshape(part, gate_width)
    other = lax.ppermute(mine, every, cores)
    grad_q, grad_k = call(
        last_kernel,
        (f32(heads, width, gate_width), f32(3 * width, gate_width)),
        [SMEM, VMEM, VMEM],
        "last",
    )(own, mine, other)
    return (target[None, None], grad_q, grad_k, loss.reshape(1))


def solution(mesh):
    placed = (P("seq", None), P("seq", "ctx", None, None), P("seq", "ctx", None), P(), P())
    return jax.shard_map(
        on_device,
        mesh=mesh,
        in_specs=placed,
        out_specs=(P("seq", "ctx", None, None, None), P(), P(), P("seq")),
        check_vma=False,
    )
```

```python
import functools
import math

import jax
import jax.numpy as jnp
from jax import lax
from jax.experimental import pallas as pl
from jax.experimental.pallas import tpu as pltpu
from jax.sharding import PartitionSpec as P

POOL = 64
LOW = -1e30
HIGHEST = lax.Precision.HIGHEST
VMEM = pl.BlockSpec(memory_space=pltpu.VMEM)
SMEM = pl.BlockSpec(memory_space=pltpu.SMEM)
ANY = pl.BlockSpec(memory_space=pl.ANY)
PARAMS = pltpu.CompilerParams(vmem_limit_bytes=40 * 1024 * 1024)
SUB = 8
NT = (((1,), (1,)), ((), ()))
TN = (((0,), (0,)), ((), ()))
NN = (((1,), (0,)), ((), ()))


def dot(a, b, dims, precision=None):
    return lax.dot_general(a, b, dims, precision=precision, preferred_element_type=jnp.float32)


def split(x):
    high = x.astype(jnp.bfloat16)
    return high, (x - high.astype(jnp.float32)).astype(jnp.bfloat16)


def dot_split(a, b, dims):
    a_high, a_low = split(a)
    b_high, b_low = split(b)
    return dot(a_high, b_high, dims) + (dot(a_high, b_low, dims) + dot(a_low, b_high, dims))


def local_kernel(scale, q_ref, k_ref, wq_ref, *refs):
    diag_ref, top_ref, tot_ref, pooled_ref, gate_q_ref, q2_ref = refs[-6:]
    heads, rows, width = q_ref.shape
    half = rows // 2
    blocks = rows // POOL
    per = half // POOL
    diag_ref[...] = jnp.full(diag_ref.shape, LOW, jnp.float32)
    key_row = lax.broadcasted_iota(jnp.int32, (half, half), 0)
    query_lane = lax.broadcasted_iota(jnp.int32, (half, half), 1)
    causal = key_row <= query_lane
    blank = jnp.zeros((SUB - blocks, width), jnp.float32)
    for h in range(heads):
        q = q_ref[h].astype(jnp.float32)
        pooled = jnp.sum(q.reshape(blocks, POOL, width), axis=1) * (1.0 / POOL)
        pooled = jnp.concatenate([pooled, blank], axis=0)
        pooled_ref[h * SUB : (h + 1) * SUB, :] = pooled
        gate_q_ref[h * SUB : (h + 1) * SUB, :] = dot(pooled, wq_ref[h], NN, HIGHEST)
        high, low = split(q * scale)
        q2_ref[h, :, 0:width] = high
        q2_ref[h, :, width:] = low
        for part in range(2):
            keys = k_ref[part * half : (part + 1) * half, :]
            s = dot(jnp.concatenate([keys, keys], axis=1), q2_ref[h, part * half : (part + 1) * half, :], NT)
            s = jnp.where(causal, s, LOW)
            block_top = jnp.max(s.reshape(per, POOL, half), axis=1)
            top = jnp.max(block_top, axis=0, keepdims=True)
            p = jnp.exp2(s - top)
            lanes = slice(h * rows + part * half, h * rows + (part + 1) * half)
            diag_ref[part * per : (part + 1) * per, lanes] = block_top
            top_ref[:, lanes] = top
            tot_ref[:, lanes] = jnp.sum(p.reshape(half // SUB, SUB, half), axis=0)


def attend(order_ref, own_ref, q2_ref, chunks, top_in, tot_in, top_ref, tot_ref, map_ref, pool_ref):
    heads, rows, _ = q2_ref.shape
    half = rows // 2
    per = half // POOL
    blocks = rows // POOL
    place, along, near = own_ref[0], own_ref[1], own_ref[3]
    tops = [top_in[:, h * rows : (h + 1) * rows] for h in range(heads)]
    tots = [tot_in[:, h * rows : (h + 1) * rows] for h in range(heads)]
    row = 0
    for first in range(0, len(chunks), 2):
        group = chunks[first : first + 2]
        keys = jnp.concatenate([read() for read, _, _ in group], axis=0)
        count = len(group) * blocks
        x = keys.astype(jnp.float32).reshape(count, POOL, keys.shape[1])
        pool_ref[row : row + count, :] = jnp.concatenate(
            [jnp.max(x, axis=1), jnp.min(x, axis=1), jnp.sum(x, axis=1) * (1.0 / POOL)], axis=1
        )
        kb_row = lax.broadcasted_iota(jnp.int32, (count, rows), 0)
        lane = lax.broadcasted_iota(jnp.int32, (count, rows), 1)
        query_half = jnp.where(lane < half, order_ref[0, 2 * place], order_ref[0, 2 * place + 1])
        key_half = jnp.zeros((count, rows), jnp.int32)
        for j, (_, base, offset) in enumerate(group):
            owner = base + lax.rem(along + offset, near)
            for part in range(2):
                key_half = jnp.where(kb_row >= j * blocks + part * per, order_ref[0, 2 * owner + part], key_half)
        seen = jnp.where(key_half < query_half, 1.0, 0.0)
        seen_rows = jnp.broadcast_to(seen[:, None, :], (count, SUB, rows)) > 0.5
        seen = seen > 0.5
        keys = jnp.concatenate([keys, keys], axis=1)
        for h in range(heads):
            s = dot(keys, q2_ref[h], NT).reshape(count, POOL // SUB, SUB, rows)
            block_top = jnp.max(jnp.max(s, axis=1), axis=1)
            block_top = jnp.where(seen, block_top, LOW)
            map_ref[row : row + count, h * rows : (h + 1) * rows] = block_top
            top = jnp.maximum(tops[h], jnp.max(block_top, axis=0, keepdims=True))
            part = jnp.sum(jnp.exp2(s - top.reshape(1, 1, 1, rows)), axis=1)
            part = jnp.sum(jnp.where(seen_rows, part, 0.0), axis=0)
            tots[h] = tots[h] * jnp.exp2(tops[h] - top) + part
            tops[h] = top
        row += count
    for h in range(heads):
        top_ref[:, h * rows : (h + 1) * rows] = tops[h]
        tot_ref[:, h * rows : (h + 1) * rows] = tots[h]


def chunks_of(refs, layout, own_ref, rows):
    chunks = []
    for ref, (other, offsets) in zip(refs, layout):
        for j, offset in enumerate(offsets):
            read = functools.partial(lambda r, j: r[j * rows : (j + 1) * rows, :], ref, j)
            chunks.append((read, own_ref[2 + 2 * other], offset))
    return chunks


def attend_kernel(layout, *refs):
    order_ref, own_ref, q2_ref, top_in, tot_in = refs[:5]
    top_ref, tot_ref, map_ref, pool_ref = refs[-4:]
    chunks = chunks_of(refs[5:-4], layout, own_ref, q2_ref.shape[1])
    attend(order_ref, own_ref, q2_ref, chunks, top_in, tot_in, top_ref, tot_ref, map_ref, pool_ref)


def finish_kernel(layout, places, *refs):
    order_ref, own_ref, q2_ref, top_in, tot_in, diag_ref, pooled_ref, gate_q_ref, wk_ref, kb_pos_ref = refs[:10]
    key_refs = refs[10 : 10 + len(layout)]
    earlier = refs[10 + len(layout) : -12]
    target_ref, keep_ref, give_ref = refs[-12:-9]
    top_ref, tot_ref, last_map, last_pool, map_ref, rel_pool, pool_ref, block_ref, grad_ref = refs[-9:]
    heads, rows, _ = q2_ref.shape
    half = rows // 2
    per = half // POOL
    blocks = rows // POOL
    total = map_ref.shape[0]
    near = total // 2
    width = pooled_ref.shape[1]
    place = own_ref[0]
    chunks = chunks_of(key_refs, layout, own_ref, rows)
    attend(order_ref, own_ref, q2_ref, chunks, top_in, tot_in, top_ref, tot_ref, last_map, last_pool)
    maps = list(earlier[0::2]) + [last_map]
    pools = list(earlier[1::2]) + [last_pool]
    for map_in, pool_in, where in zip(maps, pools, places):
        for j, (other, offset) in enumerate(where):
            here = slice(other * near + offset * blocks, other * near + (offset + 1) * blocks)
            map_ref[here, :] = map_in[j * blocks : (j + 1) * blocks, :]
            rel_pool[here, :] = pool_in[j * blocks : (j + 1) * blocks, :]
    shift = own_ref[1] * blocks
    for other in range(2):
        at = pl.multiple_of(own_ref[2 + 2 * other] * blocks, near)
        pool_ref[pl.ds(at, near), :] = pltpu.roll(rel_pool[other * near : (other + 1) * near, :], shift, 0)
    block_ref[...] = jnp.ones(block_ref.shape, jnp.float32)
    for h in range(heads):
        for part in range(2):
            lanes = slice(h * rows + part * half, h * rows + (part + 1) * half)
            own_rows = slice(part * per, (part + 1) * per)
            map_ref[own_rows, lanes] = diag_ref[own_rows, lanes]
            tot = jnp.sum(tot_ref[:, lanes], axis=0, keepdims=True)
            b = jnp.exp2(map_ref[:, lanes] - (top_ref[:, lanes] + jnp.log2(tot)))
            b = jnp.max(b.T.reshape(per, POOL, total), axis=1)
            block_ref[h * SUB + part * per : h * SUB + (part + 1) * per, :] = b
    block_map = block_ref[...]
    copies = 128 // near
    group = [
        pltpu.roll(jnp.concatenate([block_map[:, j * near : (j + 1) * near]] * copies, axis=1), shift, 1)[:, :total]
        for j in range(2)
    ]
    lane = lax.broadcasted_iota(jnp.int32, (heads * SUB, total), 1)
    in_near = (lane >= own_ref[2] * blocks) & (lane < (own_ref[2] + own_ref[3]) * blocks)
    block_map = jnp.where(in_near, group[0], group[1])
    target = block_map / jnp.sum(block_map, axis=1, keepdims=True)
    for h in range(heads):
        target_ref[h] = target[h * SUB : h * SUB + blocks, :]
    gate_q = gate_q_ref[...]
    gate_k = dot(pool_ref[...], wk_ref[...], NN, HIGHEST)
    gate_width = gate_k.shape[1]
    row = lax.broadcasted_iota(jnp.int32, (heads * SUB, total), 0) % SUB
    query_half = jnp.where(row < per, order_ref[0, 2 * place], order_ref[0, 2 * place + 1])
    visible = (kb_pos_ref[...] <= query_half * per + row % per) & (row < blocks)
    logits = dot(gate_q, gate_k, NT, HIGHEST) * gate_width ** (-0.5)
    peak = jnp.max(jnp.where(visible, logits, LOW), axis=1, keepdims=True)
    weights = jnp.where(visible, jnp.exp(logits - peak), 0.0)
    norm_sum = jnp.where(row[:, :1] < blocks, jnp.sum(weights, axis=1, keepdims=True), 1.0)
    log_gate = logits - peak - jnp.log(norm_sum)
    count = heads * total
    loss = -jnp.sum(jnp.where(visible, target * log_gate, 0.0)) / count
    d_logits = jnp.where(visible, weights / norm_sum - target, 0.0) / count * gate_width ** (-0.5)
    gate_q_grad = dot_split(d_logits, gate_k, NN)
    for h in range(heads):
        here = slice(h * SUB, (h + 1) * SUB)
        grad_ref[h * width : (h + 1) * width, :] = dot_split(pooled_ref[here, :], gate_q_grad[here], TN)
    grad_ref[heads * width :, :] = dot_split(pool_ref[...], dot_split(d_logits, gate_q, TN), TN)
    part = keep_ref.shape[0]
    keep_ref[...] = grad_ref[pl.ds(pl.multiple_of(own_ref[5] * part, part), part), :]
    give_ref[0:part, :] = grad_ref[pl.ds(pl.multiple_of((1 - own_ref[5]) * part, part), part), :]
    lane = lax.broadcasted_iota(jnp.int32, (SUB, gate_width), 1)
    give_ref[part:, :] = jnp.where(lane == own_ref[6], loss, 0.0)


def fold_kernel(keep_ref, give_ref, got_ref, out_ref):
    tiles, tile_rows, width = out_ref.shape
    part = keep_ref.shape[0]
    rows = part // tiles
    out_ref[:, 0:rows, :] = (keep_ref[...] + got_ref[0:part, :]).reshape(tiles, rows, width)
    loss = give_ref[part:, :] + got_ref[part:, :]
    out_ref[:, rows:, :] = jnp.broadcast_to(loss[None], (tiles, tile_rows - rows, width))


def sum_kernel(parts_ref, out_ref):
    total = jnp.sum(parts_ref[...], axis=0)
    for j in range(out_ref.shape[0]):
        out_ref[j] = total


def join_kernel(parts_ref, out_ref, loss_ref):
    total = jnp.sum(parts_ref[...], axis=0)
    rows = out_ref.shape[1]
    for j in range(out_ref.shape[0]):
        out_ref[j] = total[:rows]
    loss_ref[...] = total[rows:]


def last_kernel(own_ref, mine_ref, other_ref, losses_ref, grad_q_ref, grad_k_ref, loss_ref):
    heads, width, _ = grad_q_ref.shape
    part = mine_ref.shape[0]
    whole = part // width
    first = own_ref[5] == 0
    for h in range(2 * whole):
        here = slice(h % whole * width, (h % whole + 1) * width)
        mine = first if h < whole else jnp.logical_not(first)
        tile = jnp.where(mine, mine_ref[here, :], other_ref[here, :])
        if h < heads:
            grad_q_ref[h] = tile
        else:
            grad_k_ref[(h - heads) * width : (h - heads + 1) * width, :] = tile
    losses = losses_ref[0:1, :]
    lane = lax.broadcasted_iota(jnp.int32, losses.shape, 1)
    loss_ref[...] = jnp.sum(jnp.where(lane == own_ref[6], losses, 0.0), axis=1, keepdims=True)


def f32(*shape):
    return jax.ShapeDtypeStruct(shape, jnp.float32)


def call(kernel, out_shape, specs, name, scratch=(), cost=None):
    return pl.pallas_call(
        kernel,
        out_shape=out_shape,
        in_specs=specs,
        out_specs=tuple(VMEM for _ in out_shape),
        scratch_shapes=scratch,
        compiler_params=PARAMS,
        cost_estimate=cost,
        name=name,
    )


def on_device(order, queries, keys, w_query_gate, w_key_gate):
    tok_rows = queries.shape[1]
    heads = queries.shape[2]
    width = queries.shape[3]
    gate_width = w_key_gate.shape[1]
    per_half = tok_rows // 2 // POOL
    blocks = tok_rows // POOL
    ctx_count = lax.axis_size("ctx")
    seq_count = lax.axis_size("seq")
    near = ctx_count // 2
    total = ctx_count * blocks
    scale = width ** (-0.5) * math.log2(math.e)
    columns = heads * tok_rows

    place = lax.axis_index("ctx")
    own_seq = lax.axis_index("seq")
    along = lax.rem(place, near)
    base = place - along
    index = jnp.arange(8, dtype=jnp.int32)
    own = jnp.zeros((8,), jnp.int32)
    for j, value in enumerate((place, along, base, near, near - base, lax.rem(own_seq, 2), own_seq)):
        own = jnp.where(index == j, value, own)
    kb_pos = (order.reshape(-1, 1) * per_half + jnp.arange(per_half, dtype=jnp.int32)[None]).reshape(1, total)

    def get(x, offset):
        return lax.ppermute(x, "ctx", [(j, j // near * near + (j - offset) % near) for j in range(ctx_count)])

    def across(x):
        return lax.ppermute(x, "ctx", [(j, (j + near) % ctx_count) for j in range(ctx_count)])

    own_keys = keys[0]
    step = {offset: get(own_keys, offset % near) for offset in (1, -1, near // 2)}
    ahead = get(jnp.concatenate([own_keys, step[1]], axis=0), 2)
    behind = get(jnp.concatenate([own_keys, step[-1]], axis=0), near - 2)
    mid = jnp.concatenate([own_keys, step[1], step[-1], step[near // 2]], axis=0)
    mid_far = across(mid)
    mid_from = (0, 1, near - 1, near // 2)
    ahead_from = (2, 3)
    behind_from = (near - 2, near - 3)

    q = jnp.transpose(queries[0], (1, 0, 2))
    state = (f32(1, columns), f32(SUB, columns))
    diag, top, tot, pooled, gate_q, q2 = call(
        functools.partial(local_kernel, scale),
        (f32(SUB, columns),)
        + state
        + (
            f32(heads * SUB, width),
            f32(heads * SUB, gate_width),
            jax.ShapeDtypeStruct((heads, tok_rows, 2 * width), jnp.bfloat16),
        ),
        [VMEM] * 3 + [ANY] * 2,
        "local",
        cost=pl.CostEstimate(flops=4 * 10**8, bytes_accessed=10**6, transcendentals=10**5),
    )(q, own_keys, w_query_gate, step[1], step[-1])

    def attend_to(layout, top, tot, *keys):
        count = sum(len(offsets) for _, offsets in layout)
        return call(
            functools.partial(attend_kernel, layout),
            state + (f32(count * blocks, columns), f32(count * blocks, 3 * width)),
            [SMEM, SMEM] + [VMEM] * (3 + len(keys)),
            "attend",
            cost=pl.CostEstimate(flops=1200000000, bytes_accessed=10**6, transcendentals=1300000),
        )(order, own, q2, top, tot, *keys)

    layouts = (
        ((0, mid_from),),
        ((0, ahead_from), (0, behind_from)),
        ((1, mid_from),),
        ((1, ahead_from), (1, behind_from)),
    )
    places = [[(other, offset) for other, offsets in layout for offset in offsets] for layout in layouts]
    ahead_far = across(ahead)
    behind_far = across(behind)
    earlier = []
    for layout, key_parts in zip(layouts[:-1], ((mid,), (ahead, behind), (mid_far,))):
        top, tot, *found = attend_to(layout, top, tot, *key_parts)
        earlier += found

    grad_rows = heads * width + 3 * width
    part = grad_rows // 2
    last_blocks = len(places[-1]) * blocks
    target, keep, give = call(
        functools.partial(finish_kernel, layouts[-1], places),
        (f32(heads, blocks, total), f32(part, gate_width), f32(part + SUB, gate_width)),
        [SMEM, SMEM] + [VMEM] * (10 + len(earlier)),
        "finish",
        scratch=[
            pltpu.VMEM(shape, jnp.float32)
            for shape in (
                (1, columns),
                (SUB, columns),
                (last_blocks, columns),
                (last_blocks, 3 * width),
                (total, columns),
                (total, 3 * width),
                (total, 3 * width),
                (heads * SUB, total),
                (grad_rows, gate_width),
            )
        ],
    )(order, own, q2, top, tot, diag, pooled, gate_q, w_key_gate, kb_pos, ahead_far, behind_far, *earlier)

    every = ("seq", "ctx")
    half_seq = seq_count // 2

    def flat(x_lo, y, core, x_hi, z):
        return (x_lo * half_seq + y * 2 + core) * ctx_count + x_hi * near + z

    ys = range(half_seq // 2)
    zs = range(near)
    pair = (0, 1)
    cores = [
        (flat(a, y, b, c, z), flat(a, y, 1 - b, c, z)) for a in pair for y in ys for b in pair for c in pair for z in zs
    ]
    planes = [[flat(a, y, b, c, z) for a in pair for c in pair for y in ys] for b in pair for z in zs]
    tiles = len(planes[0])
    got = lax.ppermute(give, every, cores)
    (parts,) = call(
        fold_kernel, (f32(tiles, part // tiles + SUB, gate_width),), [VMEM] * 3, "fold"
    )(keep, give, got)
    parts = lax.all_to_all(parts, every, 0, 0, axis_index_groups=planes, tiled=True)
    (spread,) = call(sum_kernel, (f32(near, part // tiles + SUB, gate_width),), [VMEM], "sum")(parts)
    parts = lax.all_to_all(
        spread,
        "ctx",
        0,
        0,
        axis_index_groups=[list(range(near)), list(range(near, ctx_count))],
        tiled=True,
    )
    spread, losses = call(
        join_kernel, (f32(tiles, part // tiles, gate_width), f32(SUB, gate_width)), [VMEM], "join"
    )(parts)
    mine = lax.all_to_all(spread, every, 0, 0, axis_index_groups=planes, tiled=True).reshape(part, gate_width)
    other = lax.ppermute(mine, every, cores)
    grad_q, grad_k, loss = call(
        last_kernel,
        (f32(heads, width, gate_width), f32(3 * width, gate_width), f32(1, 1)),
        [SMEM, VMEM, VMEM, VMEM],
        "last",
    )(own, mine, other, losses)
    return (target[None, None], grad_q, grad_k, loss.reshape(1))


def solution(mesh):
    placed = (P("seq", None), P("seq", "ctx", None, None), P("seq", "ctx", None), P(), P())
    return jax.shard_map(
        on_device,
        mesh=mesh,
        in_specs=placed,
        out_specs=(P("seq", "ctx", None, None, None), P(), P(), P("seq")),
        check_vma=False,
    )
```

```python
import functools
import math

import jax
import jax.numpy as jnp
from jax import lax
from jax.experimental import pallas as pl
from jax.experimental.pallas import tpu as pltpu
from jax.sharding import PartitionSpec as P

POOL = 64
LOW = -1e30
HIGHEST = lax.Precision.HIGHEST
VMEM = pl.BlockSpec(memory_space=pltpu.VMEM)
ANY = pl.BlockSpec(memory_space=pl.ANY)
PARAMS = pltpu.CompilerParams(vmem_limit_bytes=40 * 1024 * 1024)
SUB = 8
NT = (((1,), (1,)), ((), ()))
TN = (((0,), (0,)), ((), ()))
NN = (((1,), (0,)), ((), ()))


def dot(a, b, dims, precision=None):
    return lax.dot_general(a, b, dims, precision=precision, preferred_element_type=jnp.float32)


def split(x):
    high = x.astype(jnp.bfloat16)
    return high, (x - high.astype(jnp.float32)).astype(jnp.bfloat16)


def dot_split(a, b, dims):
    a_high, a_low = split(a)
    b_high, b_low = split(b)
    return dot(a_high, b_high, dims) + (dot(a_high, b_low, dims) + dot(a_low, b_high, dims))


def pick(values, index):
    lane = lax.broadcasted_iota(jnp.int32, (index.shape[0], values.shape[1]), 1)
    return jnp.sum(jnp.where(lane == index, values, 0.0), axis=1, keepdims=True)


def local_kernel(scale, near, q_ref, k_ref, wq_ref, order_ref, *refs):
    diag_ref, top_ref, tot_ref, pooled_ref, gate_q_ref, q2_ref, seen_ref, visible_ref = refs[-8:]
    heads, rows, width = q_ref.shape
    half = rows // 2
    blocks = rows // POOL
    per = half // POOL
    diag_ref[...] = jnp.full(diag_ref.shape, LOW, jnp.float32)
    key_row = lax.broadcasted_iota(jnp.int32, (half, half), 0)
    query_lane = lax.broadcasted_iota(jnp.int32, (half, half), 1)
    causal = key_row <= query_lane
    blank = jnp.zeros((SUB - blocks, width), jnp.float32)
    for h in range(heads):
        q = q_ref[h].astype(jnp.float32)
        pooled = jnp.sum(q.reshape(blocks, POOL, width), axis=1) * (1.0 / POOL)
        pooled = jnp.concatenate([pooled, blank], axis=0)
        pooled_ref[h * SUB : (h + 1) * SUB, :] = pooled
        gate_q_ref[h * SUB : (h + 1) * SUB, :] = dot(pooled, wq_ref[h], NN, HIGHEST)
        high, low = split(q * scale)
        q2_ref[h, :, 0:width] = high
        q2_ref[h, :, width:] = low
        for part in range(2):
            keys = k_ref[part * half : (part + 1) * half, :]
            s = dot(jnp.concatenate([keys, keys], axis=1), q2_ref[h, part * half : (part + 1) * half, :], NT)
            s = jnp.where(causal, s, LOW)
            block_top = jnp.max(s.reshape(per, POOL, half), axis=1)
            top = jnp.max(block_top, axis=0, keepdims=True)
            p = jnp.exp2(s - top)
            lanes = slice(h * rows + part * half, h * rows + (part + 1) * half)
            diag_ref[part * per : (part + 1) * per, lanes] = block_top
            top_ref[:, lanes] = top
            tot_ref[:, lanes] = jnp.sum(p.reshape(half // SUB, SUB, half), axis=0)
    place = lax.axis_index("ctx")
    along = lax.rem(place, near)
    base = place - along
    group = near * blocks
    order = order_ref[...].astype(jnp.float32)
    kb = lax.broadcasted_iota(jnp.int32, (2 * group, 1), 0)
    key_half = pick(order, kb // per)
    lane = lax.broadcasted_iota(jnp.int32, (2 * group, rows), 1)
    halves = [pick(order, jnp.full((1, 1), 2 * place + part, jnp.int32)) for part in range(2)]
    seen = jnp.where(key_half < jnp.where(lane < half, halves[0], halves[1]), 1.0, 0.0)
    shift = (near - along) * blocks
    low, high = [pltpu.roll(seen[j * group : (j + 1) * group], shift, 0) for j in range(2)]
    seen_ref[0:group, :] = jnp.where(base == 0, low, high)
    seen_ref[group:, :] = jnp.where(base == 0, high, low)
    key_pos = key_half * per + (kb % per).astype(jnp.float32)
    diagonal = lax.broadcasted_iota(jnp.int32, (2 * group, 2 * group), 1) == kb
    key_pos = jnp.sum(jnp.where(diagonal, key_pos, 0.0), axis=0, keepdims=True)
    row = lax.broadcasted_iota(jnp.int32, (heads * SUB, 1), 0) % SUB
    query_pos = jnp.where(row < per, halves[0], halves[1]) * per + (row % per).astype(jnp.float32)
    visible_ref[...] = jnp.where((key_pos <= query_pos) & (row < blocks), 1.0, 0.0)


def attend(q2_ref, seen_ref, chunks, top_in, tot_in, top_ref, tot_ref, map_ref, pool_ref):
    heads, rows, _ = q2_ref.shape
    blocks = rows // POOL
    tops = [top_in[:, h * rows : (h + 1) * rows] for h in range(heads)]
    tots = [tot_in[:, h * rows : (h + 1) * rows] for h in range(heads)]
    row = 0
    for first in range(0, len(chunks), 2):
        group = chunks[first : first + 2]
        keys = jnp.concatenate([read() for read, _ in group], axis=0)
        count = len(group) * blocks
        x = keys.astype(jnp.float32).reshape(count, POOL, keys.shape[1])
        pool_ref[row : row + count, :] = jnp.concatenate(
            [jnp.max(x, axis=1), jnp.min(x, axis=1), jnp.sum(x, axis=1) * (1.0 / POOL)], axis=1
        )
        seen = jnp.concatenate([seen_ref[at : at + blocks, :] for _, at in group], axis=0)
        seen_rows = jnp.broadcast_to(seen[:, None, :], (count, SUB, rows)) > 0.5
        seen = seen > 0.5
        keys = jnp.concatenate([keys, keys], axis=1)
        for h in range(heads):
            s = dot(keys, q2_ref[h], NT).reshape(count, POOL // SUB, SUB, rows)
            block_top = jnp.max(jnp.max(s, axis=1), axis=1)
            block_top = jnp.where(seen, block_top, LOW)
            map_ref[row : row + count, h * rows : (h + 1) * rows] = block_top
            top = jnp.maximum(tops[h], jnp.max(block_top, axis=0, keepdims=True))
            part = jnp.sum(jnp.exp2(s - top.reshape(1, 1, 1, rows)), axis=1)
            part = jnp.sum(jnp.where(seen_rows, part, 0.0), axis=0)
            tots[h] = tots[h] * jnp.exp2(tops[h] - top) + part
            tops[h] = top
        row += count
    for h in range(heads):
        top_ref[:, h * rows : (h + 1) * rows] = tops[h]
        tot_ref[:, h * rows : (h + 1) * rows] = tots[h]


def chunks_of(refs, layout, rows, group):
    chunks = []
    for ref, (other, offsets) in zip(refs, layout):
        for j, offset in enumerate(offsets):
            read = functools.partial(lambda r, j: r[j * rows : (j + 1) * rows, :], ref, j)
            chunks.append((read, other * group + offset * rows // POOL))
    return chunks


def attend_kernel(layout, *refs):
    q2_ref, seen_ref, top_in, tot_in = refs[:4]
    top_ref, tot_ref, map_ref, pool_ref = refs[-4:]
    chunks = chunks_of(refs[4:-4], layout, q2_ref.shape[1], seen_ref.shape[0] // 2)
    attend(q2_ref, seen_ref, chunks, top_in, tot_in, top_ref, tot_ref, map_ref, pool_ref)


def copy_kernel(in_ref, out_ref):
    out_ref[...] = in_ref[...]


def pair_kernel(own_ref, a_ref, b_ref, ahead_ref, behind_ref):
    rows = own_ref.shape[0]
    for out_ref, other_ref in ((ahead_ref, a_ref), (behind_ref, b_ref)):
        out_ref[0:rows, :] = own_ref[...]
        out_ref[rows:, :] = other_ref[...]


def finish_kernel(layout, places, *refs):
    q2_ref, seen_ref, top_in, tot_in, diag_ref, pooled_ref, gate_q_ref, wk_ref, visible_ref = refs[:9]
    key_refs = refs[9 : 9 + len(layout)]
    earlier = refs[9 + len(layout) : -12]
    target_ref, keep_ref, give_ref = refs[-12:-9]
    top_ref, tot_ref, last_map, last_pool, map_ref, rel_pool, pool_ref, block_ref, grad_ref = refs[-9:]
    heads, rows, _ = q2_ref.shape
    half = rows // 2
    per = half // POOL
    blocks = rows // POOL
    total = map_ref.shape[0]
    near = total // 2
    width = pooled_ref.shape[1]
    devices = near // blocks
    place = lax.axis_index("ctx")
    along = lax.rem(place, devices)
    bases = (place - along, devices - (place - along))
    attend(
        q2_ref, seen_ref, chunks_of(key_refs, layout, rows, near), top_in, tot_in, top_ref, tot_ref, last_map, last_pool
    )
    maps = list(earlier[0::2]) + [last_map]
    pools = list(earlier[1::2]) + [last_pool]
    for map_in, pool_in, where in zip(maps, pools, places):
        for j, (other, offset) in enumerate(where):
            here = slice(other * near + offset * blocks, other * near + (offset + 1) * blocks)
            map_ref[here, :] = map_in[j * blocks : (j + 1) * blocks, :]
            rel_pool[here, :] = pool_in[j * blocks : (j + 1) * blocks, :]
    shift = along * blocks
    for other in range(2):
        at = pl.multiple_of(bases[other] * blocks, near)
        pool_ref[pl.ds(at, near), :] = pltpu.roll(rel_pool[other * near : (other + 1) * near, :], shift, 0)
    block_ref[...] = jnp.ones(block_ref.shape, jnp.float32)
    for h in range(heads):
        for part in range(2):
            lanes = slice(h * rows + part * half, h * rows + (part + 1) * half)
            own_rows = slice(part * per, (part + 1) * per)
            map_ref[own_rows, lanes] = diag_ref[own_rows, lanes]
            tot = jnp.sum(tot_ref[:, lanes], axis=0, keepdims=True)
            b = jnp.exp2(map_ref[:, lanes] - (top_ref[:, lanes] + jnp.log2(tot)))
            b = jnp.max(b.T.reshape(per, POOL, total), axis=1)
            block_ref[h * SUB + part * per : h * SUB + (part + 1) * per, :] = b
    block_map = block_ref[...]
    copies = 128 // near
    group = [
        pltpu.roll(jnp.concatenate([block_map[:, j * near : (j + 1) * near]] * copies, axis=1), shift, 1)[:, :total]
        for j in range(2)
    ]
    lane = lax.broadcasted_iota(jnp.int32, (heads * SUB, total), 1)
    in_near = (lane >= bases[0] * blocks) & (lane < (bases[0] + devices) * blocks)
    block_map = jnp.where(in_near, group[0], group[1])
    target = block_map / jnp.sum(block_map, axis=1, keepdims=True)
    for h in range(heads):
        target_ref[h] = target[h * SUB : h * SUB + blocks, :]
    gate_q = gate_q_ref[...]
    gate_k = dot(pool_ref[...], wk_ref[...], NN, HIGHEST)
    gate_width = gate_k.shape[1]
    row = lax.broadcasted_iota(jnp.int32, (heads * SUB, total), 0) % SUB
    visible = visible_ref[...] > 0.5
    logits = dot(gate_q, gate_k, NT, HIGHEST) * gate_width ** (-0.5)
    peak = jnp.max(jnp.where(visible, logits, LOW), axis=1, keepdims=True)
    weights = jnp.where(visible, jnp.exp(logits - peak), 0.0)
    norm_sum = jnp.where(row[:, :1] < blocks, jnp.sum(weights, axis=1, keepdims=True), 1.0)
    log_gate = logits - peak - jnp.log(norm_sum)
    count = heads * total
    loss = -jnp.sum(jnp.where(visible, target * log_gate, 0.0)) / count
    d_logits = jnp.where(visible, weights / norm_sum - target, 0.0) / count * gate_width ** (-0.5)
    gate_q_grad = dot_split(d_logits, gate_k, NN)
    for h in range(heads):
        here = slice(h * SUB, (h + 1) * SUB)
        grad_ref[h * width : (h + 1) * width, :] = dot_split(pooled_ref[here, :], gate_q_grad[here], TN)
    grad_ref[heads * width :, :] = dot_split(pool_ref[...], dot_split(d_logits, gate_q, TN), TN)
    part = keep_ref.shape[0]
    own_seq = lax.axis_index("seq")
    core = lax.rem(own_seq, 2)
    keep_ref[...] = grad_ref[pl.ds(pl.multiple_of(core * part, part), part), :]
    give_ref[0:part, :] = grad_ref[pl.ds(pl.multiple_of((1 - core) * part, part), part), :]
    lane = lax.broadcasted_iota(jnp.int32, (SUB, gate_width), 1)
    give_ref[part:, :] = jnp.where(lane == own_seq, loss, 0.0)


def fold_kernel(keep_ref, give_ref, got_ref, out_ref):
    tiles, tile_rows, width = out_ref.shape
    part = keep_ref.shape[0]
    rows = part // tiles
    out_ref[:, 0:rows, :] = (keep_ref[...] + got_ref[0:part, :]).reshape(tiles, rows, width)
    loss = give_ref[part:, :] + got_ref[part:, :]
    out_ref[:, rows:, :] = jnp.broadcast_to(loss[None], (tiles, tile_rows - rows, width))


def sum_kernel(parts_ref, out_ref):
    total = jnp.sum(parts_ref[...], axis=0)
    for j in range(out_ref.shape[0]):
        out_ref[j] = total


def join_kernel(parts_ref, out_ref, loss_ref):
    total = jnp.sum(parts_ref[...], axis=0)
    rows = out_ref.shape[1]
    for j in range(out_ref.shape[0]):
        out_ref[j] = total[:rows]
    loss_ref[...] = total[rows:]


def last_kernel(mine_ref, other_ref, losses_ref, grad_q_ref, grad_k_ref, loss_ref, sems):
    tiles = mine_ref.shape[0]
    left = grad_q_ref.shape[0] - tiles
    own_seq = lax.axis_index("seq")
    core = lax.rem(own_seq, 2)

    def write(low_ref, high_ref):
        copies = [
            pltpu.make_async_copy(source, target, sems.at[j])
            for j, (source, target) in enumerate(
                (
                    (low_ref, grad_q_ref.at[pl.ds(0, tiles)]),
                    (high_ref.at[pl.ds(0, left)], grad_q_ref.at[pl.ds(tiles, left)]),
                    (high_ref.at[pl.ds(left, tiles - left)], grad_k_ref),
                )
            )
        ]
        for copy in copies:
            copy.start()
        for copy in copies:
            copy.wait()

    @pl.when(core == 0)
    def _():
        write(mine_ref, other_ref)

    @pl.when(core != 0)
    def _():
        write(other_ref, mine_ref)

    losses = losses_ref[0:1, :]
    lane = lax.broadcasted_iota(jnp.int32, losses.shape, 1)
    loss_ref[...] = jnp.sum(jnp.where(lane == own_seq, losses, 0.0), axis=1, keepdims=True)


def f32(*shape):
    return jax.ShapeDtypeStruct(shape, jnp.float32)


def call(kernel, out_shape, specs, name, scratch=(), cost=None, out_specs=None):
    return pl.pallas_call(
        kernel,
        out_shape=out_shape,
        in_specs=specs,
        out_specs=out_specs or tuple(VMEM for _ in out_shape),
        scratch_shapes=scratch,
        compiler_params=PARAMS,
        cost_estimate=cost,
        name=name,
    )


def on_device(order, queries, keys, w_query_gate, w_key_gate):
    tok_rows = queries.shape[1]
    heads = queries.shape[2]
    width = queries.shape[3]
    gate_width = w_key_gate.shape[1]
    blocks = tok_rows // POOL
    ctx_count = lax.axis_size("ctx")
    seq_count = lax.axis_size("seq")
    near = ctx_count // 2
    total = ctx_count * blocks
    scale = width ** (-0.5) * math.log2(math.e)
    columns = heads * tok_rows

    def get(x, offset):
        return lax.ppermute(x, "ctx", [(j, j // near * near + (j - offset) % near) for j in range(ctx_count)])

    def across(x):
        return lax.ppermute(x, "ctx", [(j, (j + near) % ctx_count) for j in range(ctx_count)])

    own_keys = keys[0]
    step = {offset: get(own_keys, offset % near) for offset in (1, -1, near // 2)}
    (own_copy,) = call(
        copy_kernel,
        (jax.ShapeDtypeStruct(own_keys.shape, keys.dtype),),
        [VMEM],
        "copy",
        cost=pl.CostEstimate(flops=10**9, bytes_accessed=10**6, transcendentals=10**6),
    )(own_keys)
    two_parts = jax.ShapeDtypeStruct((2 * tok_rows, width), keys.dtype)
    ahead, behind = call(pair_kernel, (two_parts, two_parts), [VMEM] * 3, "pair")(own_copy, step[1], step[-1])
    ahead = get(ahead, 2)
    behind = get(behind, near - 2)
    mid = jnp.concatenate([own_copy, step[1], step[-1], step[near // 2]], axis=0)
    mid_far = across(mid)
    mid_from = (0, 1, near - 1, near // 2)
    ahead_from = (2, 3)
    behind_from = (near - 2, near - 3)

    q = jnp.transpose(queries[0], (1, 0, 2))
    state = (f32(1, columns), f32(SUB, columns))
    diag, top, tot, pooled, gate_q, q2, seen, visible = call(
        functools.partial(local_kernel, scale, near),
        (f32(SUB, columns),)
        + state
        + (
            f32(heads * SUB, width),
            f32(heads * SUB, gate_width),
            jax.ShapeDtypeStruct((heads, tok_rows, 2 * width), jnp.bfloat16),
            f32(total, tok_rows),
            f32(heads * SUB, total),
        ),
        [VMEM] * 4 + [ANY] * 2,
        "local",
        cost=pl.CostEstimate(flops=4 * 10**8, bytes_accessed=10**6, transcendentals=10**5),
    )(q, own_copy, w_query_gate, order, step[1], step[-1])

    def attend_to(layout, top, tot, *keys):
        count = sum(len(offsets) for _, offsets in layout)
        return call(
            functools.partial(attend_kernel, layout),
            state + (f32(count * blocks, columns), f32(count * blocks, 3 * width)),
            [VMEM] * (4 + len(keys)),
            "attend",
            cost=pl.CostEstimate(flops=1200000000, bytes_accessed=10**6, transcendentals=1300000),
        )(q2, seen, top, tot, *keys)

    layouts = (
        ((0, mid_from),),
        ((0, ahead_from), (0, behind_from)),
        ((1, mid_from),),
        ((1, ahead_from),),
        ((1, behind_from),),
    )
    places = [[(other, offset) for other, offsets in layout for offset in offsets] for layout in layouts]
    ahead_far = across(ahead)
    behind_far = across(behind)
    earlier = []
    for layout, key_parts in zip(layouts[:-1], ((mid,), (ahead, behind), (mid_far,), (ahead_far,))):
        top, tot, *found = attend_to(layout, top, tot, *key_parts)
        earlier += found

    grad_rows = heads * width + 3 * width
    part = grad_rows // 2
    last_blocks = len(places[-1]) * blocks
    target, keep, give = call(
        functools.partial(finish_kernel, layouts[-1], places),
        (f32(heads, blocks, total), f32(part, gate_width), f32(part + SUB, gate_width)),
        [VMEM] * (10 + len(earlier)),
        "finish",
        scratch=[
            pltpu.VMEM(shape, jnp.float32)
            for shape in (
                (1, columns),
                (SUB, columns),
                (last_blocks, columns),
                (last_blocks, 3 * width),
                (total, columns),
                (total, 3 * width),
                (total, 3 * width),
                (heads * SUB, total),
                (grad_rows, gate_width),
            )
        ],
    )(q2, seen, top, tot, diag, pooled, gate_q, w_key_gate, visible, behind_far, *earlier)

    every = ("seq", "ctx")
    half_seq = seq_count // 2

    def flat(x_lo, y, core, x_hi, z):
        return (x_lo * half_seq + y * 2 + core) * ctx_count + x_hi * near + z

    ys = range(half_seq // 2)
    zs = range(near)
    pair = (0, 1)
    cores = [
        (flat(a, y, b, c, z), flat(a, y, 1 - b, c, z)) for a in pair for y in ys for b in pair for c in pair for z in zs
    ]
    planes = [[flat(a, y, b, c, z) for a in pair for c in pair for y in ys] for b in pair for z in zs]
    tiles = len(planes[0])
    got = lax.ppermute(give, every, cores)
    (parts,) = call(
        fold_kernel, (f32(tiles, part // tiles + SUB, gate_width),), [VMEM] * 3, "fold"
    )(keep, give, got)
    parts = lax.all_to_all(parts, every, 0, 0, axis_index_groups=planes, tiled=True)
    (spread,) = call(sum_kernel, (f32(near, part // tiles + SUB, gate_width),), [VMEM], "sum")(parts)
    parts = lax.all_to_all(
        spread,
        "ctx",
        0,
        0,
        axis_index_groups=[list(range(near)), list(range(near, ctx_count))],
        tiled=True,
    )
    spread, losses = call(
        join_kernel, (f32(tiles, part // tiles, gate_width), f32(SUB, gate_width)), [VMEM], "join"
    )(parts)
    mine = lax.all_to_all(spread, every, 0, 0, axis_index_groups=planes, tiled=True).reshape(part, gate_width)
    other = lax.ppermute(mine, every, cores)
    tiled = (part // width, width, gate_width)
    grad_q, grad_k, loss = call(
        last_kernel,
        (f32(heads, width, gate_width), f32(3, width, gate_width), f32(1, 1)),
        [VMEM] * 3,
        "last",
        scratch=[pltpu.SemaphoreType.DMA((3,))],
        out_specs=(ANY, ANY, VMEM),
    )(mine.reshape(tiled), other.reshape(tiled), losses)
    return (target[None, None], grad_q, grad_k.reshape(3 * width, gate_width), loss.reshape(1))


def solution(mesh):
    placed = (P("seq", None), P("seq", "ctx", None, None), P("seq", "ctx", None), P(), P())
    return jax.shard_map(
        on_device,
        mesh=mesh,
        in_specs=placed,
        out_specs=(P("seq", "ctx", None, None, None), P(), P(), P("seq")),
        check_vma=False,
    )
```

```python
import functools
import math

import jax
import jax.numpy as jnp
from jax import lax
from jax.experimental import pallas as pl
from jax.experimental.pallas import tpu as pltpu
from jax.sharding import PartitionSpec as P

POOL = 64
LOW = -1e30
HIGHEST = lax.Precision.HIGHEST
VMEM = pl.BlockSpec(memory_space=pltpu.VMEM)
ANY = pl.BlockSpec(memory_space=pl.ANY)
PARAMS = pltpu.CompilerParams(vmem_limit_bytes=40 * 1024 * 1024)
SUB = 8
NT = (((1,), (1,)), ((), ()))
TN = (((0,), (0,)), ((), ()))
NN = (((1,), (0,)), ((), ()))


def dot(a, b, dims, precision=None):
    return lax.dot_general(a, b, dims, precision=precision, preferred_element_type=jnp.float32)


def split(x):
    high = x.astype(jnp.bfloat16)
    return high, (x - high.astype(jnp.float32)).astype(jnp.bfloat16)


def dot_split(a, b, dims):
    a_high, a_low = split(a)
    b_high, b_low = split(b)
    return dot(a_high, b_high, dims) + (dot(a_high, b_low, dims) + dot(a_low, b_high, dims))


def pick(values, index):
    lane = lax.broadcasted_iota(jnp.int32, (index.shape[0], values.shape[1]), 1)
    return jnp.sum(jnp.where(lane == index, values, 0.0), axis=1, keepdims=True)


def local_kernel(scale, near, q_ref, k_ref, wq_ref, order_ref, *refs):
    diag_ref, top_ref, tot_ref, pooled_ref, gate_q_ref, q2_ref, seen_ref, visible_ref = refs[-8:]
    heads, rows, width = q_ref.shape
    half = rows // 2
    blocks = rows // POOL
    per = half // POOL
    diag_ref[...] = jnp.full(diag_ref.shape, LOW, jnp.float32)
    key_row = lax.broadcasted_iota(jnp.int32, (half, half), 0)
    query_lane = lax.broadcasted_iota(jnp.int32, (half, half), 1)
    causal = key_row <= query_lane
    blank = jnp.zeros((SUB - blocks, width), jnp.float32)
    for h in range(heads):
        q = q_ref[h].astype(jnp.float32)
        pooled = jnp.sum(q.reshape(blocks, POOL, width), axis=1) * (1.0 / POOL)
        pooled = jnp.concatenate([pooled, blank], axis=0)
        pooled_ref[h * SUB : (h + 1) * SUB, :] = pooled
        gate_q_ref[h * SUB : (h + 1) * SUB, :] = dot(pooled, wq_ref[h], NN, HIGHEST)
        high, low = split(q * scale)
        q2_ref[h, :, 0:width] = high
        q2_ref[h, :, width:] = low
        for part in range(2):
            keys = k_ref[part * half : (part + 1) * half, :]
            s = dot(jnp.concatenate([keys, keys], axis=1), q2_ref[h, part * half : (part + 1) * half, :], NT)
            s = jnp.where(causal, s, LOW)
            block_top = jnp.max(s.reshape(per, POOL, half), axis=1)
            top = jnp.max(block_top, axis=0, keepdims=True)
            p = jnp.exp2(s - top)
            lanes = slice(h * rows + part * half, h * rows + (part + 1) * half)
            diag_ref[part * per : (part + 1) * per, lanes] = block_top
            top_ref[:, lanes] = top
            tot_ref[:, lanes] = jnp.sum(p.reshape(half // SUB, SUB, half), axis=0)
    place = lax.axis_index("ctx")
    along = lax.rem(place, near)
    base = place - along
    group = near * blocks
    order = order_ref[...].astype(jnp.float32)
    kb = lax.broadcasted_iota(jnp.int32, (2 * group, 1), 0)
    key_half = pick(order, kb // per)
    lane = lax.broadcasted_iota(jnp.int32, (2 * group, rows), 1)
    halves = [pick(order, jnp.full((1, 1), 2 * place + part, jnp.int32)) for part in range(2)]
    seen = jnp.where(key_half < jnp.where(lane < half, halves[0], halves[1]), 1.0, 0.0)
    shift = (near - along) * blocks
    low, high = [pltpu.roll(seen[j * group : (j + 1) * group], shift, 0) for j in range(2)]
    seen_ref[0:group, :] = jnp.where(base == 0, low, high)
    seen_ref[group:, :] = jnp.where(base == 0, high, low)
    key_pos = key_half * per + (kb % per).astype(jnp.float32)
    diagonal = lax.broadcasted_iota(jnp.int32, (2 * group, 2 * group), 1) == kb
    key_pos = jnp.sum(jnp.where(diagonal, key_pos, 0.0), axis=0, keepdims=True)
    row = lax.broadcasted_iota(jnp.int32, (heads * SUB, 1), 0) % SUB
    query_pos = jnp.where(row < per, halves[0], halves[1]) * per + (row % per).astype(jnp.float32)
    visible_ref[...] = jnp.where((key_pos <= query_pos) & (row < blocks), 1.0, 0.0)


def attend(q2_ref, seen_ref, chunks, top_in, tot_in, top_ref, tot_ref, map_ref, pool_ref):
    heads, rows, _ = q2_ref.shape
    blocks = rows // POOL
    tops = [top_in[:, h * rows : (h + 1) * rows] for h in range(heads)]
    tots = [tot_in[:, h * rows : (h + 1) * rows] for h in range(heads)]
    row = 0
    for first in range(0, len(chunks), 2):
        group = chunks[first : first + 2]
        keys = jnp.concatenate([read() for read, _ in group], axis=0)
        count = len(group) * blocks
        x = keys.astype(jnp.float32).reshape(count, POOL, keys.shape[1])
        pool_ref[row : row + count, :] = jnp.concatenate(
            [jnp.max(x, axis=1), jnp.min(x, axis=1), jnp.sum(x, axis=1) * (1.0 / POOL)], axis=1
        )
        seen = jnp.concatenate([seen_ref[at : at + blocks, :] for _, at in group], axis=0)
        seen_rows = jnp.broadcast_to(seen[:, None, :], (count, SUB, rows)) > 0.5
        seen = seen > 0.5
        keys = jnp.concatenate([keys, keys], axis=1)
        for h in range(heads):
            s = dot(keys, q2_ref[h], NT).reshape(count, POOL // SUB, SUB, rows)
            block_top = jnp.max(jnp.max(s, axis=1), axis=1)
            block_top = jnp.where(seen, block_top, LOW)
            map_ref[row : row + count, h * rows : (h + 1) * rows] = block_top
            top = jnp.maximum(tops[h], jnp.max(block_top, axis=0, keepdims=True))
            part = jnp.sum(jnp.exp2(s - top.reshape(1, 1, 1, rows)), axis=1)
            part = jnp.sum(jnp.where(seen_rows, part, 0.0), axis=0)
            tots[h] = tots[h] * jnp.exp2(tops[h] - top) + part
            tops[h] = top
        row += count
    for h in range(heads):
        top_ref[:, h * rows : (h + 1) * rows] = tops[h]
        tot_ref[:, h * rows : (h + 1) * rows] = tots[h]


def chunks_of(refs, layout, rows, group):
    chunks = []
    for ref, (other, offsets) in zip(refs, layout):
        for j, offset in enumerate(offsets):
            read = functools.partial(lambda r, j: r[j * rows : (j + 1) * rows, :], ref, j)
            chunks.append((read, other * group + offset * rows // POOL))
    return chunks


def attend_kernel(layout, *refs):
    q2_ref, seen_ref, top_in, tot_in = refs[:4]
    top_ref, tot_ref, map_ref, pool_ref = refs[-4:]
    chunks = chunks_of(refs[4:-4], layout, q2_ref.shape[1], seen_ref.shape[0] // 2)
    attend(q2_ref, seen_ref, chunks, top_in, tot_in, top_ref, tot_ref, map_ref, pool_ref)


def copy_kernel(in_ref, out_ref):
    out_ref[...] = in_ref[...]


def pair_kernel(own_ref, a_ref, b_ref, ahead_ref, behind_ref):
    rows = own_ref.shape[0]
    for out_ref, other_ref in ((ahead_ref, a_ref), (behind_ref, b_ref)):
        out_ref[0:rows, :] = own_ref[...]
        out_ref[rows:, :] = other_ref[...]


def finish_kernel(layout, places, *refs):
    q2_ref, seen_ref, top_in, tot_in, diag_ref, pooled_ref, gate_q_ref, wk_ref, visible_ref = refs[:9]
    key_refs = refs[9 : 9 + len(layout)]
    earlier = refs[9 + len(layout) : -12]
    target_ref, keep_ref, give_ref = refs[-12:-9]
    top_ref, tot_ref, last_map, last_pool, map_ref, rel_pool, pool_ref, block_ref, grad_ref = refs[-9:]
    heads, rows, _ = q2_ref.shape
    half = rows // 2
    per = half // POOL
    blocks = rows // POOL
    total = map_ref.shape[0]
    near = total // 2
    width = pooled_ref.shape[1]
    devices = near // blocks
    place = lax.axis_index("ctx")
    along = lax.rem(place, devices)
    bases = (place - along, devices - (place - along))
    attend(
        q2_ref, seen_ref, chunks_of(key_refs, layout, rows, near), top_in, tot_in, top_ref, tot_ref, last_map, last_pool
    )
    maps = list(earlier[0::2]) + [last_map]
    pools = list(earlier[1::2]) + [last_pool]
    for map_in, pool_in, where in zip(maps, pools, places):
        for j, (other, offset) in enumerate(where):
            here = slice(other * near + offset * blocks, other * near + (offset + 1) * blocks)
            map_ref[here, :] = map_in[j * blocks : (j + 1) * blocks, :]
            rel_pool[here, :] = pool_in[j * blocks : (j + 1) * blocks, :]
    shift = along * blocks
    for other in range(2):
        at = pl.multiple_of(bases[other] * blocks, near)
        pool_ref[pl.ds(at, near), :] = pltpu.roll(rel_pool[other * near : (other + 1) * near, :], shift, 0)
    block_ref[...] = jnp.ones(block_ref.shape, jnp.float32)
    for h in range(heads):
        for part in range(2):
            lanes = slice(h * rows + part * half, h * rows + (part + 1) * half)
            own_rows = slice(part * per, (part + 1) * per)
            map_ref[own_rows, lanes] = diag_ref[own_rows, lanes]
            tot = jnp.sum(tot_ref[:, lanes], axis=0, keepdims=True)
            b = jnp.exp2(map_ref[:, lanes] - (top_ref[:, lanes] + jnp.log2(tot)))
            b = jnp.max(b.T.reshape(per, POOL, total), axis=1)
            block_ref[h * SUB + part * per : h * SUB + (part + 1) * per, :] = b
    block_map = block_ref[...]
    copies = 128 // near
    group = [
        pltpu.roll(jnp.concatenate([block_map[:, j * near : (j + 1) * near]] * copies, axis=1), shift, 1)[:, :total]
        for j in range(2)
    ]
    lane = lax.broadcasted_iota(jnp.int32, (heads * SUB, total), 1)
    in_near = (lane >= bases[0] * blocks) & (lane < (bases[0] + devices) * blocks)
    block_map = jnp.where(in_near, group[0], group[1])
    target = block_map / jnp.sum(block_map, axis=1, keepdims=True)
    for h in range(heads):
        target_ref[h] = target[h * SUB : h * SUB + blocks, :]
    gate_q = gate_q_ref[...]
    gate_k = dot(pool_ref[...], wk_ref[...], NN, HIGHEST)
    gate_width = gate_k.shape[1]
    row = lax.broadcasted_iota(jnp.int32, (heads * SUB, total), 0) % SUB
    visible = visible_ref[...] > 0.5
    logits = dot(gate_q, gate_k, NT, HIGHEST) * gate_width ** (-0.5)
    peak = jnp.max(jnp.where(visible, logits, LOW), axis=1, keepdims=True)
    weights = jnp.where(visible, jnp.exp(logits - peak), 0.0)
    norm_sum = jnp.where(row[:, :1] < blocks, jnp.sum(weights, axis=1, keepdims=True), 1.0)
    log_gate = logits - peak - jnp.log(norm_sum)
    count = heads * total
    loss = -jnp.sum(jnp.where(visible, target * log_gate, 0.0)) / count
    d_logits = jnp.where(visible, weights / norm_sum - target, 0.0) / count * gate_width ** (-0.5)
    gate_q_grad = dot_split(d_logits, gate_k, NN)
    for h in range(heads):
        here = slice(h * SUB, (h + 1) * SUB)
        grad_ref[h * width : (h + 1) * width, :] = dot_split(pooled_ref[here, :], gate_q_grad[here], TN)
    grad_ref[heads * width :, :] = dot_split(pool_ref[...], dot_split(d_logits, gate_q, TN), TN)
    part = keep_ref.shape[0]
    own_seq = lax.axis_index("seq")
    core = lax.rem(own_seq, 2)
    keep_ref[...] = grad_ref[pl.ds(pl.multiple_of(core * part, part), part), :]
    give_ref[0:part, :] = grad_ref[pl.ds(pl.multiple_of((1 - core) * part, part), part), :]
    lane = lax.broadcasted_iota(jnp.int32, (SUB, gate_width), 1)
    give_ref[part:, :] = jnp.where(lane == own_seq, loss, 0.0)


def fold_kernel(keep_ref, give_ref, got_ref, out_ref):
    tiles, tile_rows, width = out_ref.shape
    part = keep_ref.shape[0]
    rows = part // tiles
    out_ref[:, 0:rows, :] = (keep_ref[...] + got_ref[0:part, :]).reshape(tiles, rows, width)
    loss = give_ref[part:, :] + got_ref[part:, :]
    out_ref[:, rows:, :] = jnp.broadcast_to(loss[None], (tiles, tile_rows - rows, width))


def sum_kernel(parts_ref, out_ref):
    total = jnp.sum(parts_ref[...], axis=0)
    for j in range(out_ref.shape[0]):
        out_ref[j] = total


def join_kernel(parts_ref, out_ref, loss_ref):
    total = jnp.sum(parts_ref[...], axis=0)
    rows = out_ref.shape[1]
    for j in range(out_ref.shape[0]):
        out_ref[j] = total[:rows]
    loss_ref[...] = total[rows:]


def last_kernel(
    mine_ref, other_ref, losses_ref, target_in, grad_q_ref, grad_k_ref, loss_ref, target_ref, loss_row, sems
):
    tiles = mine_ref.shape[0]
    left = grad_q_ref.shape[0] - tiles
    own_seq = lax.axis_index("seq")
    core = lax.rem(own_seq, 2)

    def grads(low_ref, high_ref):
        pairs = (
            (low_ref, grad_q_ref.at[pl.ds(0, tiles)]),
            (high_ref.at[pl.ds(0, left)], grad_q_ref.at[pl.ds(tiles, left)]),
            (high_ref.at[pl.ds(left, tiles - left)], grad_k_ref),
        )
        return [pltpu.make_async_copy(source, target, sems.at[j]) for j, (source, target) in enumerate(pairs)]

    @pl.when(core == 0)
    def _():
        for copy in grads(mine_ref, other_ref):
            copy.start()

    @pl.when(core != 0)
    def _():
        for copy in grads(other_ref, mine_ref):
            copy.start()

    losses = losses_ref[0:1, :]
    lane = lax.broadcasted_iota(jnp.int32, losses.shape, 1)
    loss_row[...] = jnp.sum(jnp.where(lane == own_seq, losses, 0.0), axis=1, keepdims=True)
    rest = [
        pltpu.make_async_copy(loss_row, loss_ref, sems.at[3]),
        pltpu.make_async_copy(target_in, target_ref, sems.at[4]),
    ]
    for copy in rest:
        copy.start()
    for copy in grads(mine_ref, other_ref) + rest:
        copy.wait()


def f32(*shape):
    return jax.ShapeDtypeStruct(shape, jnp.float32)


def call(kernel, out_shape, specs, name, scratch=(), cost=None, out_specs=None):
    return pl.pallas_call(
        kernel,
        out_shape=out_shape,
        in_specs=specs,
        out_specs=out_specs or tuple(VMEM for _ in out_shape),
        scratch_shapes=scratch,
        compiler_params=PARAMS,
        cost_estimate=cost,
        name=name,
    )


def on_device(order, queries, keys, w_query_gate, w_key_gate):
    tok_rows = queries.shape[1]
    heads = queries.shape[2]
    width = queries.shape[3]
    gate_width = w_key_gate.shape[1]
    blocks = tok_rows // POOL
    ctx_count = lax.axis_size("ctx")
    seq_count = lax.axis_size("seq")
    near = ctx_count // 2
    total = ctx_count * blocks
    scale = width ** (-0.5) * math.log2(math.e)
    columns = heads * tok_rows

    def get(x, offset):
        return lax.ppermute(x, "ctx", [(j, j // near * near + (j - offset) % near) for j in range(ctx_count)])

    def across(x):
        return lax.ppermute(x, "ctx", [(j, (j + near) % ctx_count) for j in range(ctx_count)])

    own_keys = keys[0]
    step = {offset: get(own_keys, offset % near) for offset in (1, -1, near // 2)}
    (own_copy,) = call(
        copy_kernel,
        (jax.ShapeDtypeStruct(own_keys.shape, keys.dtype),),
        [VMEM],
        "copy",
        cost=pl.CostEstimate(flops=10**9, bytes_accessed=10**6, transcendentals=10**6),
    )(own_keys)
    two_parts = jax.ShapeDtypeStruct((2 * tok_rows, width), keys.dtype)
    ahead, behind = call(pair_kernel, (two_parts, two_parts), [VMEM] * 3, "pair")(own_copy, step[1], step[-1])
    ahead = get(ahead, 2)
    behind = get(behind, near - 2)
    mid = jnp.concatenate([own_copy, step[1], step[-1]], axis=0)
    mid_far = across(mid)
    mid_from = (0, 1, near - 1)
    quad_from = (near // 2,)
    ahead_from = (2, 3)
    behind_from = (near - 2, near - 3)

    q = jnp.transpose(queries[0], (1, 0, 2))
    state = (f32(1, columns), f32(SUB, columns))
    diag, top, tot, pooled, gate_q, q2, seen, visible = call(
        functools.partial(local_kernel, scale, near),
        (f32(SUB, columns),)
        + state
        + (
            f32(heads * SUB, width),
            f32(heads * SUB, gate_width),
            jax.ShapeDtypeStruct((heads, tok_rows, 2 * width), jnp.bfloat16),
            f32(total, tok_rows),
            f32(heads * SUB, total),
        ),
        [VMEM] * 4 + [ANY] * 2,
        "local",
        cost=pl.CostEstimate(flops=4 * 10**8, bytes_accessed=10**6, transcendentals=10**5),
    )(q, own_copy, w_query_gate, order, step[1], step[-1])

    def attend_to(layout, top, tot, *keys):
        count = sum(len(offsets) for _, offsets in layout)
        return call(
            functools.partial(attend_kernel, layout),
            state + (f32(count * blocks, columns), f32(count * blocks, 3 * width)),
            [VMEM] * (4 + len(keys)),
            "attend",
            cost=pl.CostEstimate(flops=1200000000, bytes_accessed=10**6, transcendentals=1300000),
        )(q2, seen, top, tot, *keys)

    layouts = (
        ((0, mid_from),),
        ((0, ahead_from), (0, behind_from), (0, quad_from)),
        ((1, mid_from), (1, quad_from)),
        ((1, ahead_from),),
        ((1, behind_from),),
    )
    places = [[(other, offset) for other, offsets in layout for offset in offsets] for layout in layouts]
    quad = step[near // 2]
    quad_far = across(quad)
    ahead_far = across(ahead)
    behind_far = across(behind)
    earlier = []
    for layout, key_parts in zip(layouts[:-1], ((mid,), (ahead, behind, quad), (mid_far, quad_far), (ahead_far,))):
        top, tot, *found = attend_to(layout, top, tot, *key_parts)
        earlier += found

    grad_rows = heads * width + 3 * width
    part = grad_rows // 2
    last_blocks = len(places[-1]) * blocks
    target, keep, give = call(
        functools.partial(finish_kernel, layouts[-1], places),
        (f32(heads, blocks, total), f32(part, gate_width), f32(part + SUB, gate_width)),
        [VMEM] * (10 + len(earlier)),
        "finish",
        scratch=[
            pltpu.VMEM(shape, jnp.float32)
            for shape in (
                (1, columns),
                (SUB, columns),
                (last_blocks, columns),
                (last_blocks, 3 * width),
                (total, columns),
                (total, 3 * width),
                (total, 3 * width),
                (heads * SUB, total),
                (grad_rows, gate_width),
            )
        ],
    )(q2, seen, top, tot, diag, pooled, gate_q, w_key_gate, visible, behind_far, *earlier)

    every = ("seq", "ctx")
    half_seq = seq_count // 2

    def flat(x_lo, y, core, x_hi, z):
        return (x_lo * half_seq + y * 2 + core) * ctx_count + x_hi * near + z

    ys = range(half_seq // 2)
    zs = range(near)
    pair = (0, 1)
    cores = [
        (flat(a, y, b, c, z), flat(a, y, 1 - b, c, z)) for a in pair for y in ys for b in pair for c in pair for z in zs
    ]
    planes = [[flat(a, y, b, c, z) for a in pair for c in pair for y in ys] for b in pair for z in zs]
    tiles = len(planes[0])
    got = lax.ppermute(give, every, cores)
    (parts,) = call(
        fold_kernel, (f32(tiles, part // tiles + SUB, gate_width),), [VMEM] * 3, "fold"
    )(keep, give, got)
    parts = lax.all_to_all(parts, every, 0, 0, axis_index_groups=planes, tiled=True)
    (spread,) = call(sum_kernel, (f32(near, part // tiles + SUB, gate_width),), [VMEM], "sum")(parts)
    parts = lax.all_to_all(
        spread,
        "ctx",
        0,
        0,
        axis_index_groups=[list(range(near)), list(range(near, ctx_count))],
        tiled=True,
    )
    spread, losses = call(
        join_kernel, (f32(tiles, part // tiles, gate_width), f32(SUB, gate_width)), [VMEM], "join"
    )(parts)
    mine = lax.all_to_all(spread, every, 0, 0, axis_index_groups=planes, tiled=True).reshape(part, gate_width)
    other = lax.ppermute(mine, every, cores)
    tiled = (part // width, width, gate_width)
    grad_q, grad_k, loss, target = call(
        last_kernel,
        (f32(heads, width, gate_width), f32(3, width, gate_width), f32(1, 1), f32(*target.shape)),
        [VMEM] * 4,
        "last",
        scratch=[pltpu.VMEM((1, 1), jnp.float32), pltpu.SemaphoreType.DMA((5,))],
        out_specs=(ANY,) * 4,
    )(mine.reshape(tiled), other.reshape(tiled), losses, target)
    return (target[None, None], grad_q, grad_k.reshape(3 * width, gate_width), loss.reshape(1))


def solution(mesh):
    placed = (P("seq", None), P("seq", "ctx", None, None), P("seq", "ctx", None), P(), P())
    return jax.shard_map(
        on_device,
        mesh=mesh,
        in_specs=placed,
        out_specs=(P("seq", "ctx", None, None, None), P(), P(), P("seq")),
        check_vma=False,
    )
```

```python
import functools
import math

import jax
import jax.numpy as jnp
from jax import lax
from jax.experimental import pallas as pl
from jax.experimental.pallas import tpu as pltpu
from jax.sharding import PartitionSpec as P

POOL = 64
LOW = -1e30
HIGHEST = lax.Precision.HIGHEST
VMEM = pl.BlockSpec(memory_space=pltpu.VMEM)
ANY = pl.BlockSpec(memory_space=pl.ANY)
PARAMS = pltpu.CompilerParams(vmem_limit_bytes=40 * 1024 * 1024)
SUB = 8
NT = (((1,), (1,)), ((), ()))
TN = (((0,), (0,)), ((), ()))
NN = (((1,), (0,)), ((), ()))


def dot(a, b, dims, precision=None):
    return lax.dot_general(a, b, dims, precision=precision, preferred_element_type=jnp.float32)


def split(x):
    high = x.astype(jnp.bfloat16)
    return high, (x - high.astype(jnp.float32)).astype(jnp.bfloat16)


def dot_split(a, b, dims):
    a_high, a_low = split(a)
    b_high, b_low = split(b)
    return dot(a_high, b_high, dims) + (dot(a_high, b_low, dims) + dot(a_low, b_high, dims))


def pick(values, index):
    lane = lax.broadcasted_iota(jnp.int32, (index.shape[0], values.shape[1]), 1)
    return jnp.sum(jnp.where(lane == index, values, 0.0), axis=1, keepdims=True)


def local_kernel(scale, near, q_ref, k_ref, wq_ref, order_ref, *refs):
    diag_ref, top_ref, tot_ref, pooled_ref, gate_q_ref, q2_ref, seen_ref, visible_ref = refs[-8:]
    heads, rows, width = q_ref.shape
    half = rows // 2
    blocks = rows // POOL
    per = half // POOL
    diag_ref[...] = jnp.full(diag_ref.shape, LOW, jnp.float32)
    key_row = lax.broadcasted_iota(jnp.int32, (half, half), 0)
    query_lane = lax.broadcasted_iota(jnp.int32, (half, half), 1)
    causal = key_row <= query_lane
    blank = jnp.zeros((SUB - blocks, width), jnp.float32)
    for h in range(heads):
        q = q_ref[h].astype(jnp.float32)
        pooled = jnp.sum(q.reshape(blocks, POOL, width), axis=1) * (1.0 / POOL)
        pooled = jnp.concatenate([pooled, blank], axis=0)
        pooled_ref[h * SUB : (h + 1) * SUB, :] = pooled
        gate_q_ref[h * SUB : (h + 1) * SUB, :] = dot(pooled, wq_ref[h], NN, HIGHEST)
        high, low = split(q * scale)
        q2_ref[h, :, 0:width] = high
        q2_ref[h, :, width:] = low
        for part in range(2):
            keys = k_ref[part * half : (part + 1) * half, :]
            s = dot(jnp.concatenate([keys, keys], axis=1), q2_ref[h, part * half : (part + 1) * half, :], NT)
            s = jnp.where(causal, s, LOW)
            block_top = jnp.max(s.reshape(per, POOL, half), axis=1)
            top = jnp.max(block_top, axis=0, keepdims=True)
            p = jnp.exp2(s - top)
            lanes = slice(h * rows + part * half, h * rows + (part + 1) * half)
            diag_ref[part * per : (part + 1) * per, lanes] = block_top
            top_ref[:, lanes] = top
            tot_ref[:, lanes] = jnp.sum(p.reshape(half // SUB, SUB, half), axis=0)
    place = lax.axis_index("ctx")
    along = lax.rem(place, near)
    base = place - along
    group = near * blocks
    order = order_ref[...].astype(jnp.float32)
    kb = lax.broadcasted_iota(jnp.int32, (2 * group, 1), 0)
    key_half = pick(order, kb // per)
    lane = lax.broadcasted_iota(jnp.int32, (2 * group, rows), 1)
    halves = [pick(order, jnp.full((1, 1), 2 * place + part, jnp.int32)) for part in range(2)]
    seen = jnp.where(key_half < jnp.where(lane < half, halves[0], halves[1]), 1.0, 0.0)
    shift = lax.rem(near - along, near) * blocks
    low, high = [pltpu.roll(seen[j * group : (j + 1) * group], shift, 0) for j in range(2)]
    seen_ref[0:group, :] = jnp.where(base == 0, low, high)
    seen_ref[group:, :] = jnp.where(base == 0, high, low)
    key_pos = key_half * per + (kb % per).astype(jnp.float32)
    diagonal = lax.broadcasted_iota(jnp.int32, (2 * group, 2 * group), 1) == kb
    key_pos = jnp.sum(jnp.where(diagonal, key_pos, 0.0), axis=0, keepdims=True)
    row = lax.broadcasted_iota(jnp.int32, (heads * SUB, 1), 0) % SUB
    query_pos = jnp.where(row < per, halves[0], halves[1]) * per + (row % per).astype(jnp.float32)
    visible_ref[...] = jnp.where((key_pos <= query_pos) & (row < blocks), 1.0, 0.0)


def pool_of(keys):
    x = keys.astype(jnp.float32).reshape(keys.shape[0] // POOL, POOL, keys.shape[1])
    return jnp.concatenate([jnp.max(x, axis=1), jnp.min(x, axis=1), jnp.sum(x, axis=1) * (1.0 / POOL)], axis=1)


def attend(q2_ref, seen_ref, chunks, top_in, tot_in, top_ref, tot_ref, map_ref, pool_ref):
    heads, rows, _ = q2_ref.shape
    blocks = rows // POOL
    tops = [top_in[:, h * rows : (h + 1) * rows] for h in range(heads)]
    tots = [tot_in[:, h * rows : (h + 1) * rows] for h in range(heads)]
    row = 0
    for first in range(0, len(chunks), 2):
        group = chunks[first : first + 2]
        keys = jnp.concatenate([read() for read, _ in group], axis=0)
        count = len(group) * blocks
        pool_ref[row : row + count, :] = pool_of(keys)
        seen = jnp.concatenate([seen_ref[at : at + blocks, :] for _, at in group], axis=0)
        seen_rows = jnp.broadcast_to(seen[:, None, :], (count, SUB, rows)) > 0.5
        seen = seen > 0.5
        keys = jnp.concatenate([keys, keys], axis=1)
        for h in range(heads):
            s = dot(keys, q2_ref[h], NT).reshape(count, POOL // SUB, SUB, rows)
            block_top = jnp.max(jnp.max(s, axis=1), axis=1)
            block_top = jnp.where(seen, block_top, LOW)
            map_ref[row : row + count, h * rows : (h + 1) * rows] = block_top
            top = jnp.maximum(tops[h], jnp.max(block_top, axis=0, keepdims=True))
            part = jnp.sum(jnp.exp2(s - top.reshape(1, 1, 1, rows)), axis=1)
            part = jnp.sum(jnp.where(seen_rows, part, 0.0), axis=0)
            tots[h] = tots[h] * jnp.exp2(tops[h] - top) + part
            tops[h] = top
        row += count
    for h in range(heads):
        top_ref[:, h * rows : (h + 1) * rows] = tops[h]
        tot_ref[:, h * rows : (h + 1) * rows] = tots[h]


def chunks_of(refs, layout, rows, group):
    chunks = []
    for ref, (other, offsets) in zip(refs, layout):
        for j, offset in enumerate(offsets):
            read = functools.partial(lambda r, j: r[j * rows : (j + 1) * rows, :], ref, j)
            chunks.append((read, other * group + offset * rows // POOL))
    return chunks


def attend_kernel(layout, *refs):
    q2_ref, seen_ref, top_in, tot_in = refs[:4]
    top_ref, tot_ref, map_ref, pool_ref = refs[-4:]
    chunks = chunks_of(refs[4:-4], layout, q2_ref.shape[1], seen_ref.shape[0] // 2)
    attend(q2_ref, seen_ref, chunks, top_in, tot_in, top_ref, tot_ref, map_ref, pool_ref)


def copy_kernel(in_ref, out_ref):
    out_ref[...] = in_ref[...]


def pair_kernel(own_ref, a_ref, b_ref, ahead_ref, behind_ref):
    rows = own_ref.shape[0]
    for out_ref, other_ref in ((ahead_ref, a_ref), (behind_ref, b_ref)):
        out_ref[0:rows, :] = own_ref[...]
        out_ref[rows:, :] = other_ref[...]


def gradient_half(low, pooled_ref, gate_q_grad_ref, pool_ref, gate_k_grad_ref, out_ref):
    heads = pooled_ref.shape[0] // SUB
    width = pooled_ref.shape[1]
    whole = (heads + pool_ref.shape[1] // width) // 2
    chosen = range(whole) if low else range(whole, heads)
    for j, h in enumerate(chosen):
        here = slice(h * SUB, (h + 1) * SUB)
        out_ref[j * width : (j + 1) * width, :] = dot_split(pooled_ref[here, :], gate_q_grad_ref[here, :], TN)
    if not low:
        out_ref[len(chosen) * width : whole * width, :] = dot_split(pool_ref[...], gate_k_grad_ref[...], TN)


def finish_kernel(layout, places, *refs):
    q2_ref, seen_ref, top_in, tot_in, diag_ref, pooled_ref, gate_q_ref, wk_ref, visible_ref = refs[:9]
    key_refs = refs[9 : 9 + len(layout)]
    earlier = refs[9 + len(layout) : -12]
    target_ref, give_ref, gate_q_grad_ref, gate_k_grad_ref, pool_ref = refs[-12:-7]
    top_ref, tot_ref, last_map, last_pool, map_ref, rel_pool, block_ref = refs[-7:]
    heads, rows, _ = q2_ref.shape
    half = rows // 2
    per = half // POOL
    blocks = rows // POOL
    total = map_ref.shape[0]
    near = total // 2
    width = pooled_ref.shape[1]
    devices = near // blocks
    place = lax.axis_index("ctx")
    along = lax.rem(place, devices)
    bases = (place - along, devices - (place - along))
    attend(
        q2_ref, seen_ref, chunks_of(key_refs, layout, rows, near), top_in, tot_in, top_ref, tot_ref, last_map, last_pool
    )
    maps = list(earlier[0::2]) + [last_map]
    pools = list(earlier[1::2]) + [last_pool]
    for map_in, pool_in, where in zip(maps, pools, places):
        for j, (other, offset) in enumerate(where):
            here = slice(other * near + offset * blocks, other * near + (offset + 1) * blocks)
            map_ref[here, :] = map_in[j * blocks : (j + 1) * blocks, :]
            rel_pool[here, :] = pool_in[j * blocks : (j + 1) * blocks, :]
    shift = along * blocks
    for other in range(2):
        at = pl.multiple_of(bases[other] * blocks, near)
        pool_ref[pl.ds(at, near), :] = pltpu.roll(rel_pool[other * near : (other + 1) * near, :], shift, 0)
    block_ref[...] = jnp.ones(block_ref.shape, jnp.float32)
    for h in range(heads):
        for part in range(2):
            lanes = slice(h * rows + part * half, h * rows + (part + 1) * half)
            own_rows = slice(part * per, (part + 1) * per)
            map_ref[own_rows, lanes] = diag_ref[own_rows, lanes]
            tot = jnp.sum(tot_ref[:, lanes], axis=0, keepdims=True)
            b = jnp.exp2(map_ref[:, lanes] - (top_ref[:, lanes] + jnp.log2(tot)))
            b = jnp.max(b.T.reshape(per, POOL, total), axis=1)
            block_ref[h * SUB + part * per : h * SUB + (part + 1) * per, :] = b
    block_map = block_ref[...]
    copies = 128 // near
    group = [
        pltpu.roll(jnp.concatenate([block_map[:, j * near : (j + 1) * near]] * copies, axis=1), shift, 1)[:, :total]
        for j in range(2)
    ]
    lane = lax.broadcasted_iota(jnp.int32, (heads * SUB, total), 1)
    in_near = (lane >= bases[0] * blocks) & (lane < (bases[0] + devices) * blocks)
    block_map = jnp.where(in_near, group[0], group[1])
    target = block_map / jnp.sum(block_map, axis=1, keepdims=True)
    for h in range(heads):
        target_ref[h] = target[h * SUB : h * SUB + blocks, :]
    gate_q = gate_q_ref[...]
    gate_k = dot(pool_ref[...], wk_ref[...], NN, HIGHEST)
    gate_width = gate_k.shape[1]
    row = lax.broadcasted_iota(jnp.int32, (heads * SUB, total), 0) % SUB
    visible = visible_ref[...] > 0.5
    logits = dot(gate_q, gate_k, NT, HIGHEST) * gate_width ** (-0.5)
    peak = jnp.max(jnp.where(visible, logits, LOW), axis=1, keepdims=True)
    weights = jnp.where(visible, jnp.exp(logits - peak), 0.0)
    norm_sum = jnp.where(row[:, :1] < blocks, jnp.sum(weights, axis=1, keepdims=True), 1.0)
    log_gate = logits - peak - jnp.log(norm_sum)
    count = heads * total
    loss = -jnp.sum(jnp.where(visible, target * log_gate, 0.0)) / count
    d_logits = jnp.where(visible, weights / norm_sum - target, 0.0) / count * gate_width ** (-0.5)
    gate_q_grad_ref[...] = dot_split(d_logits, gate_k, NN)
    gate_k_grad_ref[...] = dot_split(d_logits, gate_q, TN)
    own_seq = lax.axis_index("seq")
    terms = (pooled_ref, gate_q_grad_ref, pool_ref, gate_k_grad_ref)
    pl.when(lax.rem(own_seq, 2) == 0)(lambda: gradient_half(False, *terms, give_ref))
    pl.when(lax.rem(own_seq, 2) != 0)(lambda: gradient_half(True, *terms, give_ref))
    lane = lax.broadcasted_iota(jnp.int32, (SUB, gate_width), 1)
    give_ref[give_ref.shape[0] - SUB :, :] = jnp.where(lane == own_seq, loss, 0.0)


def keep_kernel(pooled_ref, gate_q_grad_ref, pool_ref, gate_k_grad_ref, keep_ref):
    terms = (pooled_ref, gate_q_grad_ref, pool_ref, gate_k_grad_ref)
    core = lax.rem(lax.axis_index("seq"), 2)
    pl.when(core == 0)(lambda: gradient_half(True, *terms, keep_ref))
    pl.when(core != 0)(lambda: gradient_half(False, *terms, keep_ref))


def fold_kernel(keep_ref, give_ref, got_ref, out_ref):
    tiles, tile_rows, width = out_ref.shape
    part = keep_ref.shape[0]
    rows = part // tiles
    out_ref[:, 0:rows, :] = (keep_ref[...] + got_ref[0:part, :]).reshape(tiles, rows, width)
    loss = give_ref[part:, :] + got_ref[part:, :]
    out_ref[:, rows:, :] = jnp.broadcast_to(loss[None], (tiles, tile_rows - rows, width))


def sum_kernel(parts_ref, out_ref):
    total = jnp.sum(parts_ref[...], axis=0)
    for j in range(out_ref.shape[0]):
        out_ref[j] = total


def join_kernel(parts_ref, out_ref, loss_ref):
    total = jnp.sum(parts_ref[...], axis=0)
    rows = out_ref.shape[1]
    for j in range(out_ref.shape[0]):
        out_ref[j] = total[:rows]
    loss_ref[...] = total[rows:]


def last_kernel(
    mine_ref, other_ref, losses_ref, target_in, grad_q_ref, grad_k_ref, loss_ref, target_ref, loss_row, sems
):
    tiles = mine_ref.shape[0]
    left = grad_q_ref.shape[0] - tiles
    own_seq = lax.axis_index("seq")
    core = lax.rem(own_seq, 2)

    def grads(low_ref, high_ref):
        pairs = (
            (low_ref, grad_q_ref.at[pl.ds(0, tiles)]),
            (high_ref.at[pl.ds(0, left)], grad_q_ref.at[pl.ds(tiles, left)]),
            (high_ref.at[pl.ds(left, tiles - left)], grad_k_ref),
        )
        return [pltpu.make_async_copy(source, target, sems.at[j]) for j, (source, target) in enumerate(pairs)]

    @pl.when(core == 0)
    def _():
        for copy in grads(mine_ref, other_ref):
            copy.start()

    @pl.when(core != 0)
    def _():
        for copy in grads(other_ref, mine_ref):
            copy.start()

    losses = losses_ref[0:1, :]
    lane = lax.broadcasted_iota(jnp.int32, losses.shape, 1)
    loss_row[...] = jnp.sum(jnp.where(lane == own_seq, losses, 0.0), axis=1, keepdims=True)
    rest = [
        pltpu.make_async_copy(loss_row, loss_ref, sems.at[3]),
        pltpu.make_async_copy(target_in, target_ref, sems.at[4]),
    ]
    for copy in rest:
        copy.start()
    for copy in grads(mine_ref, other_ref) + rest:
        copy.wait()


def f32(*shape):
    return jax.ShapeDtypeStruct(shape, jnp.float32)


def call(kernel, out_shape, specs, name, scratch=(), cost=None, out_specs=None):
    return pl.pallas_call(
        kernel,
        out_shape=out_shape,
        in_specs=specs,
        out_specs=out_specs or tuple(VMEM for _ in out_shape),
        scratch_shapes=scratch,
        compiler_params=PARAMS,
        cost_estimate=cost,
        name=name,
    )


def on_device(order, queries, keys, w_query_gate, w_key_gate):
    tok_rows = queries.shape[1]
    heads = queries.shape[2]
    width = queries.shape[3]
    gate_width = w_key_gate.shape[1]
    blocks = tok_rows // POOL
    ctx_count = lax.axis_size("ctx")
    seq_count = lax.axis_size("seq")
    near = ctx_count // 2
    total = ctx_count * blocks
    scale = width ** (-0.5) * math.log2(math.e)
    columns = heads * tok_rows

    def get(x, offset):
        return lax.ppermute(x, "ctx", [(j, j // near * near + (j - offset) % near) for j in range(ctx_count)])

    def across(x):
        return lax.ppermute(x, "ctx", [(j, (j + near) % ctx_count) for j in range(ctx_count)])

    own_keys = keys[0]
    step = {offset: get(own_keys, offset % near) for offset in (1, -1, near // 2)}
    (own_copy,) = call(
        copy_kernel,
        (jax.ShapeDtypeStruct(own_keys.shape, keys.dtype),),
        [VMEM],
        "copy",
        cost=pl.CostEstimate(flops=10**9, bytes_accessed=10**6, transcendentals=10**6),
    )(own_keys)
    two_parts = jax.ShapeDtypeStruct((2 * tok_rows, width), keys.dtype)
    ahead, behind = call(pair_kernel, (two_parts, two_parts), [VMEM] * 3, "pair")(own_copy, step[1], step[-1])
    ahead = get(ahead, 2)
    behind = get(behind, near - 2)
    mid = jnp.concatenate([own_copy, step[1], step[-1]], axis=0)
    mid_far = across(mid)
    mid_from = (0, 1, near - 1)
    quad_from = (near // 2,)
    ahead_from = (2, 3)
    behind_from = (near - 2, near - 3)

    q = jnp.transpose(queries[0], (1, 0, 2))
    state = (f32(1, columns), f32(SUB, columns))
    diag, top, tot, pooled, gate_q, q2, seen, visible = call(
        functools.partial(local_kernel, scale, near),
        (f32(SUB, columns),)
        + state
        + (
            f32(heads * SUB, width),
            f32(heads * SUB, gate_width),
            jax.ShapeDtypeStruct((heads, tok_rows, 2 * width), jnp.bfloat16),
            f32(total, tok_rows),
            f32(heads * SUB, total),
        ),
        [VMEM] * 4 + [ANY] * 2,
        "local",
        cost=pl.CostEstimate(flops=4 * 10**8, bytes_accessed=10**6, transcendentals=10**5),
    )(q, own_copy, w_query_gate, order, step[1], step[-1])

    def attend_to(layout, top, tot, *keys):
        count = sum(len(offsets) for _, offsets in layout)
        return call(
            functools.partial(attend_kernel, layout),
            state + (f32(count * blocks, columns), f32(count * blocks, 3 * width)),
            [VMEM] * (4 + len(keys)),
            "attend",
            cost=pl.CostEstimate(flops=1200000000, bytes_accessed=10**6, transcendentals=1300000),
        )(q2, seen, top, tot, *keys)

    layouts = (
        ((0, mid_from),),
        ((0, ahead_from), (0, behind_from), (0, quad_from)),
        ((1, mid_from), (1, quad_from)),
        ((1, ahead_from),),
        ((1, behind_from),),
    )
    places = [[(other, offset) for other, offsets in layout for offset in offsets] for layout in layouts]
    quad = step[near // 2]
    quad_far = across(quad)
    ahead_far = across(ahead)
    behind_far = across(behind)
    earlier = []
    for layout, key_parts in zip(layouts[:-1], ((mid,), (ahead, behind, quad), (mid_far, quad_far), (ahead_far,))):
        top, tot, *found = attend_to(layout, top, tot, *key_parts)
        earlier += found

    grad_rows = heads * width + 3 * width
    part = grad_rows // 2
    last_blocks = len(places[-1]) * blocks
    target, give, *terms = call(
        functools.partial(finish_kernel, layouts[-1], places),
        (
            f32(heads, blocks, total),
            f32(part + SUB, gate_width),
            f32(heads * SUB, gate_width),
            f32(total, gate_width),
            f32(total, 3 * width),
        ),
        [VMEM] * (10 + len(earlier)),
        "finish",
        scratch=[
            pltpu.VMEM(shape, jnp.float32)
            for shape in (
                (1, columns),
                (SUB, columns),
                (last_blocks, columns),
                (last_blocks, 3 * width),
                (total, columns),
                (total, 3 * width),
                (heads * SUB, total),
            )
        ],
    )(q2, seen, top, tot, diag, pooled, gate_q, w_key_gate, visible, behind_far, *earlier)

    every = ("seq", "ctx")
    half_seq = seq_count // 2

    def flat(x_lo, y, core, x_hi, z):
        return (x_lo * half_seq + y * 2 + core) * ctx_count + x_hi * near + z

    ys = range(half_seq // 2)
    zs = range(near)
    pair = (0, 1)
    cores = [
        (flat(a, y, b, c, z), flat(a, y, 1 - b, c, z)) for a in pair for y in ys for b in pair for c in pair for z in zs
    ]
    planes = [[flat(a, y, b, c, z) for a in pair for c in pair for y in ys] for b in pair for z in zs]
    tiles = len(planes[0])
    got = lax.ppermute(give, every, cores)
    (keep,) = call(keep_kernel, (f32(part, gate_width),), [VMEM] * 4, "keep")(
        pooled, terms[0], terms[2], terms[1]
    )
    (parts,) = call(
        fold_kernel, (f32(tiles, part // tiles + SUB, gate_width),), [VMEM] * 3, "fold"
    )(keep, give, got)
    parts = lax.all_to_all(parts, every, 0, 0, axis_index_groups=planes, tiled=True)
    (spread,) = call(sum_kernel, (f32(near, part // tiles + SUB, gate_width),), [VMEM], "sum")(parts)
    parts = lax.all_to_all(
        spread,
        "ctx",
        0,
        0,
        axis_index_groups=[list(range(near)), list(range(near, ctx_count))],
        tiled=True,
    )
    spread, losses = call(
        join_kernel, (f32(tiles, part // tiles, gate_width), f32(SUB, gate_width)), [VMEM], "join"
    )(parts)
    mine = lax.all_to_all(spread, every, 0, 0, axis_index_groups=planes, tiled=True).reshape(part, gate_width)
    other = lax.ppermute(mine, every, cores)
    tiled = (part // width, width, gate_width)
    grad_q, grad_k, loss, target = call(
        last_kernel,
        (f32(heads, width, gate_width), f32(3, width, gate_width), f32(1, 1), f32(*target.shape)),
        [VMEM] * 4,
        "last",
        scratch=[pltpu.VMEM((1, 1), jnp.float32), pltpu.SemaphoreType.DMA((5,))],
        out_specs=(ANY,) * 4,
    )(mine.reshape(tiled), other.reshape(tiled), losses, target)
    return (target[None, None], grad_q, grad_k.reshape(3 * width, gate_width), loss.reshape(1))


def solution(mesh):
    placed = (P("seq", None), P("seq", "ctx", None, None), P("seq", "ctx", None), P(), P())
    return jax.shard_map(
        on_device,
        mesh=mesh,
        in_specs=placed,
        out_specs=(P("seq", "ctx", None, None, None), P(), P(), P("seq")),
        check_vma=False,
    )
```

```python
import functools
import math

import jax
import jax.numpy as jnp
from jax import lax
from jax.experimental import pallas as pl
from jax.experimental.pallas import tpu as pltpu
from jax.sharding import PartitionSpec as P

POOL = 64
LOW = -1e30
HIGHEST = lax.Precision.HIGHEST
VMEM = pl.BlockSpec(memory_space=pltpu.VMEM)
ANY = pl.BlockSpec(memory_space=pl.ANY)
PARAMS = pltpu.CompilerParams(vmem_limit_bytes=40 * 1024 * 1024)
SUB = 8
NT = (((1,), (1,)), ((), ()))
TN = (((0,), (0,)), ((), ()))
NN = (((1,), (0,)), ((), ()))


def dot(a, b, dims, precision=None):
    return lax.dot_general(a, b, dims, precision=precision, preferred_element_type=jnp.float32)


def split(x):
    high = x.astype(jnp.bfloat16)
    return high, (x - high.astype(jnp.float32)).astype(jnp.bfloat16)


def dot_split(a, b, dims):
    a_high, a_low = split(a)
    b_high, b_low = split(b)
    return dot(a_high, b_high, dims) + (dot(a_high, b_low, dims) + dot(a_low, b_high, dims))


def pick(values, index):
    lane = lax.broadcasted_iota(jnp.int32, (index.shape[0], values.shape[1]), 1)
    return jnp.sum(jnp.where(lane == index, values, 0.0), axis=1, keepdims=True)


def local_kernel(scale, near, q_ref, k_ref, wq_ref, order_ref, *refs):
    diag_ref, top_ref, tot_ref, pooled_ref, gate_q_ref, q2_ref, seen_ref, visible_ref = refs[-8:]
    heads, rows, width = q_ref.shape
    half = rows // 2
    blocks = rows // POOL
    per = half // POOL
    diag_ref[...] = jnp.full(diag_ref.shape, LOW, jnp.float32)
    key_row = lax.broadcasted_iota(jnp.int32, (half, half), 0)
    query_lane = lax.broadcasted_iota(jnp.int32, (half, half), 1)
    causal = key_row <= query_lane
    blank = jnp.zeros((SUB - blocks, width), jnp.float32)
    for h in range(heads):
        q = q_ref[h].astype(jnp.float32)
        pooled = jnp.sum(q.reshape(blocks, POOL, width), axis=1) * (1.0 / POOL)
        pooled = jnp.concatenate([pooled, blank], axis=0)
        pooled_ref[h * SUB : (h + 1) * SUB, :] = pooled
        gate_q_ref[h * SUB : (h + 1) * SUB, :] = dot(pooled, wq_ref[h], NN, HIGHEST)
        high, low = split(q * scale)
        q2_ref[h, :, 0:width] = high
        q2_ref[h, :, width:] = low
        for part in range(2):
            keys = k_ref[part * half : (part + 1) * half, :]
            s = dot(jnp.concatenate([keys, keys], axis=1), q2_ref[h, part * half : (part + 1) * half, :], NT)
            s = jnp.where(causal, s, LOW)
            block_top = jnp.max(s.reshape(per, POOL, half), axis=1)
            top = jnp.max(block_top, axis=0, keepdims=True)
            p = jnp.exp2(s - top)
            lanes = slice(h * rows + part * half, h * rows + (part + 1) * half)
            diag_ref[part * per : (part + 1) * per, lanes] = block_top
            top_ref[:, lanes] = top
            tot_ref[:, lanes] = jnp.sum(p.reshape(half // SUB, SUB, half), axis=0)
    place = lax.axis_index("ctx")
    along = lax.rem(place, near)
    base = place - along
    group = near * blocks
    order = order_ref[...].astype(jnp.float32)
    kb = lax.broadcasted_iota(jnp.int32, (2 * group, 1), 0)
    key_half = pick(order, kb // per)
    lane = lax.broadcasted_iota(jnp.int32, (2 * group, rows), 1)
    halves = [pick(order, jnp.full((1, 1), 2 * place + part, jnp.int32)) for part in range(2)]
    seen = jnp.where(key_half < jnp.where(lane < half, halves[0], halves[1]), 1.0, 0.0)
    shift = lax.rem(near - along, near) * blocks
    low, high = [pltpu.roll(seen[j * group : (j + 1) * group], shift, 0) for j in range(2)]
    seen_ref[0:group, :] = jnp.where(base == 0, low, high)
    seen_ref[group:, :] = jnp.where(base == 0, high, low)
    key_pos = key_half * per + (kb % per).astype(jnp.float32)
    diagonal = lax.broadcasted_iota(jnp.int32, (2 * group, 2 * group), 1) == kb
    key_pos = jnp.sum(jnp.where(diagonal, key_pos, 0.0), axis=0, keepdims=True)
    row = lax.broadcasted_iota(jnp.int32, (heads * SUB, 1), 0) % SUB
    query_pos = jnp.where(row < per, halves[0], halves[1]) * per + (row % per).astype(jnp.float32)
    visible_ref[...] = jnp.where((key_pos <= query_pos) & (row < blocks), 1.0, 0.0)


def pool_of(keys):
    x = keys.astype(jnp.float32).reshape(keys.shape[0] // POOL, POOL, keys.shape[1])
    return jnp.concatenate([jnp.max(x, axis=1), jnp.min(x, axis=1), jnp.sum(x, axis=1) * (1.0 / POOL)], axis=1)


def attend(q2_ref, seen_ref, chunks, top_in, tot_in, top_ref, tot_ref, map_ref, pool_ref):
    heads, rows, _ = q2_ref.shape
    blocks = rows // POOL
    tops = [top_in[:, h * rows : (h + 1) * rows] for h in range(heads)]
    tots = [tot_in[:, h * rows : (h + 1) * rows] for h in range(heads)]
    row = 0
    for first in range(0, len(chunks), 2):
        group = chunks[first : first + 2]
        keys = jnp.concatenate([read() for read, _ in group], axis=0)
        count = len(group) * blocks
        pool_ref[row : row + count, :] = pool_of(keys)
        seen = jnp.concatenate([seen_ref[at : at + blocks, :] for _, at in group], axis=0)
        seen_rows = jnp.broadcast_to(seen[:, None, :], (count, SUB, rows)) > 0.5
        seen = seen > 0.5
        keys = jnp.concatenate([keys, keys], axis=1)
        for h in range(heads):
            s = dot(keys, q2_ref[h], NT).reshape(count, POOL // SUB, SUB, rows)
            block_top = jnp.max(jnp.max(s, axis=1), axis=1)
            block_top = jnp.where(seen, block_top, LOW)
            map_ref[row : row + count, h * rows : (h + 1) * rows] = block_top
            top = jnp.maximum(tops[h], jnp.max(block_top, axis=0, keepdims=True))
            part = jnp.sum(jnp.exp2(s - top.reshape(1, 1, 1, rows)), axis=1)
            part = jnp.sum(jnp.where(seen_rows, part, 0.0), axis=0)
            tots[h] = tots[h] * jnp.exp2(tops[h] - top) + part
            tops[h] = top
        row += count
    for h in range(heads):
        top_ref[:, h * rows : (h + 1) * rows] = tops[h]
        tot_ref[:, h * rows : (h + 1) * rows] = tots[h]


def chunks_of(refs, layout, rows, group):
    chunks = []
    for ref, (other, offsets) in zip(refs, layout):
        for j, offset in enumerate(offsets):
            read = functools.partial(lambda r, j: r[j * rows : (j + 1) * rows, :], ref, j)
            chunks.append((read, other * group + offset * rows // POOL))
    return chunks


def attend_kernel(layout, *refs):
    q2_ref, seen_ref, top_in, tot_in = refs[:4]
    top_ref, tot_ref, map_ref, pool_ref = refs[-4:]
    chunks = chunks_of(refs[4:-4], layout, q2_ref.shape[1], seen_ref.shape[0] // 2)
    attend(q2_ref, seen_ref, chunks, top_in, tot_in, top_ref, tot_ref, map_ref, pool_ref)


def copy_kernel(in_ref, out_ref):
    out_ref[...] = in_ref[...]


def pair_kernel(own_ref, a_ref, b_ref, ahead_ref, behind_ref):
    rows = own_ref.shape[0]
    for out_ref, other_ref in ((ahead_ref, a_ref), (behind_ref, b_ref)):
        out_ref[0:rows, :] = own_ref[...]
        out_ref[rows:, :] = other_ref[...]


def gradient_half(low, pooled_ref, gate_q_grad_ref, pool_ref, gate_k_grad_ref, out_ref):
    heads = pooled_ref.shape[0] // SUB
    width = pooled_ref.shape[1]
    whole = (heads + pool_ref.shape[1] // width) // 2
    chosen = range(whole) if low else range(whole, heads)
    for j, h in enumerate(chosen):
        here = slice(h * SUB, (h + 1) * SUB)
        out_ref[j * width : (j + 1) * width, :] = dot_split(pooled_ref[here, :], gate_q_grad_ref[here, :], TN)
    if not low:
        out_ref[len(chosen) * width : whole * width, :] = dot_split(pool_ref[...], gate_k_grad_ref[...], TN)


def finish_kernel(layout, places, *refs):
    q2_ref, seen_ref, top_in, tot_in, diag_ref, pooled_ref, gate_q_ref, wk_ref, visible_ref = refs[:9]
    key_refs = refs[9 : 9 + len(layout)]
    earlier = refs[9 + len(layout) : -12]
    target_ref, give_ref, gate_q_grad_ref, gate_k_grad_ref, pool_ref = refs[-12:-7]
    top_ref, tot_ref, last_map, last_pool, map_ref, rel_pool, block_ref = refs[-7:]
    heads, rows, _ = q2_ref.shape
    half = rows // 2
    per = half // POOL
    blocks = rows // POOL
    total = map_ref.shape[0]
    near = total // 2
    width = pooled_ref.shape[1]
    devices = near // blocks
    place = lax.axis_index("ctx")
    along = lax.rem(place, devices)
    bases = (place - along, devices - (place - along))
    attend(
        q2_ref, seen_ref, chunks_of(key_refs, layout, rows, near), top_in, tot_in, top_ref, tot_ref, last_map, last_pool
    )
    maps = list(earlier[0::2]) + [last_map]
    pools = list(earlier[1::2]) + [last_pool]
    for map_in, pool_in, where in zip(maps, pools, places):
        for j, (other, offset) in enumerate(where):
            here = slice(other * near + offset * blocks, other * near + (offset + 1) * blocks)
            map_ref[here, :] = map_in[j * blocks : (j + 1) * blocks, :]
            rel_pool[here, :] = pool_in[j * blocks : (j + 1) * blocks, :]
    shift = along * blocks
    for other in range(2):
        at = pl.multiple_of(bases[other] * blocks, near)
        pool_ref[pl.ds(at, near), :] = pltpu.roll(rel_pool[other * near : (other + 1) * near, :], shift, 0)
    block_ref[...] = jnp.ones(block_ref.shape, jnp.float32)
    for h in range(heads):
        for part in range(2):
            lanes = slice(h * rows + part * half, h * rows + (part + 1) * half)
            own_rows = slice(part * per, (part + 1) * per)
            map_ref[own_rows, lanes] = diag_ref[own_rows, lanes]
            tot = jnp.sum(tot_ref[:, lanes], axis=0, keepdims=True)
            b = jnp.exp2(map_ref[:, lanes] - (top_ref[:, lanes] + jnp.log2(tot)))
            b = jnp.max(b.T.reshape(per, POOL, total), axis=1)
            block_ref[h * SUB + part * per : h * SUB + (part + 1) * per, :] = b
    block_map = block_ref[...]
    copies = 128 // near
    group = [
        pltpu.roll(jnp.concatenate([block_map[:, j * near : (j + 1) * near]] * copies, axis=1), shift, 1)[:, :total]
        for j in range(2)
    ]
    lane = lax.broadcasted_iota(jnp.int32, (heads * SUB, total), 1)
    in_near = (lane >= bases[0] * blocks) & (lane < (bases[0] + devices) * blocks)
    block_map = jnp.where(in_near, group[0], group[1])
    target = block_map / jnp.sum(block_map, axis=1, keepdims=True)
    for h in range(heads):
        target_ref[h] = target[h * SUB : h * SUB + blocks, :]
    gate_q = gate_q_ref[...]
    gate_k = dot(pool_ref[...], wk_ref[...], NN, HIGHEST)
    gate_width = gate_k.shape[1]
    row = lax.broadcasted_iota(jnp.int32, (heads * SUB, total), 0) % SUB
    visible = visible_ref[...] > 0.5
    logits = dot(gate_q, gate_k, NT, HIGHEST) * gate_width ** (-0.5)
    peak = jnp.max(jnp.where(visible, logits, LOW), axis=1, keepdims=True)
    weights = jnp.where(visible, jnp.exp(logits - peak), 0.0)
    norm_sum = jnp.where(row[:, :1] < blocks, jnp.sum(weights, axis=1, keepdims=True), 1.0)
    log_gate = logits - peak - jnp.log(norm_sum)
    count = heads * total
    loss = -jnp.sum(jnp.where(visible, target * log_gate, 0.0)) / count
    d_logits = jnp.where(visible, weights / norm_sum - target, 0.0) / count * gate_width ** (-0.5)
    gate_q_grad_ref[...] = dot_split(d_logits, gate_k, NN)
    gate_k_grad_ref[...] = dot_split(d_logits, gate_q, TN)
    own_seq = lax.axis_index("seq")
    terms = (pooled_ref, gate_q_grad_ref, pool_ref, gate_k_grad_ref)
    pl.when(lax.rem(own_seq, 2) == 0)(lambda: gradient_half(False, *terms, give_ref))
    pl.when(lax.rem(own_seq, 2) != 0)(lambda: gradient_half(True, *terms, give_ref))
    lane = lax.broadcasted_iota(jnp.int32, (SUB, gate_width), 1)
    give_ref[give_ref.shape[0] - SUB :, :] = jnp.where(lane == own_seq, loss, 0.0)


def keep_kernel(pooled_ref, gate_q_grad_ref, pool_ref, gate_k_grad_ref, keep_ref):
    terms = (pooled_ref, gate_q_grad_ref, pool_ref, gate_k_grad_ref)
    core = lax.rem(lax.axis_index("seq"), 2)
    pl.when(core == 0)(lambda: gradient_half(True, *terms, keep_ref))
    pl.when(core != 0)(lambda: gradient_half(False, *terms, keep_ref))


def fold_kernel(keep_ref, give_ref, got_ref, out_ref):
    tiles, tile_rows, width = out_ref.shape
    part = keep_ref.shape[0]
    rows = part // tiles
    out_ref[:, 0:rows, :] = (keep_ref[...] + got_ref[0:part, :]).reshape(tiles, rows, width)
    loss = give_ref[part:, :] + got_ref[part:, :]
    out_ref[:, rows:, :] = jnp.broadcast_to(loss[None], (tiles, tile_rows - rows, width))


def sum_kernel(parts_ref, out_ref):
    total = jnp.sum(parts_ref[...], axis=0)
    for j in range(out_ref.shape[0]):
        out_ref[j] = total


def join_kernel(parts_ref, out_ref, loss_ref):
    total = jnp.sum(parts_ref[...], axis=0)
    rows = out_ref.shape[1]
    for j in range(out_ref.shape[0]):
        out_ref[j] = total[:rows]
    loss_ref[...] = total[rows:]


def write_half(low, source_ref, grad_q_ref, grad_k_ref, sems, others=()):
    tiles = source_ref.shape[0]
    left = grad_q_ref.shape[0] - tiles
    if low:
        pairs = [(source_ref, grad_q_ref.at[pl.ds(0, tiles)])]
    else:
        pairs = [
            (source_ref.at[pl.ds(0, left)], grad_q_ref.at[pl.ds(tiles, left)]),
            (source_ref.at[pl.ds(left, tiles - left)], grad_k_ref),
        ]
    pairs += others
    copies = [pltpu.make_async_copy(source, target, sems.at[j]) for j, (source, target) in enumerate(pairs)]
    for copy in copies:
        copy.start()
    for copy in copies:
        copy.wait()


def mine_kernel(
    mine_ref, losses_ref, target_in, grad_q_ref, grad_k_ref, loss_ref, target_ref, loss_row, sems
):
    own_seq = lax.axis_index("seq")
    core = lax.rem(own_seq, 2)
    losses = losses_ref[0:1, :]
    lane = lax.broadcasted_iota(jnp.int32, losses.shape, 1)
    loss_row[...] = jnp.sum(jnp.where(lane == own_seq, losses, 0.0), axis=1, keepdims=True)
    others = [(loss_row, loss_ref), (target_in, target_ref)]
    pl.when(core == 0)(lambda: write_half(True, mine_ref, grad_q_ref, grad_k_ref, sems, others))
    pl.when(core != 0)(lambda: write_half(False, mine_ref, grad_q_ref, grad_k_ref, sems, others))


def other_kernel(other_ref, grad_q_in, grad_k_in, grad_q_ref, grad_k_ref, sems):
    core = lax.rem(lax.axis_index("seq"), 2)
    pl.when(core == 0)(lambda: write_half(False, other_ref, grad_q_ref, grad_k_ref, sems))
    pl.when(core != 0)(lambda: write_half(True, other_ref, grad_q_ref, grad_k_ref, sems))


def f32(*shape):
    return jax.ShapeDtypeStruct(shape, jnp.float32)


def call(kernel, out_shape, specs, name, scratch=(), cost=None, out_specs=None, aliases={}):
    return pl.pallas_call(
        kernel,
        out_shape=out_shape,
        in_specs=specs,
        out_specs=out_specs or tuple(VMEM for _ in out_shape),
        scratch_shapes=scratch,
        compiler_params=PARAMS,
        cost_estimate=cost,
        input_output_aliases=aliases,
        name=name,
    )


def on_device(order, queries, keys, w_query_gate, w_key_gate):
    tok_rows = queries.shape[1]
    heads = queries.shape[2]
    width = queries.shape[3]
    gate_width = w_key_gate.shape[1]
    blocks = tok_rows // POOL
    ctx_count = lax.axis_size("ctx")
    seq_count = lax.axis_size("seq")
    near = ctx_count // 2
    total = ctx_count * blocks
    scale = width ** (-0.5) * math.log2(math.e)
    columns = heads * tok_rows

    def get(x, offset):
        return lax.ppermute(x, "ctx", [(j, j // near * near + (j - offset) % near) for j in range(ctx_count)])

    def across(x):
        return lax.ppermute(x, "ctx", [(j, (j + near) % ctx_count) for j in range(ctx_count)])

    own_keys = keys[0]
    step = {offset: get(own_keys, offset % near) for offset in (1, -1, near // 2)}
    (own_copy,) = call(
        copy_kernel,
        (jax.ShapeDtypeStruct(own_keys.shape, keys.dtype),),
        [VMEM],
        "copy",
        cost=pl.CostEstimate(flops=10**9, bytes_accessed=10**6, transcendentals=10**6),
    )(own_keys)
    two_parts = jax.ShapeDtypeStruct((2 * tok_rows, width), keys.dtype)
    ahead, behind = call(pair_kernel, (two_parts, two_parts), [VMEM] * 3, "pair")(own_copy, step[1], step[-1])
    ahead = get(ahead, 2)
    behind = get(behind, near - 2)
    mid = jnp.concatenate([own_copy, step[1], step[-1]], axis=0)
    mid_far = across(mid)
    mid_from = (0, 1, near - 1)
    quad_from = (near // 2,)
    ahead_from = (2, 3)
    behind_from = (near - 2, near - 3)

    q = jnp.transpose(queries[0], (1, 0, 2))
    state = (f32(1, columns), f32(SUB, columns))
    diag, top, tot, pooled, gate_q, q2, seen, visible = call(
        functools.partial(local_kernel, scale, near),
        (f32(SUB, columns),)
        + state
        + (
            f32(heads * SUB, width),
            f32(heads * SUB, gate_width),
            jax.ShapeDtypeStruct((heads, tok_rows, 2 * width), jnp.bfloat16),
            f32(total, tok_rows),
            f32(heads * SUB, total),
        ),
        [VMEM] * 4 + [ANY] * 2,
        "local",
        cost=pl.CostEstimate(flops=4 * 10**8, bytes_accessed=10**6, transcendentals=10**5),
    )(q, own_copy, w_query_gate, order, step[1], step[-1])

    def attend_to(layout, top, tot, *keys):
        count = sum(len(offsets) for _, offsets in layout)
        return call(
            functools.partial(attend_kernel, layout),
            state + (f32(count * blocks, columns), f32(count * blocks, 3 * width)),
            [VMEM] * (4 + len(keys)),
            "attend",
            cost=pl.CostEstimate(flops=1200000000, bytes_accessed=10**6, transcendentals=1300000),
        )(q2, seen, top, tot, *keys)

    layouts = (
        ((0, mid_from),),
        ((0, ahead_from), (0, behind_from), (0, quad_from)),
        ((1, mid_from), (1, quad_from)),
        ((1, ahead_from),),
        ((1, behind_from),),
    )
    places = [[(other, offset) for other, offsets in layout for offset in offsets] for layout in layouts]
    quad = step[near // 2]
    quad_far = across(quad)
    ahead_far = across(ahead)
    behind_far = across(behind)
    earlier = []
    for layout, key_parts in zip(layouts[:-1], ((mid,), (ahead, behind, quad), (mid_far, quad_far), (ahead_far,))):
        top, tot, *found = attend_to(layout, top, tot, *key_parts)
        earlier += found

    grad_rows = heads * width + 3 * width
    part = grad_rows // 2
    last_blocks = len(places[-1]) * blocks
    target, give, *terms = call(
        functools.partial(finish_kernel, layouts[-1], places),
        (
            f32(heads, blocks, total),
            f32(part + SUB, gate_width),
            f32(heads * SUB, gate_width),
            f32(total, gate_width),
            f32(total, 3 * width),
        ),
        [VMEM] * (10 + len(earlier)),
        "finish",
        scratch=[
            pltpu.VMEM(shape, jnp.float32)
            for shape in (
                (1, columns),
                (SUB, columns),
                (last_blocks, columns),
                (last_blocks, 3 * width),
                (total, columns),
                (total, 3 * width),
                (heads * SUB, total),
            )
        ],
    )(q2, seen, top, tot, diag, pooled, gate_q, w_key_gate, visible, behind_far, *earlier)

    every = ("seq", "ctx")
    half_seq = seq_count // 2

    def flat(x_lo, y, core, x_hi, z):
        return (x_lo * half_seq + y * 2 + core) * ctx_count + x_hi * near + z

    ys = range(half_seq // 2)
    zs = range(near)
    pair = (0, 1)
    cores = [
        (flat(a, y, b, c, z), flat(a, y, 1 - b, c, z)) for a in pair for y in ys for b in pair for c in pair for z in zs
    ]
    planes = [[flat(a, y, b, c, z) for a in pair for c in pair for y in ys] for b in pair for z in zs]
    tiles = len(planes[0])
    got = lax.ppermute(give, every, cores)
    (keep,) = call(keep_kernel, (f32(part, gate_width),), [VMEM] * 4, "keep")(
        pooled, terms[0], terms[2], terms[1]
    )
    (parts,) = call(
        fold_kernel, (f32(tiles, part // tiles + SUB, gate_width),), [VMEM] * 3, "fold"
    )(keep, give, got)
    parts = lax.all_to_all(parts, every, 0, 0, axis_index_groups=planes, tiled=True)
    (spread,) = call(sum_kernel, (f32(near, part // tiles + SUB, gate_width),), [VMEM], "sum")(parts)
    parts = lax.all_to_all(
        spread,
        "ctx",
        0,
        0,
        axis_index_groups=[list(range(near)), list(range(near, ctx_count))],
        tiled=True,
    )
    spread, losses = call(
        join_kernel, (f32(tiles, part // tiles, gate_width), f32(SUB, gate_width)), [VMEM], "join"
    )(parts)
    mine = lax.all_to_all(spread, every, 0, 0, axis_index_groups=planes, tiled=True).reshape(part, gate_width)
    other = lax.ppermute(mine, every, cores)
    tiled = (part // width, width, gate_width)
    grads = (f32(heads, width, gate_width), f32(3, width, gate_width))
    grad_q, grad_k, loss, target = call(
        mine_kernel,
        grads + (f32(1, 1), f32(*target.shape)),
        [VMEM] * 3,
        "mine",
        scratch=[pltpu.VMEM((1, 1), jnp.float32), pltpu.SemaphoreType.DMA((4,))],
        out_specs=(ANY,) * 4,
    )(mine.reshape(tiled), losses, target)
    grad_q, grad_k = call(
        other_kernel,
        grads,
        [VMEM, ANY, ANY],
        "other",
        scratch=[pltpu.SemaphoreType.DMA((2,))],
        out_specs=(ANY,) * 2,
        aliases={1: 0, 2: 1},
    )(other.reshape(tiled), grad_q, grad_k)
    return (target[None, None], grad_q, grad_k.reshape(3 * width, gate_width), loss.reshape(1))


def solution(mesh):
    placed = (P("seq", None), P("seq", "ctx", None, None), P("seq", "ctx", None), P(), P())
    return jax.shard_map(
        on_device,
        mesh=mesh,
        in_specs=placed,
        out_specs=(P("seq", "ctx", None, None, None), P(), P(), P("seq")),
        check_vma=False,
    )
```

```python
import functools
import math

import jax
import jax.numpy as jnp
from jax import lax
from jax.experimental import pallas as pl
from jax.experimental.pallas import tpu as pltpu
from jax.sharding import PartitionSpec as P

POOL = 64
LOW = -1e30
HIGHEST = lax.Precision.HIGHEST
VMEM = pl.BlockSpec(memory_space=pltpu.VMEM)
ANY = pl.BlockSpec(memory_space=pl.ANY)
PARAMS = pltpu.CompilerParams(vmem_limit_bytes=40 * 1024 * 1024)
SUB = 8
NT = (((1,), (1,)), ((), ()))
TN = (((0,), (0,)), ((), ()))
NN = (((1,), (0,)), ((), ()))


def dot(a, b, dims, precision=None):
    return lax.dot_general(a, b, dims, precision=precision, preferred_element_type=jnp.float32)


def split(x):
    high = x.astype(jnp.bfloat16)
    return high, (x - high.astype(jnp.float32)).astype(jnp.bfloat16)


def dot_split(a, b, dims):
    a_high, a_low = split(a)
    b_high, b_low = split(b)
    return dot(a_high, b_high, dims) + (dot(a_high, b_low, dims) + dot(a_low, b_high, dims))


def pick(values, index):
    lane = lax.broadcasted_iota(jnp.int32, (index.shape[0], values.shape[1]), 1)
    return jnp.sum(jnp.where(lane == index, values, 0.0), axis=1, keepdims=True)


def local_kernel(scale, near, q_ref, k_ref, wq_ref, order_ref, *refs):
    diag_ref, top_ref, tot_ref, pooled_ref, gate_q_ref, q2_ref, seen_ref, visible_ref = refs[-8:]
    heads, rows, width = q_ref.shape
    half = rows // 2
    blocks = rows // POOL
    per = half // POOL
    diag_ref[...] = jnp.full(diag_ref.shape, LOW, jnp.float32)
    key_row = lax.broadcasted_iota(jnp.int32, (half, half), 0)
    query_lane = lax.broadcasted_iota(jnp.int32, (half, half), 1)
    causal = key_row <= query_lane
    blank = jnp.zeros((SUB - blocks, width), jnp.float32)
    for h in range(heads):
        q = q_ref[h].astype(jnp.float32)
        pooled = jnp.sum(q.reshape(blocks, POOL, width), axis=1) * (1.0 / POOL)
        pooled = jnp.concatenate([pooled, blank], axis=0)
        pooled_ref[h * SUB : (h + 1) * SUB, :] = pooled
        gate_q_ref[h * SUB : (h + 1) * SUB, :] = dot(pooled, wq_ref[h], NN, HIGHEST)
        high, low = split(q * scale)
        q2_ref[h, :, 0:width] = high
        q2_ref[h, :, width:] = low
        for part in range(2):
            keys = k_ref[part * half : (part + 1) * half, :]
            s = dot(jnp.concatenate([keys, keys], axis=1), q2_ref[h, part * half : (part + 1) * half, :], NT)
            s = jnp.where(causal, s, LOW)
            block_top = jnp.max(s.reshape(per, POOL, half), axis=1)
            top = jnp.max(block_top, axis=0, keepdims=True)
            p = jnp.exp2(s - top)
            lanes = slice(h * rows + part * half, h * rows + (part + 1) * half)
            diag_ref[part * per : (part + 1) * per, lanes] = block_top
            top_ref[:, lanes] = top
            tot_ref[:, lanes] = jnp.sum(p.reshape(half // SUB, SUB, half), axis=0)
    place = lax.axis_index("ctx")
    along = lax.rem(place, near)
    base = place - along
    group = near * blocks
    order = order_ref[...].astype(jnp.float32)
    kb = lax.broadcasted_iota(jnp.int32, (2 * group, 1), 0)
    key_half = pick(order, kb // per)
    lane = lax.broadcasted_iota(jnp.int32, (2 * group, rows), 1)
    halves = [pick(order, jnp.full((1, 1), 2 * place + part, jnp.int32)) for part in range(2)]
    seen = jnp.where(key_half < jnp.where(lane < half, halves[0], halves[1]), 1.0, 0.0)
    shift = lax.rem(near - along, near) * blocks
    low, high = [pltpu.roll(seen[j * group : (j + 1) * group], shift, 0) for j in range(2)]
    seen_ref[0:group, :] = jnp.where(base == 0, low, high)
    seen_ref[group:, :] = jnp.where(base == 0, high, low)
    key_pos = key_half * per + (kb % per).astype(jnp.float32)
    diagonal = lax.broadcasted_iota(jnp.int32, (2 * group, 2 * group), 1) == kb
    key_pos = jnp.sum(jnp.where(diagonal, key_pos, 0.0), axis=0, keepdims=True)
    row = lax.broadcasted_iota(jnp.int32, (heads * SUB, 1), 0) % SUB
    query_pos = jnp.where(row < per, halves[0], halves[1]) * per + (row % per).astype(jnp.float32)
    visible_ref[...] = jnp.where((key_pos <= query_pos) & (row < blocks), 1.0, 0.0)


def pool_of(keys):
    x = keys.astype(jnp.float32).reshape(keys.shape[0] // POOL, POOL, keys.shape[1])
    return jnp.concatenate([jnp.max(x, axis=1), jnp.min(x, axis=1), jnp.sum(x, axis=1) * (1.0 / POOL)], axis=1)


def attend(q2_ref, seen_ref, chunks, top_in, tot_in, top_ref, tot_ref, map_ref, pool_ref):
    heads, rows, _ = q2_ref.shape
    blocks = rows // POOL
    tops = [top_in[:, h * rows : (h + 1) * rows] for h in range(heads)]
    tots = [tot_in[:, h * rows : (h + 1) * rows] for h in range(heads)]
    row = 0
    for first in range(0, len(chunks), 2):
        group = chunks[first : first + 2]
        keys = jnp.concatenate([read() for read, _ in group], axis=0)
        count = len(group) * blocks
        pool_ref[row : row + count, :] = pool_of(keys)
        seen = jnp.concatenate([seen_ref[at : at + blocks, :] for _, at in group], axis=0)
        seen_rows = jnp.broadcast_to(seen[:, None, :], (count, SUB, rows)) > 0.5
        seen = seen > 0.5
        keys = jnp.concatenate([keys, keys], axis=1)
        for h in range(heads):
            s = dot(keys, q2_ref[h], NT).reshape(count, POOL // SUB, SUB, rows)
            block_top = jnp.max(jnp.max(s, axis=1), axis=1)
            block_top = jnp.where(seen, block_top, LOW)
            map_ref[row : row + count, h * rows : (h + 1) * rows] = block_top
            top = jnp.maximum(tops[h], jnp.max(block_top, axis=0, keepdims=True))
            part = jnp.sum(jnp.exp2(s - top.reshape(1, 1, 1, rows)), axis=1)
            part = jnp.sum(jnp.where(seen_rows, part, 0.0), axis=0)
            tots[h] = tots[h] * jnp.exp2(tops[h] - top) + part
            tops[h] = top
        row += count
    for h in range(heads):
        top_ref[:, h * rows : (h + 1) * rows] = tops[h]
        tot_ref[:, h * rows : (h + 1) * rows] = tots[h]


def chunks_of(refs, layout, rows, group):
    chunks = []
    for ref, (other, offsets) in zip(refs, layout):
        for j, offset in enumerate(offsets):
            read = functools.partial(lambda r, j: r[j * rows : (j + 1) * rows, :], ref, j)
            chunks.append((read, other * group + offset * rows // POOL))
    return chunks


def attend_kernel(layout, *refs):
    q2_ref, seen_ref, top_in, tot_in = refs[:4]
    top_ref, tot_ref, map_ref, pool_ref = refs[-4:]
    chunks = chunks_of(refs[4:-4], layout, q2_ref.shape[1], seen_ref.shape[0] // 2)
    attend(q2_ref, seen_ref, chunks, top_in, tot_in, top_ref, tot_ref, map_ref, pool_ref)


def copy_kernel(in_ref, out_ref):
    out_ref[...] = in_ref[...]


def pair_kernel(own_ref, other_ref, out_ref):
    rows = own_ref.shape[0]
    out_ref[0:rows, :] = own_ref[...]
    out_ref[rows:, :] = other_ref[...]


def gradient_half(low, pooled_ref, gate_q_grad_ref, pool_ref, gate_k_grad_ref, out_ref):
    heads = pooled_ref.shape[0] // SUB
    width = pooled_ref.shape[1]
    whole = (heads + pool_ref.shape[1] // width) // 2
    chosen = range(whole) if low else range(whole, heads)
    for j, h in enumerate(chosen):
        here = slice(h * SUB, (h + 1) * SUB)
        out_ref[j * width : (j + 1) * width, :] = dot_split(pooled_ref[here, :], gate_q_grad_ref[here, :], TN)
    if not low:
        out_ref[len(chosen) * width : whole * width, :] = dot_split(pool_ref[...], gate_k_grad_ref[...], TN)


def finish_kernel(layout, places, *refs):
    q2_ref, seen_ref, top_in, tot_in, diag_ref, pooled_ref, gate_q_ref, wk_ref, visible_ref = refs[:9]
    key_refs = refs[9 : 9 + len(layout)]
    earlier = refs[9 + len(layout) : -12]
    target_ref, give_ref, gate_q_grad_ref, gate_k_grad_ref, pool_ref = refs[-12:-7]
    top_ref, tot_ref, last_map, last_pool, map_ref, rel_pool, block_ref = refs[-7:]
    heads, rows, _ = q2_ref.shape
    half = rows // 2
    per = half // POOL
    blocks = rows // POOL
    total = map_ref.shape[0]
    near = total // 2
    width = pooled_ref.shape[1]
    devices = near // blocks
    place = lax.axis_index("ctx")
    along = lax.rem(place, devices)
    bases = (place - along, devices - (place - along))
    attend(
        q2_ref, seen_ref, chunks_of(key_refs, layout, rows, near), top_in, tot_in, top_ref, tot_ref, last_map, last_pool
    )
    maps = list(earlier[0::2]) + [last_map]
    pools = list(earlier[1::2]) + [last_pool]
    for map_in, pool_in, where in zip(maps, pools, places):
        for j, (other, offset) in enumerate(where):
            here = slice(other * near + offset * blocks, other * near + (offset + 1) * blocks)
            map_ref[here, :] = map_in[j * blocks : (j + 1) * blocks, :]
            rel_pool[here, :] = pool_in[j * blocks : (j + 1) * blocks, :]
    shift = along * blocks
    for other in range(2):
        at = pl.multiple_of(bases[other] * blocks, near)
        pool_ref[pl.ds(at, near), :] = pltpu.roll(rel_pool[other * near : (other + 1) * near, :], shift, 0)
    block_ref[...] = jnp.ones(block_ref.shape, jnp.float32)
    for h in range(heads):
        for part in range(2):
            lanes = slice(h * rows + part * half, h * rows + (part + 1) * half)
            own_rows = slice(part * per, (part + 1) * per)
            map_ref[own_rows, lanes] = diag_ref[own_rows, lanes]
            tot = jnp.sum(tot_ref[:, lanes], axis=0, keepdims=True)
            b = jnp.exp2(map_ref[:, lanes] - (top_ref[:, lanes] + jnp.log2(tot)))
            b = jnp.max(b.T.reshape(per, POOL, total), axis=1)
            block_ref[h * SUB + part * per : h * SUB + (part + 1) * per, :] = b
    block_map = block_ref[...]
    copies = 128 // near
    group = [
        pltpu.roll(jnp.concatenate([block_map[:, j * near : (j + 1) * near]] * copies, axis=1), shift, 1)[:, :total]
        for j in range(2)
    ]
    lane = lax.broadcasted_iota(jnp.int32, (heads * SUB, total), 1)
    in_near = (lane >= bases[0] * blocks) & (lane < (bases[0] + devices) * blocks)
    block_map = jnp.where(in_near, group[0], group[1])
    target = block_map / jnp.sum(block_map, axis=1, keepdims=True)
    for h in range(heads):
        target_ref[h] = target[h * SUB : h * SUB + blocks, :]
    gate_q = gate_q_ref[...]
    gate_k = dot(pool_ref[...], wk_ref[...], NN, HIGHEST)
    gate_width = gate_k.shape[1]
    row = lax.broadcasted_iota(jnp.int32, (heads * SUB, total), 0) % SUB
    visible = visible_ref[...] > 0.5
    logits = dot(gate_q, gate_k, NT, HIGHEST) * gate_width ** (-0.5)
    peak = jnp.max(jnp.where(visible, logits, LOW), axis=1, keepdims=True)
    weights = jnp.where(visible, jnp.exp(logits - peak), 0.0)
    norm_sum = jnp.where(row[:, :1] < blocks, jnp.sum(weights, axis=1, keepdims=True), 1.0)
    log_gate = logits - peak - jnp.log(norm_sum)
    count = heads * total
    loss = -jnp.sum(jnp.where(visible, target * log_gate, 0.0)) / count
    d_logits = jnp.where(visible, weights / norm_sum - target, 0.0) / count * gate_width ** (-0.5)
    gate_q_grad_ref[...] = dot_split(d_logits, gate_k, NN)
    gate_k_grad_ref[...] = dot_split(d_logits, gate_q, TN)
    own_seq = lax.axis_index("seq")
    terms = (pooled_ref, gate_q_grad_ref, pool_ref, gate_k_grad_ref)
    pl.when(lax.rem(own_seq, 2) == 0)(lambda: gradient_half(False, *terms, give_ref))
    pl.when(lax.rem(own_seq, 2) != 0)(lambda: gradient_half(True, *terms, give_ref))
    lane = lax.broadcasted_iota(jnp.int32, (SUB, gate_width), 1)
    give_ref[give_ref.shape[0] - SUB :, :] = jnp.where(lane == own_seq, loss, 0.0)


def keep_kernel(pooled_ref, gate_q_grad_ref, pool_ref, gate_k_grad_ref, keep_ref):
    terms = (pooled_ref, gate_q_grad_ref, pool_ref, gate_k_grad_ref)
    core = lax.rem(lax.axis_index("seq"), 2)
    pl.when(core == 0)(lambda: gradient_half(True, *terms, keep_ref))
    pl.when(core != 0)(lambda: gradient_half(False, *terms, keep_ref))


def fold_kernel(keep_ref, give_ref, got_ref, out_ref):
    tiles, tile_rows, width = out_ref.shape
    part = keep_ref.shape[0]
    rows = part // tiles
    out_ref[:, 0:rows, :] = (keep_ref[...] + got_ref[0:part, :]).reshape(tiles, rows, width)
    loss = give_ref[part:, :] + got_ref[part:, :]
    out_ref[:, rows:, :] = jnp.broadcast_to(loss[None], (tiles, tile_rows - rows, width))


def sum_kernel(parts_ref, out_ref):
    total = jnp.sum(parts_ref[...], axis=0)
    for j in range(out_ref.shape[0]):
        out_ref[j] = total


def join_kernel(parts_ref, out_ref, loss_ref):
    total = jnp.sum(parts_ref[...], axis=0)
    rows = out_ref.shape[1]
    for j in range(out_ref.shape[0]):
        out_ref[j] = total[:rows]
    loss_ref[...] = total[rows:]


def last_kernel(
    mine_ref, other_ref, losses_ref, target_in, grad_q_ref, grad_k_ref, loss_ref, target_ref, loss_row, sems
):
    tiles = mine_ref.shape[0]
    left = grad_q_ref.shape[0] - tiles
    own_seq = lax.axis_index("seq")
    core = lax.rem(own_seq, 2)

    def grads(low_ref, high_ref):
        pairs = (
            (low_ref, grad_q_ref.at[pl.ds(0, tiles)]),
            (high_ref.at[pl.ds(0, left)], grad_q_ref.at[pl.ds(tiles, left)]),
            (high_ref.at[pl.ds(left, tiles - left)], grad_k_ref),
        )
        return [pltpu.make_async_copy(source, target, sems.at[j]) for j, (source, target) in enumerate(pairs)]

    @pl.when(core == 0)
    def _():
        for copy in grads(mine_ref, other_ref):
            copy.start()

    @pl.when(core != 0)
    def _():
        for copy in grads(other_ref, mine_ref):
            copy.start()

    losses = losses_ref[0:1, :]
    lane = lax.broadcasted_iota(jnp.int32, losses.shape, 1)
    loss_row[...] = jnp.sum(jnp.where(lane == own_seq, losses, 0.0), axis=1, keepdims=True)
    rest = [
        pltpu.make_async_copy(loss_row, loss_ref, sems.at[3]),
        pltpu.make_async_copy(target_in, target_ref, sems.at[4]),
    ]
    for copy in rest:
        copy.start()
    for copy in grads(mine_ref, other_ref) + rest:
        copy.wait()


def f32(*shape):
    return jax.ShapeDtypeStruct(shape, jnp.float32)


def call(kernel, out_shape, specs, name, scratch=(), cost=None, out_specs=None):
    return pl.pallas_call(
        kernel,
        out_shape=out_shape,
        in_specs=specs,
        out_specs=out_specs or tuple(VMEM for _ in out_shape),
        scratch_shapes=scratch,
        compiler_params=PARAMS,
        cost_estimate=cost,
        name=name,
    )


def on_device(order, queries, keys, w_query_gate, w_key_gate):
    tok_rows = queries.shape[1]
    heads = queries.shape[2]
    width = queries.shape[3]
    gate_width = w_key_gate.shape[1]
    blocks = tok_rows // POOL
    ctx_count = lax.axis_size("ctx")
    seq_count = lax.axis_size("seq")
    near = ctx_count // 2
    total = ctx_count * blocks
    scale = width ** (-0.5) * math.log2(math.e)
    columns = heads * tok_rows

    def get(x, offset):
        return lax.ppermute(x, "ctx", [(j, j // near * near + (j - offset) % near) for j in range(ctx_count)])

    def across(x):
        return lax.ppermute(x, "ctx", [(j, (j + near) % ctx_count) for j in range(ctx_count)])

    own_keys = keys[0]
    step = {offset: get(own_keys, offset % near) for offset in (1, -1, near // 2)}
    (own_copy,) = call(
        copy_kernel,
        (jax.ShapeDtypeStruct(own_keys.shape, keys.dtype),),
        [VMEM],
        "copy",
        cost=pl.CostEstimate(flops=10**9, bytes_accessed=10**6, transcendentals=10**6),
    )(own_keys)
    two_parts = jax.ShapeDtypeStruct((2 * tok_rows, width), keys.dtype)
    (ahead,) = call(pair_kernel, (two_parts,), [VMEM] * 2, "ahead")(own_copy, step[1])
    ahead = get(ahead, 2)
    (behind,) = call(pair_kernel, (two_parts,), [VMEM] * 2, "behind")(own_copy, step[-1])
    behind = get(behind, near - 2)
    mid = jnp.concatenate([own_copy, step[1], step[-1]], axis=0)
    mid_far = across(mid)
    mid_from = (0, 1, near - 1)
    quad_from = (near // 2,)
    ahead_from = (2, 3)
    behind_from = (near - 2, near - 3)

    q = jnp.transpose(queries[0], (1, 0, 2))
    state = (f32(1, columns), f32(SUB, columns))
    diag, top, tot, pooled, gate_q, q2, seen, visible = call(
        functools.partial(local_kernel, scale, near),
        (f32(SUB, columns),)
        + state
        + (
            f32(heads * SUB, width),
            f32(heads * SUB, gate_width),
            jax.ShapeDtypeStruct((heads, tok_rows, 2 * width), jnp.bfloat16),
            f32(total, tok_rows),
            f32(heads * SUB, total),
        ),
        [VMEM] * 4 + [ANY] * 2,
        "local",
        cost=pl.CostEstimate(flops=4 * 10**8, bytes_accessed=10**6, transcendentals=10**5),
    )(q, own_copy, w_query_gate, order, step[1], step[-1])

    def attend_to(layout, top, tot, *keys):
        count = sum(len(offsets) for _, offsets in layout)
        return call(
            functools.partial(attend_kernel, layout),
            state + (f32(count * blocks, columns), f32(count * blocks, 3 * width)),
            [VMEM] * (4 + len(keys)),
            "attend",
            cost=pl.CostEstimate(flops=1200000000, bytes_accessed=10**6, transcendentals=1300000),
        )(q2, seen, top, tot, *keys)

    layouts = (
        ((0, mid_from),),
        ((0, ahead_from), (0, behind_from), (0, quad_from)),
        ((1, mid_from), (1, quad_from)),
        ((1, ahead_from),),
        ((1, behind_from),),
    )
    places = [[(other, offset) for other, offsets in layout for offset in offsets] for layout in layouts]
    quad = step[near // 2]
    quad_far = across(quad)
    ahead_far = across(ahead)
    behind_far = across(behind)
    earlier = []
    for layout, key_parts in zip(layouts[:-1], ((mid,), (ahead, behind, quad), (mid_far, quad_far), (ahead_far,))):
        top, tot, *found = attend_to(layout, top, tot, *key_parts)
        earlier += found

    grad_rows = heads * width + 3 * width
    part = grad_rows // 2
    last_blocks = len(places[-1]) * blocks
    target, give, *terms = call(
        functools.partial(finish_kernel, layouts[-1], places),
        (
            f32(heads, blocks, total),
            f32(part + SUB, gate_width),
            f32(heads * SUB, gate_width),
            f32(total, gate_width),
            f32(total, 3 * width),
        ),
        [VMEM] * (10 + len(earlier)),
        "finish",
        scratch=[
            pltpu.VMEM(shape, jnp.float32)
            for shape in (
                (1, columns),
                (SUB, columns),
                (last_blocks, columns),
                (last_blocks, 3 * width),
                (total, columns),
                (total, 3 * width),
                (heads * SUB, total),
            )
        ],
    )(q2, seen, top, tot, diag, pooled, gate_q, w_key_gate, visible, behind_far, *earlier)

    every = ("seq", "ctx")
    half_seq = seq_count // 2

    def flat(x_lo, y, core, x_hi, z):
        return (x_lo * half_seq + y * 2 + core) * ctx_count + x_hi * near + z

    ys = range(half_seq // 2)
    zs = range(near)
    pair = (0, 1)
    cores = [
        (flat(a, y, b, c, z), flat(a, y, 1 - b, c, z)) for a in pair for y in ys for b in pair for c in pair for z in zs
    ]
    planes = [[flat(a, y, b, c, z) for a in pair for c in pair for y in ys] for b in pair for z in zs]
    tiles = len(planes[0])
    got = lax.ppermute(give, every, cores)
    (keep,) = call(keep_kernel, (f32(part, gate_width),), [VMEM] * 4, "keep")(
        pooled, terms[0], terms[2], terms[1]
    )
    (parts,) = call(
        fold_kernel, (f32(tiles, part // tiles + SUB, gate_width),), [VMEM] * 3, "fold"
    )(keep, give, got)
    parts = lax.all_to_all(parts, every, 0, 0, axis_index_groups=planes, tiled=True)
    (spread,) = call(sum_kernel, (f32(near, part // tiles + SUB, gate_width),), [VMEM], "sum")(parts)
    parts = lax.all_to_all(
        spread,
        "ctx",
        0,
        0,
        axis_index_groups=[list(range(near)), list(range(near, ctx_count))],
        tiled=True,
    )
    spread, losses = call(
        join_kernel, (f32(tiles, part // tiles, gate_width), f32(SUB, gate_width)), [VMEM], "join"
    )(parts)
    mine = lax.all_to_all(spread, every, 0, 0, axis_index_groups=planes, tiled=True).reshape(part, gate_width)
    other = lax.ppermute(mine, every, cores)
    tiled = (part // width, width, gate_width)
    grad_q, grad_k, loss, target = call(
        last_kernel,
        (f32(heads, width, gate_width), f32(3, width, gate_width), f32(1, 1), f32(*target.shape)),
        [VMEM] * 4,
        "last",
        scratch=[pltpu.VMEM((1, 1), jnp.float32), pltpu.SemaphoreType.DMA((5,))],
        out_specs=(ANY,) * 4,
    )(mine.reshape(tiled), other.reshape(tiled), losses, target)
    return (target[None, None], grad_q, grad_k.reshape(3 * width, gate_width), loss.reshape(1))


def solution(mesh):
    placed = (P("seq", None), P("seq", "ctx", None, None), P("seq", "ctx", None), P(), P())
    return jax.shard_map(
        on_device,
        mesh=mesh,
        in_specs=placed,
        out_specs=(P("seq", "ctx", None, None, None), P(), P(), P("seq")),
        check_vma=False,
    )
```

```python
import functools
import math

import jax
import jax.numpy as jnp
from jax import lax
from jax.experimental import pallas as pl
from jax.experimental.pallas import tpu as pltpu
from jax.sharding import PartitionSpec as P

POOL = 64
LOW = -1e30
HIGHEST = lax.Precision.HIGHEST
VMEM = pl.BlockSpec(memory_space=pltpu.VMEM)
ANY = pl.BlockSpec(memory_space=pl.ANY)
PARAMS = pltpu.CompilerParams(vmem_limit_bytes=40 * 1024 * 1024)
SUB = 8
NT = (((1,), (1,)), ((), ()))
TN = (((0,), (0,)), ((), ()))
NN = (((1,), (0,)), ((), ()))


def dot(a, b, dims, precision=None):
    return lax.dot_general(a, b, dims, precision=precision, preferred_element_type=jnp.float32)


def split(x):
    high = x.astype(jnp.bfloat16)
    return high, (x - high.astype(jnp.float32)).astype(jnp.bfloat16)


def dot_split(a, b, dims):
    a_high, a_low = split(a)
    b_high, b_low = split(b)
    return dot(a_high, b_high, dims) + (dot(a_high, b_low, dims) + dot(a_low, b_high, dims))


def pick(values, index):
    lane = lax.broadcasted_iota(jnp.int32, (index.shape[0], values.shape[1]), 1)
    return jnp.sum(jnp.where(lane == index, values, 0.0), axis=1, keepdims=True)


def local_kernel(scale, near, q_ref, k_ref, wq_ref, order_ref, *refs):
    diag_ref, top_ref, tot_ref, pooled_ref, gate_q_ref, q2_ref, seen_ref, visible_ref = refs[-8:]
    heads, rows, width = q_ref.shape
    half = rows // 2
    blocks = rows // POOL
    per = half // POOL
    diag_ref[...] = jnp.full(diag_ref.shape, LOW, jnp.float32)
    key_row = lax.broadcasted_iota(jnp.int32, (half, half), 0)
    query_lane = lax.broadcasted_iota(jnp.int32, (half, half), 1)
    causal = key_row <= query_lane
    blank = jnp.zeros((SUB - blocks, width), jnp.float32)
    for h in range(heads):
        q = q_ref[h].astype(jnp.float32)
        pooled = jnp.sum(q.reshape(blocks, POOL, width), axis=1) * (1.0 / POOL)
        pooled = jnp.concatenate([pooled, blank], axis=0)
        pooled_ref[h * SUB : (h + 1) * SUB, :] = pooled
        gate_q_ref[h * SUB : (h + 1) * SUB, :] = dot(pooled, wq_ref[h], NN, HIGHEST)
        high, low = split(q * scale)
        q2_ref[h, :, 0:width] = high
        q2_ref[h, :, width:] = low
        for part in range(2):
            keys = k_ref[part * half : (part + 1) * half, :]
            s = dot(jnp.concatenate([keys, keys], axis=1), q2_ref[h, part * half : (part + 1) * half, :], NT)
            s = jnp.where(causal, s, LOW)
            block_top = jnp.max(s.reshape(per, POOL, half), axis=1)
            top = jnp.max(block_top, axis=0, keepdims=True)
            p = jnp.exp2(s - top)
            lanes = slice(h * rows + part * half, h * rows + (part + 1) * half)
            diag_ref[part * per : (part + 1) * per, lanes] = block_top
            top_ref[:, lanes] = top
            tot_ref[:, lanes] = jnp.sum(p.reshape(half // SUB, SUB, half), axis=0)
    place = lax.axis_index("ctx")
    along = lax.rem(place, near)
    base = place - along
    group = near * blocks
    order = order_ref[...].astype(jnp.float32)
    kb = lax.broadcasted_iota(jnp.int32, (2 * group, 1), 0)
    key_half = pick(order, kb // per)
    lane = lax.broadcasted_iota(jnp.int32, (2 * group, rows), 1)
    halves = [pick(order, jnp.full((1, 1), 2 * place + part, jnp.int32)) for part in range(2)]
    seen = jnp.where(key_half < jnp.where(lane < half, halves[0], halves[1]), 1.0, 0.0)
    shift = lax.rem(near - along, near) * blocks
    low, high = [pltpu.roll(seen[j * group : (j + 1) * group], shift, 0) for j in range(2)]
    seen_ref[0:group, :] = jnp.where(base == 0, low, high)
    seen_ref[group:, :] = jnp.where(base == 0, high, low)
    key_pos = key_half * per + (kb % per).astype(jnp.float32)
    diagonal = lax.broadcasted_iota(jnp.int32, (2 * group, 2 * group), 1) == kb
    key_pos = jnp.sum(jnp.where(diagonal, key_pos, 0.0), axis=0, keepdims=True)
    row = lax.broadcasted_iota(jnp.int32, (heads * SUB, 1), 0) % SUB
    query_pos = jnp.where(row < per, halves[0], halves[1]) * per + (row % per).astype(jnp.float32)
    visible_ref[...] = jnp.where((key_pos <= query_pos) & (row < blocks), 1.0, 0.0)


def pool_of(keys):
    x = keys.astype(jnp.float32).reshape(keys.shape[0] // POOL, POOL, keys.shape[1])
    return jnp.concatenate([jnp.max(x, axis=1), jnp.min(x, axis=1), jnp.sum(x, axis=1) * (1.0 / POOL)], axis=1)


def attend(q2_ref, seen_ref, chunks, top_in, tot_in, top_ref, tot_ref, map_ref, pool_ref):
    heads, rows, _ = q2_ref.shape
    blocks = rows // POOL
    tops = [top_in[:, h * rows : (h + 1) * rows] for h in range(heads)]
    tots = [tot_in[:, h * rows : (h + 1) * rows] for h in range(heads)]
    row = 0
    for first in range(0, len(chunks), 2):
        group = chunks[first : first + 2]
        keys = jnp.concatenate([read() for read, _ in group], axis=0)
        count = len(group) * blocks
        pool_ref[row : row + count, :] = pool_of(keys)
        seen = jnp.concatenate([seen_ref[at : at + blocks, :] for _, at in group], axis=0)
        seen_rows = jnp.broadcast_to(seen[:, None, :], (count, SUB, rows)) > 0.5
        seen = seen > 0.5
        keys = jnp.concatenate([keys, keys], axis=1)
        for h in range(heads):
            s = dot(keys, q2_ref[h], NT).reshape(count, POOL // SUB, SUB, rows)
            block_top = jnp.max(jnp.max(s, axis=1), axis=1)
            block_top = jnp.where(seen, block_top, LOW)
            map_ref[row : row + count, h * rows : (h + 1) * rows] = block_top
            top = jnp.maximum(tops[h], jnp.max(block_top, axis=0, keepdims=True))
            part = jnp.sum(jnp.exp2(s - top.reshape(1, 1, 1, rows)), axis=1)
            part = jnp.sum(jnp.where(seen_rows, part, 0.0), axis=0)
            tots[h] = tots[h] * jnp.exp2(tops[h] - top) + part
            tops[h] = top
        row += count
    for h in range(heads):
        top_ref[:, h * rows : (h + 1) * rows] = tops[h]
        tot_ref[:, h * rows : (h + 1) * rows] = tots[h]


def chunks_of(refs, layout, rows, group):
    chunks = []
    for ref, (other, offsets) in zip(refs, layout):
        for j, offset in enumerate(offsets):
            read = functools.partial(lambda r, j: r[j * rows : (j + 1) * rows, :], ref, j)
            chunks.append((read, other * group + offset * rows // POOL))
    return chunks


def attend_kernel(layout, *refs):
    q2_ref, seen_ref, top_in, tot_in = refs[:4]
    top_ref, tot_ref, map_ref, pool_ref = refs[-4:]
    chunks = chunks_of(refs[4:-4], layout, q2_ref.shape[1], seen_ref.shape[0] // 2)
    attend(q2_ref, seen_ref, chunks, top_in, tot_in, top_ref, tot_ref, map_ref, pool_ref)


def copy_kernel(in_ref, out_ref):
    out_ref[...] = in_ref[...]


def pair_kernel(own_ref, other_ref, out_ref):
    rows = own_ref.shape[0]
    out_ref[0:rows, :] = own_ref[...]
    out_ref[rows:, :] = other_ref[...]


def gradient_half(low, pooled_ref, gate_q_grad_ref, pool_ref, gate_k_grad_ref, out_ref):
    heads = pooled_ref.shape[0] // SUB
    width = pooled_ref.shape[1]
    whole = (heads + pool_ref.shape[1] // width) // 2
    chosen = range(whole) if low else range(whole, heads)
    for j, h in enumerate(chosen):
        here = slice(h * SUB, (h + 1) * SUB)
        out_ref[j * width : (j + 1) * width, :] = dot_split(pooled_ref[here, :], gate_q_grad_ref[here, :], TN)
    if not low:
        out_ref[len(chosen) * width : whole * width, :] = dot_split(pool_ref[...], gate_k_grad_ref[...], TN)


def finish_kernel(layout, places, *refs):
    q2_ref, seen_ref, top_in, tot_in, diag_ref, pooled_ref, gate_q_ref, wk_ref, visible_ref = refs[:9]
    key_refs = refs[9 : 9 + len(layout)]
    earlier = refs[9 + len(layout) : -12]
    target_ref, give_ref, gate_q_grad_ref, gate_k_grad_ref, pool_ref = refs[-12:-7]
    top_ref, tot_ref, last_map, last_pool, map_ref, rel_pool, block_ref = refs[-7:]
    heads, rows, _ = q2_ref.shape
    half = rows // 2
    per = half // POOL
    blocks = rows // POOL
    total = map_ref.shape[0]
    near = total // 2
    width = pooled_ref.shape[1]
    devices = near // blocks
    place = lax.axis_index("ctx")
    along = lax.rem(place, devices)
    bases = (place - along, devices - (place - along))
    attend(
        q2_ref, seen_ref, chunks_of(key_refs, layout, rows, near), top_in, tot_in, top_ref, tot_ref, last_map, last_pool
    )
    maps = list(earlier[0::2]) + [last_map]
    pools = list(earlier[1::2]) + [last_pool]
    for map_in, pool_in, where in zip(maps, pools, places):
        for j, (other, offset) in enumerate(where):
            here = slice(other * near + offset * blocks, other * near + (offset + 1) * blocks)
            map_ref[here, :] = map_in[j * blocks : (j + 1) * blocks, :]
            rel_pool[here, :] = pool_in[j * blocks : (j + 1) * blocks, :]
    shift = along * blocks
    for other in range(2):
        at = pl.multiple_of(bases[other] * blocks, near)
        pool_ref[pl.ds(at, near), :] = pltpu.roll(rel_pool[other * near : (other + 1) * near, :], shift, 0)
    block_ref[...] = jnp.ones(block_ref.shape, jnp.float32)
    for h in range(heads):
        for part in range(2):
            lanes = slice(h * rows + part * half, h * rows + (part + 1) * half)
            own_rows = slice(part * per, (part + 1) * per)
            map_ref[own_rows, lanes] = diag_ref[own_rows, lanes]
            tot = jnp.sum(tot_ref[:, lanes], axis=0, keepdims=True)
            b = jnp.exp2(map_ref[:, lanes] - (top_ref[:, lanes] + jnp.log2(tot)))
            b = jnp.max(b.T.reshape(per, POOL, total), axis=1)
            block_ref[h * SUB + part * per : h * SUB + (part + 1) * per, :] = b
    block_map = block_ref[...]
    copies = 128 // near
    group = [
        pltpu.roll(jnp.concatenate([block_map[:, j * near : (j + 1) * near]] * copies, axis=1), shift, 1)[:, :total]
        for j in range(2)
    ]
    lane = lax.broadcasted_iota(jnp.int32, (heads * SUB, total), 1)
    in_near = (lane >= bases[0] * blocks) & (lane < (bases[0] + devices) * blocks)
    block_map = jnp.where(in_near, group[0], group[1])
    target = block_map / jnp.sum(block_map, axis=1, keepdims=True)
    for h in range(heads):
        target_ref[h] = target[h * SUB : h * SUB + blocks, :]
    gate_q = gate_q_ref[...]
    gate_k = dot(pool_ref[...], wk_ref[...], NN, HIGHEST)
    gate_width = gate_k.shape[1]
    row = lax.broadcasted_iota(jnp.int32, (heads * SUB, total), 0) % SUB
    visible = visible_ref[...] > 0.5
    logits = dot(gate_q, gate_k, NT, HIGHEST) * gate_width ** (-0.5)
    peak = jnp.max(jnp.where(visible, logits, LOW), axis=1, keepdims=True)
    weights = jnp.where(visible, jnp.exp(logits - peak), 0.0)
    norm_sum = jnp.where(row[:, :1] < blocks, jnp.sum(weights, axis=1, keepdims=True), 1.0)
    log_gate = logits - peak - jnp.log(norm_sum)
    count = heads * total
    loss = -jnp.sum(jnp.where(visible, target * log_gate, 0.0)) / count
    d_logits = jnp.where(visible, weights / norm_sum - target, 0.0) / count * gate_width ** (-0.5)
    gate_q_grad_ref[...] = dot_split(d_logits, gate_k, NN)
    gate_k_grad_ref[...] = dot_split(d_logits, gate_q, TN)
    own_seq = lax.axis_index("seq")
    terms = (pooled_ref, gate_q_grad_ref, pool_ref, gate_k_grad_ref)
    pl.when(lax.rem(own_seq, 2) == 0)(lambda: gradient_half(False, *terms, give_ref))
    pl.when(lax.rem(own_seq, 2) != 0)(lambda: gradient_half(True, *terms, give_ref))
    lane = lax.broadcasted_iota(jnp.int32, (SUB, gate_width), 1)
    give_ref[give_ref.shape[0] - SUB :, :] = jnp.where(lane == own_seq, loss, 0.0)


def keep_kernel(pooled_ref, gate_q_grad_ref, pool_ref, gate_k_grad_ref, keep_ref):
    terms = (pooled_ref, gate_q_grad_ref, pool_ref, gate_k_grad_ref)
    core = lax.rem(lax.axis_index("seq"), 2)
    pl.when(core == 0)(lambda: gradient_half(True, *terms, keep_ref))
    pl.when(core != 0)(lambda: gradient_half(False, *terms, keep_ref))


def fold_kernel(keep_ref, give_ref, got_ref, out_ref):
    tiles, tile_rows, width = out_ref.shape
    part = keep_ref.shape[0]
    rows = part // tiles
    out_ref[:, 0:rows, :] = (keep_ref[...] + got_ref[0:part, :]).reshape(tiles, rows, width)
    loss = give_ref[part:, :] + got_ref[part:, :]
    out_ref[:, rows:, :] = jnp.broadcast_to(loss[None], (tiles, tile_rows - rows, width))


def sum_kernel(parts_ref, out_ref):
    total = jnp.sum(parts_ref[...], axis=0)
    for j in range(out_ref.shape[0]):
        out_ref[j] = total


def join_kernel(parts_ref, out_ref, loss_ref):
    total = jnp.sum(parts_ref[...], axis=0)
    rows = out_ref.shape[1]
    for j in range(out_ref.shape[0]):
        out_ref[j] = total[:rows]
    loss_ref[...] = total[rows:]


def write_half(low, source_ref, grad_q_ref, grad_k_ref, sems, others=()):
    tiles = source_ref.shape[0]
    left = grad_q_ref.shape[0] - tiles
    if low:
        pairs = [(source_ref, grad_q_ref.at[pl.ds(0, tiles)])]
    else:
        pairs = [
            (source_ref.at[pl.ds(0, left)], grad_q_ref.at[pl.ds(tiles, left)]),
            (source_ref.at[pl.ds(left, tiles - left)], grad_k_ref),
        ]
    pairs += others
    copies = [pltpu.make_async_copy(source, target, sems.at[j]) for j, (source, target) in enumerate(pairs)]
    for copy in copies:
        copy.start()
    for copy in copies:
        copy.wait()


def mine_kernel(
    mine_ref, losses_ref, target_in, grad_q_ref, grad_k_ref, loss_ref, target_ref, loss_row, sems
):
    own_seq = lax.axis_index("seq")
    core = lax.rem(own_seq, 2)
    losses = losses_ref[0:1, :]
    lane = lax.broadcasted_iota(jnp.int32, losses.shape, 1)
    loss_row[...] = jnp.sum(jnp.where(lane == own_seq, losses, 0.0), axis=1, keepdims=True)
    others = [(loss_row, loss_ref), (target_in, target_ref)]
    pl.when(core == 0)(lambda: write_half(True, mine_ref, grad_q_ref, grad_k_ref, sems, others))
    pl.when(core != 0)(lambda: write_half(False, mine_ref, grad_q_ref, grad_k_ref, sems, others))


def other_kernel(other_ref, grad_q_in, grad_k_in, grad_q_ref, grad_k_ref, sems):
    core = lax.rem(lax.axis_index("seq"), 2)
    pl.when(core == 0)(lambda: write_half(False, other_ref, grad_q_ref, grad_k_ref, sems))
    pl.when(core != 0)(lambda: write_half(True, other_ref, grad_q_ref, grad_k_ref, sems))


def f32(*shape):
    return jax.ShapeDtypeStruct(shape, jnp.float32)


def call(kernel, out_shape, specs, name, scratch=(), cost=None, out_specs=None, aliases={}):
    return pl.pallas_call(
        kernel,
        out_shape=out_shape,
        in_specs=specs,
        out_specs=out_specs or tuple(VMEM for _ in out_shape),
        scratch_shapes=scratch,
        compiler_params=PARAMS,
        cost_estimate=cost,
        input_output_aliases=aliases,
        name=name,
    )


def on_device(order, queries, keys, w_query_gate, w_key_gate):
    tok_rows = queries.shape[1]
    heads = queries.shape[2]
    width = queries.shape[3]
    gate_width = w_key_gate.shape[1]
    blocks = tok_rows // POOL
    ctx_count = lax.axis_size("ctx")
    seq_count = lax.axis_size("seq")
    near = ctx_count // 2
    total = ctx_count * blocks
    scale = width ** (-0.5) * math.log2(math.e)
    columns = heads * tok_rows

    def get(x, offset):
        return lax.ppermute(x, "ctx", [(j, j // near * near + (j - offset) % near) for j in range(ctx_count)])

    def across(x):
        return lax.ppermute(x, "ctx", [(j, (j + near) % ctx_count) for j in range(ctx_count)])

    own_keys = keys[0]
    step = {offset: get(own_keys, offset % near) for offset in (1, -1, near // 2)}
    (own_copy,) = call(
        copy_kernel,
        (jax.ShapeDtypeStruct(own_keys.shape, keys.dtype),),
        [VMEM],
        "copy",
        cost=pl.CostEstimate(flops=10**9, bytes_accessed=10**6, transcendentals=10**6),
    )(own_keys)
    two_parts = jax.ShapeDtypeStruct((2 * tok_rows, width), keys.dtype)
    (ahead,) = call(pair_kernel, (two_parts,), [VMEM] * 2, "ahead")(own_copy, step[1])
    ahead = get(ahead, 2)
    (behind,) = call(pair_kernel, (two_parts,), [VMEM] * 2, "behind")(own_copy, step[-1])
    behind = get(behind, near - 2)
    mid = jnp.concatenate([own_copy, step[1], step[-1]], axis=0)
    mid_far = across(mid)
    mid_from = (0, 1, near - 1)
    quad_from = (near // 2,)
    ahead_from = (2, 3)
    behind_from = (near - 2, near - 3)

    q = jnp.transpose(queries[0], (1, 0, 2))
    state = (f32(1, columns), f32(SUB, columns))
    diag, top, tot, pooled, gate_q, q2, seen, visible = call(
        functools.partial(local_kernel, scale, near),
        (f32(SUB, columns),)
        + state
        + (
            f32(heads * SUB, width),
            f32(heads * SUB, gate_width),
            jax.ShapeDtypeStruct((heads, tok_rows, 2 * width), jnp.bfloat16),
            f32(total, tok_rows),
            f32(heads * SUB, total),
        ),
        [VMEM] * 4 + [ANY] * 2,
        "local",
        cost=pl.CostEstimate(flops=4 * 10**8, bytes_accessed=10**6, transcendentals=10**5),
    )(q, own_copy, w_query_gate, order, step[1], step[-1])

    def attend_to(layout, top, tot, *keys):
        count = sum(len(offsets) for _, offsets in layout)
        return call(
            functools.partial(attend_kernel, layout),
            state + (f32(count * blocks, columns), f32(count * blocks, 3 * width)),
            [VMEM] * (4 + len(keys)),
            "attend",
            cost=pl.CostEstimate(flops=1200000000, bytes_accessed=10**6, transcendentals=1300000),
        )(q2, seen, top, tot, *keys)

    layouts = (
        ((0, mid_from),),
        ((0, ahead_from), (0, behind_from), (0, quad_from)),
        ((1, mid_from), (1, quad_from)),
        ((1, ahead_from),),
        ((1, behind_from),),
    )
    places = [[(other, offset) for other, offsets in layout for offset in offsets] for layout in layouts]
    quad = step[near // 2]
    quad_far = across(quad)
    ahead_far = across(ahead)
    behind_far = across(behind)
    earlier = []
    for layout, key_parts in zip(layouts[:-1], ((mid,), (ahead, behind, quad), (mid_far, quad_far), (ahead_far,))):
        top, tot, *found = attend_to(layout, top, tot, *key_parts)
        earlier += found

    grad_rows = heads * width + 3 * width
    part = grad_rows // 2
    last_blocks = len(places[-1]) * blocks
    target, give, *terms = call(
        functools.partial(finish_kernel, layouts[-1], places),
        (
            f32(heads, blocks, total),
            f32(part + SUB, gate_width),
            f32(heads * SUB, gate_width),
            f32(total, gate_width),
            f32(total, 3 * width),
        ),
        [VMEM] * (10 + len(earlier)),
        "finish",
        scratch=[
            pltpu.VMEM(shape, jnp.float32)
            for shape in (
                (1, columns),
                (SUB, columns),
                (last_blocks, columns),
                (last_blocks, 3 * width),
                (total, columns),
                (total, 3 * width),
                (heads * SUB, total),
            )
        ],
    )(q2, seen, top, tot, diag, pooled, gate_q, w_key_gate, visible, behind_far, *earlier)

    every = ("seq", "ctx")
    half_seq = seq_count // 2

    def flat(x_lo, y, core, x_hi, z):
        return (x_lo * half_seq + y * 2 + core) * ctx_count + x_hi * near + z

    ys = range(half_seq // 2)
    zs = range(near)
    pair = (0, 1)
    cores = [
        (flat(a, y, b, c, z), flat(a, y, 1 - b, c, z)) for a in pair for y in ys for b in pair for c in pair for z in zs
    ]
    planes = [[flat(a, y, b, c, z) for a in pair for c in pair for y in ys] for b in pair for z in zs]
    tiles = len(planes[0])
    got = lax.ppermute(give, every, cores)
    (keep,) = call(keep_kernel, (f32(part, gate_width),), [VMEM] * 4, "keep")(
        pooled, terms[0], terms[2], terms[1]
    )
    (parts,) = call(
        fold_kernel, (f32(tiles, part // tiles + SUB, gate_width),), [VMEM] * 3, "fold"
    )(keep, give, got)
    parts = lax.all_to_all(parts, every, 0, 0, axis_index_groups=planes, tiled=True)
    (spread,) = call(sum_kernel, (f32(near, part // tiles + SUB, gate_width),), [VMEM], "sum")(parts)
    parts = lax.all_to_all(
        spread,
        "ctx",
        0,
        0,
        axis_index_groups=[list(range(near)), list(range(near, ctx_count))],
        tiled=True,
    )
    spread, losses = call(
        join_kernel, (f32(tiles, part // tiles, gate_width), f32(SUB, gate_width)), [VMEM], "join"
    )(parts)
    mine = lax.all_to_all(spread, every, 0, 0, axis_index_groups=planes, tiled=True).reshape(part, gate_width)
    other = lax.ppermute(mine, every, cores)
    tiled = (part // width, width, gate_width)
    grads = (f32(heads, width, gate_width), f32(3, width, gate_width))
    grad_q, grad_k, loss, target = call(
        mine_kernel,
        grads + (f32(1, 1), f32(*target.shape)),
        [VMEM] * 3,
        "mine",
        scratch=[pltpu.VMEM((1, 1), jnp.float32), pltpu.SemaphoreType.DMA((4,))],
        out_specs=(ANY,) * 4,
    )(mine.reshape(tiled), losses, target)
    grad_q, grad_k = call(
        other_kernel,
        grads,
        [VMEM, ANY, ANY],
        "other",
        scratch=[pltpu.SemaphoreType.DMA((2,))],
        out_specs=(ANY,) * 2,
        aliases={1: 0, 2: 1},
    )(other.reshape(tiled), grad_q, grad_k)
    return (target[None, None], grad_q, grad_k.reshape(3 * width, gate_width), loss.reshape(1))


def solution(mesh):
    placed = (P("seq", None), P("seq", "ctx", None, None), P("seq", "ctx", None), P(), P())
    return jax.shard_map(
        on_device,
        mesh=mesh,
        in_specs=placed,
        out_specs=(P("seq", "ctx", None, None, None), P(), P(), P("seq")),
        check_vma=False,
    )
```
